32 devices in a mesh: seg: 8 (over z, core), fsdp: 4 (over y, x).
Axes of the slice: x: 2, y: 2, z: 4, core: 2. Of those that a mesh axis runs over, the one named last changes fastest.
Arguments:
- frames: bfloat16 [4, 64, 16, 1024], P('fsdp', 'seg'), may hold values from -6 to 6
- memory_in: bfloat16 [4, 64, 1024], P('fsdp', 'seg'), may hold values from -6 to 6
- lengths: int32 [4], P('fsdp'), may hold values from 1 to 64, as said below
- ln_gain: float32 [1024], replicated, may hold values from 0.25 to 1.75
- w_query: bfloat16 [1024, 1024], P('fsdp'), may hold values from -1 to 1
- w_key: bfloat16 [1024, 1024], P('fsdp'), may hold values from -12 to 12
- w_value: bfloat16 [1024, 1024], P('fsdp'), may hold values from -0.1875 to 0.1875
- w_out: bfloat16 [1024, 1024], P('fsdp'), may hold values from -0.1875 to 0.1875
- grad_frames: bfloat16 [4, 64, 16, 1024], P('fsdp', 'seg'), may hold values from -6 to 6
- grad_memory: bfloat16 [4, 64, 1024], P('fsdp', 'seg'), may hold values from -6 to 6
Outputs:
- frames_out: bfloat16 [4, 64, 16, 1024], P('fsdp', 'seg')
- memory_out: bfloat16 [4, 64, 1024], P('fsdp', 'seg')
- value_grad: float32 [1024, 1024], P('fsdp')
The draws below stay inside these ranges and needn't reach their ends.
Inputs may be any that keep to these rules, and one draw needn't show every extreme that they name: `lengths`: in every aligned block of 1 utterances (those of one fsdp index) at least one has length 64.
All inputs are finite; a program needn't handle non-finite values.
Results may differ from the reference program's by a relative error of at most 0.04.
Values may be sent and summed in bfloat16 or wider, within the bound.
No kernel may reach another device: no remote copies, remote signals or barrier semaphores. Data moves between devices by JAX's collectives and lax.ppermute only.
A program may use at most 64 MiB of HBM per device.

```python
import math
import jax
import jax.numpy as jnp
from jax import lax

D = 1024
HEADS = 16
FRAMES = 16
LEFT = 16
MEMORY = 8
UTT_DEV = 1
UTT = 4
SEGS = 64
KEYS = 40


def projection_pair(key):
    base_matrix = jax.random.normal(jax.random.fold_in(key, 101), (D, D), jnp.float32) / math.sqrt(D)
    other_matrix = jax.random.normal(jax.random.fold_in(key, 202), (D, D), jnp.float32) / math.sqrt(D)
    keyed = other_matrix
    return (jnp.clip(base_matrix, -1.0, 1.0), jnp.clip(keyed, -12.0, 12.0))


def draw_w_query(key, part):
    return projection_pair(key)[0].astype(jnp.bfloat16)


def draw_w_key(key, part):
    return projection_pair(key)[1].astype(jnp.bfloat16)


def draw_lengths(key, part):
    picked = jax.random.randint(jax.random.fold_in(key, 7), (UTT,), 1, SEGS + 1)
    full_slot = jax.random.randint(jax.random.fold_in(key, 8), (UTT // UTT_DEV, 1), 0, UTT_DEV)
    is_full = (jnp.arange(UTT_DEV)[None, :] == full_slot).reshape(UTT)
    return jnp.where(is_full, SEGS, picked).astype(jnp.int32)


def levels(key, extent, shards, least, largest):
    loudness = 1.0
    for axis_at, parts in shards:
        draws = jax.random.uniform(jax.random.fold_in(jax.random.fold_in(key, 6), axis_at), (parts,), jnp.float32, least / len(shards), largest / len(shards))
        loudness = loudness * jnp.repeat(jnp.exp(draws), extent[axis_at] // parts).reshape((-1,) + (1,) * (len(extent) - 1 - axis_at))
    return loudness


def gaussian(rng, extent, width, reach, split=(), held_as=jnp.bfloat16):
    entries = jax.random.normal(rng, extent, jnp.float32) * width
    if len(split) > 0:
        entries = levels(rng, extent, split, -0.22, 0.18) * entries
    return jnp.clip(entries, min=-reach, max=reach).astype(held_as)


def setup_inputs(seed: int = 0) -> dict:
    keys = jax.random.split(jax.random.key(seed), 11)
    frames = gaussian(keys[0], (UTT, SEGS, FRAMES, D), 1.0, 6.0, ((0, 4), (1, 8)))
    memory_in = gaussian(keys[1], (UTT, SEGS, D), 1.0, 6.0, ((0, 4), (1, 8)))
    lengths = draw_lengths(jax.random.fold_in(keys[10], 71), 0)
    ln_gain = jnp.clip(1.0 + 0.15 * jax.random.normal(keys[3], (D,), jnp.float32), 0.25, 1.75)
    w_query = draw_w_query(jax.random.fold_in(keys[10], 71), 0)
    w_key = draw_w_key(jax.random.fold_in(keys[10], 71), 0)
    w_value = gaussian(keys[6], (D, D), D ** -0.5, 0.1875, ((0, 4),))
    w_out = gaussian(keys[7], (D, D), D ** -0.5, 0.1875, ((0, 4),))
    grad_frames = gaussian(keys[8], (UTT, SEGS, FRAMES, D), 1.0, 6.0, ((0, 4), (1, 8)))
    grad_memory = gaussian(keys[9], (UTT, SEGS, D), 1.0, 6.0, ((0, 4), (1, 8)))
    return dict(frames=frames, memory_in=memory_in, lengths=lengths, ln_gain=ln_gain, w_query=w_query, w_key=w_key, w_value=w_value, w_out=w_out, grad_frames=grad_frames, grad_memory=grad_memory)


epsilon = 1e-05
masked_score = -1e+30

def reference(frames, memory_in, lengths, ln_gain, w_query, w_key, w_value, w_out, grad_frames, grad_memory):
    head_dim = D // HEADS
    query_count = FRAMES + 1

    def per_utterance(running, sliced):
        utter_frames, utter_memory, utter_length, utter_grad, memory_grad = sliced
        seg_count = utter_frames.shape[0]
        wide_frames = utter_frames.astype(jnp.float32)
        row_mean = lax.optimization_barrier(jnp.mean(wide_frames, axis=-1, keepdims=True))
        centred = wide_frames - row_mean
        row_var = lax.optimization_barrier(jnp.mean(centred * centred, axis=-1, keepdims=True))
        normed = (centred * lax.rsqrt(row_var + epsilon) * ln_gain).astype(jnp.bfloat16)
        summary = lax.optimization_barrier(jnp.mean(normed.astype(jnp.float32), axis=1)).astype(jnp.bfloat16)
        query_rows = jnp.concatenate([normed, summary[:, None, :]], axis=1)
        queries = jnp.dot(query_rows.reshape(-1, D), w_query, preferred_element_type=jnp.float32).astype(jnp.bfloat16)
        queries = queries.reshape(seg_count, query_count, HEADS, head_dim).astype(jnp.float32)
        flat_normed = normed.reshape(-1, D)
        own_key = jnp.dot(flat_normed, w_key, preferred_element_type=jnp.float32).astype(jnp.bfloat16).reshape(seg_count, FRAMES, D)
        own_value = jnp.dot(flat_normed, w_value, preferred_element_type=jnp.float32).astype(jnp.bfloat16).reshape(seg_count, FRAMES, D)
        memory_key = jnp.dot(utter_memory, w_key, preferred_element_type=jnp.float32).astype(jnp.bfloat16)
        memory_value = jnp.dot(utter_memory, w_value, preferred_element_type=jnp.float32).astype(jnp.bfloat16)
        position = jnp.arange(seg_count).astype(jnp.int32)
        source = position[:, None] - 1 - jnp.arange(MEMORY).astype(jnp.int32)[None, :]
        memory_valid = source >= 0
        clipped = jnp.clip(source, 0, seg_count - 1).astype(jnp.int32)

        def window(table):
            return jnp.where(memory_valid[:, :, None], table[clipped], jnp.zeros((), table.dtype))

        def previous(block):
            return jnp.concatenate([jnp.zeros((1, LEFT, D), block.dtype), block[:-1, FRAMES - LEFT:]], axis=0)
        key_proj = jnp.concatenate([window(memory_key), previous(own_key), own_key], axis=1)
        value_proj = jnp.concatenate([window(memory_value), previous(own_value), own_value], axis=1)
        key_proj = key_proj.reshape(seg_count, KEYS, HEADS, head_dim).astype(jnp.float32)
        value_proj = value_proj.reshape(seg_count, KEYS, HEADS, head_dim).astype(jnp.float32)
        scores = jnp.einsum('sqhd,skhd->shqk', queries, key_proj) / math.sqrt(head_dim)
        left_valid = jnp.broadcast_to((position >= 1)[:, None], (seg_count, LEFT))
        own_valid = jnp.ones((seg_count, FRAMES), dtype=bool)
        valid_key = jnp.concatenate([memory_valid, left_valid, own_valid], axis=1)
        scores = jnp.where(valid_key[:, None, None, :], scores, masked_score)
        highest = lax.optimization_barrier(jnp.max(scores, axis=-1, keepdims=True))
        exponent = jnp.exp(scores - highest)
        soft_weights = (exponent / lax.optimization_barrier(jnp.sum(exponent, axis=-1, keepdims=True))).astype(jnp.bfloat16).astype(jnp.float32)
        attended = jnp.einsum('shqk,skhd->sqhd', soft_weights, value_proj).astype(jnp.bfloat16).reshape(-1, D)
        projected = jnp.dot(attended, w_out, preferred_element_type=jnp.float32).reshape(seg_count, query_count, D)
        live_mask = (position < utter_length).astype(jnp.float32)
        out_frames = (wide_frames + live_mask[:, None, None] * projected[:, :FRAMES]).astype(jnp.bfloat16)
        out_memory = (live_mask[:, None] * projected[:, FRAMES]).astype(jnp.bfloat16)
        upstream = jnp.concatenate([utter_grad, memory_grad[:, None, :]], axis=1).reshape(-1, D)
        back_proj = jnp.dot(upstream, w_out.T, preferred_element_type=jnp.float32).reshape(seg_count, query_count, D)
        grad_attended = (live_mask[:, None, None] * back_proj).astype(jnp.bfloat16)
        grad_attended = grad_attended.reshape(seg_count, query_count, HEADS, head_dim).astype(jnp.float32)
        grad_values = jnp.einsum('shqk,sqhd->skhd', soft_weights, grad_attended).astype(jnp.bfloat16)
        grad_values = grad_values.astype(jnp.float32).reshape(seg_count, KEYS, D)
        own_total = grad_values[:, MEMORY + LEFT:]
        own_total = own_total.at[:-1, FRAMES - LEFT:].add(grad_values[1:, MEMORY:MEMORY + LEFT])
        memory_total = jnp.zeros((seg_count, D), jnp.float32)
        for memory_slot in range(MEMORY):
            padded = jnp.concatenate([grad_values[:, memory_slot], jnp.zeros((1 + memory_slot, D), jnp.float32)], axis=0)
            memory_total = memory_total + padded[1 + memory_slot:1 + memory_slot + seg_count]
        grad_term = jnp.dot(flat_normed.astype(jnp.float32).T, own_total.reshape(-1, D), precision=lax.Precision.HIGHEST)
        grad_term = grad_term + jnp.dot(utter_memory.astype(jnp.float32).T, memory_total, precision=lax.Precision.HIGHEST)
        return (running + grad_term, (out_frames, out_memory))
    zero_grad = jnp.zeros((D, D), jnp.float32)
    value_grad, outputs = lax.scan(per_utterance, zero_grad, (frames, memory_in, lengths, grad_frames, grad_memory))
    return (outputs[0], outputs[1], value_grad)
```

```python
import functools
import math

import jax
import jax.numpy as jnp
from jax import lax
from jax.experimental import pallas as pl
from jax.experimental.pallas import tpu as pltpu
from jax.sharding import PartitionSpec as P

HEADS = 16
LEFT = 16
MEMORY = 8


epsilon = 1e-05
masked_score = -1e30
bf16 = jnp.bfloat16
f32 = jnp.float32
vmem = pl.BlockSpec(memory_space=pltpu.VMEM)
smem = pl.BlockSpec(memory_space=pltpu.SMEM)
NT = (((1,), (1,)), ((), ()))
TN = (((0,), (0,)), ((), ()))


def cost(flops, moved):
    return pl.CostEstimate(flops=flops, bytes_accessed=moved, transcendentals=0)


def params():
    return pltpu.CompilerParams(vmem_limit_bytes=40 * 1024 * 1024)


def swapped(array, axis, bit):
    size = lax.axis_size(axis)
    return lax.ppermute(array, axis, [(i, i ^ bit) for i in range(size)])


def passed_along(array, axis, by):
    size = lax.axis_size(axis)
    return lax.ppermute(array, axis, [(i, i + by) for i in range(size - by)])


def halving_bits(size):
    return [1 << b for b in range(size.bit_length() - 1)]


def pack_kernel(scal, wq, wk, wv, wo, gf, gm, oq, ok, ov, oo, u):
    oq[...] = wq[...]
    ok[...] = wk[...]
    oo[...] = wo[...]
    ov[...] = wv[...]
    rows = gf.shape[0]
    u[:rows, :] = gf[...]
    u[rows:, :] = jnp.concatenate([jnp.zeros(gm.shape, gm.dtype), gm[...]], axis=0)


def normed_rows(rows, gain):
    wide = rows.astype(f32)
    centred = wide - jnp.mean(wide, axis=-1, keepdims=True)
    var = jnp.mean(centred * centred, axis=-1, keepdims=True)
    return (centred * lax.rsqrt(var + epsilon) * gain).astype(bf16)


def norm_kernel(frame_count, frames, halo, mem, halo_mem, gain, x):
    rows, width = frames.shape
    segs = rows // frame_count
    gain_row = gain[...]
    x[:LEFT, :] = normed_rows(halo[...], gain_row)
    x[LEFT : LEFT + 2 * MEMORY, :] = jnp.concatenate(
        [halo_mem[...], jnp.zeros_like(halo_mem)], axis=0
    )
    start = LEFT + 2 * MEMORY
    normed = normed_rows(frames[...], gain_row)
    x[start : start + rows, :] = normed
    summary = jnp.sum(normed.astype(f32).reshape(segs, frame_count, width), axis=1) / frame_count
    x[start + rows :, :] = jnp.concatenate([mem[...], summary.astype(bf16)], axis=0)


def merge_kernel(count, *refs):
    parts, x_all, x_turned = refs[:count], refs[count], refs[count + 1]
    rows = parts[0].shape[0]
    for i in range(count):
        x_all[i * rows : (i + 1) * rows, :] = parts[i][...]
    x_turned[...] = x_all[...].T


def assemble(scal, pieces, whole, rows):
    own = scal[1]
    for j, piece in enumerate(pieces):
        at = pl.multiple_of((own ^ j) * rows, rows)
        whole[pl.ds(at, rows), :] = piece[...]


def chunk_kernel(count, group, scal, *refs):
    pieces, outs, whole = refs[:count], refs[count : count + group], refs[count + group]
    assemble(scal, pieces, whole, pieces[0].shape[0])
    rows = outs[0].shape[0]
    for i in range(group):
        at = pl.multiple_of((scal[0] ^ i) * rows, rows)
        outs[i][...] = whole[pl.ds(at, rows), :]


def head_stack(array, heads):
    width = array.shape[1]
    head = lax.broadcasted_iota(jnp.int32, array.shape, 1) // (width // heads)
    zero = jnp.zeros_like(array)
    return jnp.concatenate([jnp.where(head == h, array, zero) for h in range(heads)], axis=0)


def weights_kernel(count, heads, frame_count, segs, scal, x_all, *refs):
    wq_parts, wk_parts = refs[:count], refs[count : 2 * count]
    soft, wq, wk = refs[2 * count :]
    part_rows = wq_parts[0].shape[0]
    assemble(scal, wq_parts, wq, part_rows)
    assemble(scal, wk_parts, wk, part_rows)
    blocks, keys, lanes = soft.shape
    queries = lanes // heads
    first = keys - queries
    frames = segs * frame_count
    q_all = jnp.dot(x_all[...], wq[...], preferred_element_type=f32).astype(bf16)
    k_all = jnp.dot(x_all[...], wk[...], preferred_element_type=f32).astype(bf16)
    key = lax.broadcasted_iota(jnp.int32, (keys, lanes), 0)
    row = lax.broadcasted_iota(jnp.int32, (keys, lanes), 1)
    for h in range(1, heads):
        row = jnp.where(row >= queries, row - queries, row)
    at = jnp.where(row < frames, row // frame_count, jnp.maximum(row - frames - segs, 0))
    own = key - first
    own_seg = own // frame_count
    own_mem = own - frames
    valid_own = ((own >= 0) & (own < frames) & ((own_seg == at) | (own_seg == at - 1))) | (
        (own_mem >= 0) & (own_mem < segs) & (own_mem < at) & (own_mem >= at - MEMORY)
    )
    halo_mem = key - LEFT
    valid_halo = ((key < LEFT) & (at == 0)) | (
        (halo_mem >= 0) & (halo_mem < MEMORY) & (halo_mem >= at)
    )
    head_dim = wq.shape[1] // heads
    scale = 1.0 / math.sqrt(head_dim)
    for i in range(blocks):
        base = (scal[2] // segs ^ i) * segs
        valid = valid_own | (valid_halo & (base > 0))
        q_i = head_stack(q_all[i * keys + first : (i + 1) * keys], heads)
        scores = (
            lax.dot_general(k_all[i * keys : (i + 1) * keys], q_i, NT, preferred_element_type=f32)
            * scale
        )
        scores = jnp.where(valid, scores, masked_score)
        exponent = jnp.exp(scores - jnp.max(scores, axis=0, keepdims=True))
        soft[i] = (exponent / jnp.sum(exponent, axis=0, keepdims=True)).astype(bf16)


def grad_kernel(count, group, heads, frame_count, segs, scal, x_turned, soft, *refs):
    up, wo_parts = refs[:group], refs[group : 2 * group]
    outs, wo, whole = refs[2 * group : 2 * group + count], refs[-2], refs[-1]
    width = wo_parts[0].shape[1]
    blocks, keys, lanes = soft.shape
    queries = lanes // heads
    frames = segs * frame_count
    for i in range(group):
        at = pl.multiple_of((scal[0] ^ i) * width, width)
        wo[:, pl.ds(at, width)] = wo_parts[i][...]
    row = lax.broadcasted_iota(jnp.int32, (queries, width), 0)
    seg_of = jnp.where(row < frames, row // frame_count, row - frames - segs)
    values = []
    for i in range(group):
        base = (scal[2] // segs ^ i) * segs
        back = lax.dot_general(up[i][...], wo[...], NT, preferred_element_type=f32)
        live = (base + seg_of < scal[3]).astype(f32)
        grad_attended = head_stack((live * back).astype(bf16), heads)
        values.append(
            jnp.dot(soft[i], grad_attended, preferred_element_type=f32).astype(bf16)
        )
    whole[...] = jnp.dot(
        x_turned[...], jnp.concatenate(values, axis=0), preferred_element_type=f32
    ).astype(bf16)
    rows = outs[0].shape[0]
    for j in range(count):
        at = pl.multiple_of((scal[1] ^ j) * rows, rows)
        outs[j][...] = whole[pl.ds(at, rows), :]


def out_kernel(count, heads, scal, x_all, soft, wo, *refs):
    wv_parts, keep, send, wv = refs[:count], refs[count], refs[count + 1], refs[count + 2]
    assemble(scal, wv_parts, wv, wv_parts[0].shape[0])
    blocks, keys, lanes = soft.shape
    queries = lanes // heads
    v_all = jnp.dot(x_all[...], wv[...], preferred_element_type=f32).astype(bf16)
    width = wv.shape[1]
    head = lax.broadcasted_iota(jnp.int32, (queries, width), 1) // (width // heads)
    for i in range(blocks):
        stacked = lax.dot_general(
            soft[i], v_all[i * keys : (i + 1) * keys], TN, preferred_element_type=f32
        )
        attended = stacked[:queries]
        for h in range(1, heads):
            attended = jnp.where(head == h, stacked[h * queries : (h + 1) * queries], attended)
        projected = jnp.dot(attended.astype(bf16), wo[...], preferred_element_type=f32)
        into = send if i & 1 else keep
        into[i // 2] = projected.astype(into.dtype)


def on_device(
    frames, memory_in, lengths, ln_gain, w_query, w_key, w_value, w_out, grad_frames, grad_memory
):
    utterances, segs, frame_count, width = frames.shape
    seg_size = lax.axis_size("seg")
    fsdp_size = lax.axis_size("fsdp")
    group = 4
    assert utterances == 1 and segs == MEMORY and frame_count == LEFT and seg_size % group == 0
    heads = HEADS // group
    block = width // group
    rows = w_query.shape[0]
    frame_rows = segs * frame_count
    queries = frame_rows + 2 * segs
    keys = LEFT + 2 * MEMORY + queries
    seg = lax.axis_index("seg")
    member = seg % group
    scal = jnp.stack(
        [member, lax.axis_index("fsdp"), seg * segs, lengths[0]]
    ).astype(jnp.int32)
    flat_frames = frames.reshape(frame_rows, width)
    flat_mem = memory_in.reshape(segs, width)

    halo = passed_along(frames[0, segs - 1, frame_count - LEFT :], "seg", 1)
    halo_mem = passed_along(flat_mem[segs - MEMORY :], "seg", 1)

    column = pl.BlockSpec((rows, block), lambda i, s: (0, s[0]))
    whole = lambda a, b: pl.BlockSpec((a, b), lambda i, s: (0, 0))
    wq, wk, wv, wo, up = pl.pallas_call(
        pack_kernel,
        grid_spec=pltpu.PrefetchScalarGridSpec(
            num_scalar_prefetch=1,
            grid=(1,),
            in_specs=[column] * 4 + [whole(frame_rows, width), whole(segs, width)],
            out_specs=[whole(rows, block)] * 4 + [whole(queries, width)],
        ),
        out_shape=[jax.ShapeDtypeStruct((rows, block), bf16)] * 4
        + [jax.ShapeDtypeStruct((queries, width), bf16)],
        compiler_params=params(),
        cost_estimate=cost(0, 4 * 1024 * 1024),
        name="pack",
    )(
        scal, w_query, w_key, w_value, w_out,
        grad_frames.reshape(frame_rows, width), grad_memory.reshape(segs, width),
    )

    x_own = pl.pallas_call(
        functools.partial(norm_kernel, frame_count),
        in_specs=[vmem] * 5,
        out_specs=vmem,
        out_shape=jax.ShapeDtypeStruct((keys, width), bf16),
        compiler_params=params(),
        cost_estimate=cost(0, 2 * 1024 * 1024),
        name="norm",
    )(flat_frames, halo, flat_mem, halo_mem, ln_gain.reshape(1, width))

    bits = halving_bits(fsdp_size)

    def gathered(piece, order):
        pieces = {0: piece}
        for bit in order:
            for have in sorted(pieces):
                pieces[have ^ bit] = swapped(pieces[have], "fsdp", bit)
        return [pieces[j] for j in range(fsdp_size)]

    def grouped(piece):
        far = swapped(piece, "seg", 2)
        return [piece, swapped(piece, "seg", 1), far, swapped(far, "seg", 1)]

    wo_parts = gathered(wo, bits)
    wq_parts = gathered(wq, bits[::-1])
    wk_parts = gathered(wk, bits)
    wv_parts = gathered(wv, bits[::-1])
    up_parts = grouped(up)
    x_parts = grouped(x_own)

    chunks = pl.pallas_call(
        functools.partial(chunk_kernel, fsdp_size, group),
        in_specs=[smem] + [vmem] * fsdp_size,
        out_specs=[vmem] * group,
        out_shape=[jax.ShapeDtypeStruct((block, block), bf16)] * group,
        scratch_shapes=[pltpu.VMEM((width, block), bf16)],
        compiler_params=params(),
        cost_estimate=cost(0, 1024 * 1024),
        name="wo_chunks",
    )(scal, *wo_parts)
    wo_rows = [chunks[0]] + [swapped(chunks[i], "seg", i) for i in range(1, group)]

    x_all, x_turned = pl.pallas_call(
        functools.partial(merge_kernel, group),
        in_specs=[vmem] * group,
        out_specs=[vmem] * 2,
        out_shape=[
            jax.ShapeDtypeStruct((group * keys, width), bf16),
            jax.ShapeDtypeStruct((width, group * keys), bf16),
        ],
        compiler_params=params(),
        cost_estimate=cost(0, 5 * 1024 * 1024),
        name="merge",
    )(*x_parts)

    soft = pl.pallas_call(
        functools.partial(weights_kernel, fsdp_size, heads, frame_count, segs),
        in_specs=[smem] + [vmem] * (1 + 2 * fsdp_size),
        out_specs=vmem,
        out_shape=jax.ShapeDtypeStruct((group, keys, heads * queries), bf16),
        scratch_shapes=[pltpu.VMEM((width, block), bf16)] * 2,
        compiler_params=params(),
        cost_estimate=cost(2 * 2 * group * keys * width * block, 4 * 1024 * 1024),
        name="soft_weights",
    )(scal, x_all, *wq_parts, *wk_parts)

    *grad_chunks, wo_mine = pl.pallas_call(
        functools.partial(grad_kernel, fsdp_size, group, heads, frame_count, segs),
        in_specs=[smem] + [vmem] * (2 + 2 * group),
        out_specs=[vmem] * (fsdp_size + 1),
        out_shape=[jax.ShapeDtypeStruct((rows, block), bf16)] * fsdp_size
        + [jax.ShapeDtypeStruct((block, width), bf16)],
        scratch_shapes=[pltpu.VMEM((width, block), bf16)],
        compiler_params=params(),
        cost_estimate=cost(2 * 2 * group * keys * width * block, 5 * 1024 * 1024),
        name="value_grad",
    )(scal, x_turned, soft, *up_parts, *wo_rows)

    grad_sum = grad_chunks[0].astype(f32)
    for j in range(1, fsdp_size):
        grad_sum = grad_sum + swapped(grad_chunks[j], "fsdp", j).astype(f32)
    bit = group
    while bit < seg_size:
        mine = grad_sum.astype(bf16)
        grad_sum = mine.astype(f32) + swapped(mine, "seg", bit).astype(f32)
        bit *= 2
    mine = grad_sum.astype(bf16)

    keep, send = pl.pallas_call(
        functools.partial(out_kernel, fsdp_size, heads),
        in_specs=[smem] + [vmem] * (3 + fsdp_size),
        out_specs=[vmem] * 2,
        out_shape=[
            jax.ShapeDtypeStruct((group // 2, queries, width), f32),
            jax.ShapeDtypeStruct((group // 2, queries, width), bf16),
        ],
        scratch_shapes=[pltpu.VMEM((width, block), bf16)],
        compiler_params=params(),
        cost_estimate=cost(2 * 2 * group * keys * width * block, 5 * 1024 * 1024),
        name="attend_project",
    )(scal, x_all, soft, wo_mine, *wv_parts)
    keep = keep + swapped(send, "seg", 1).astype(f32)
    projected = keep[0] + swapped(keep[1].astype(bf16), "seg", 2).astype(f32)

    live = (seg * segs + jnp.arange(segs) < lengths[0]).astype(f32)
    frames_out = (
        frames.astype(f32)
        + live[None, :, None, None]
        * projected[:frame_rows].reshape(1, segs, frame_count, width)
    ).astype(bf16)
    memory_out = (live[None, :, None] * projected[None, frame_rows + segs :]).astype(bf16)

    far = swapped(mine, "seg", 2)
    high = (member & 2) > 0
    pair = jnp.stack([jnp.where(high, far, mine), jnp.where(high, mine, far)])
    near = swapped(pair, "seg", 1)
    odd = (member & 1) > 0
    value_grad = jnp.concatenate(
        [
            part[j]
            for j in range(2)
            for part in (jnp.where(odd, near, pair), jnp.where(odd, pair, near))
        ],
        axis=1,
    ).astype(f32)
    return (frames_out, memory_out, value_grad)


def solution(mesh):
    return jax.shard_map(
        on_device,
        mesh=mesh,
        in_specs=(
            P("fsdp", "seg", None, None),
            P("fsdp", "seg", None),
            P("fsdp"),
            P(),
            P("fsdp", None),
            P("fsdp", None),
            P("fsdp", None),
            P("fsdp", None),
            P("fsdp", "seg", None, None),
            P("fsdp", "seg", None),
        ),
        out_specs=(P("fsdp", "seg", None, None), P("fsdp", "seg", None), P("fsdp", None)),
        check_vma=False,
    )
```

```python
import functools
import math

import jax
import jax.numpy as jnp
from jax import lax
from jax.experimental import pallas as pl
from jax.experimental.pallas import tpu as pltpu
from jax.sharding import PartitionSpec as P

HEADS = 16
LEFT = 16
MEMORY = 8
GROUP = 4


epsilon = 1e-05
masked_score = -1e30
bf16 = jnp.bfloat16
f32 = jnp.float32
vmem = pl.BlockSpec(memory_space=pltpu.VMEM)
smem = pl.BlockSpec(memory_space=pltpu.SMEM)
hbm = pl.BlockSpec(memory_space=pltpu.HBM)
NT = (((1,), (1,)), ((), ()))
TN = (((0,), (0,)), ((), ()))


def params(mib=40):
    return pltpu.CompilerParams(vmem_limit_bytes=mib * 1024 * 1024)


def swapped(array, axis, bit):
    size = lax.axis_size(axis)
    return lax.ppermute(array, axis, [(i, i ^ bit) for i in range(size)])


def halving_bits(size):
    return [1 << b for b in range(size.bit_length() - 1)]


def member_of():
    return lax.axis_index("seg") % GROUP


def aligned(start, step):
    return pl.multiple_of(start * step, step)


def normed_rows(rows, gain):
    wide = rows.astype(f32)
    centred = wide - jnp.mean(wide, axis=-1, keepdims=True)
    var = jnp.mean(centred * centred, axis=-1, keepdims=True)
    return (centred * lax.rsqrt(var + epsilon) * gain).astype(bf16)


def pack_kernel(frame_count, wq, wk, wv, frames, gf, mem, gm, gain, *refs):
    blocks, (tokens, raw, few, one, sems) = refs[:-5], refs[-5:]
    width = blocks[0].shape[1] // 3
    rows, model_width = gf.shape
    segs = mem.shape[0]
    half = tokens.shape[0] // 2
    copies = [
        pltpu.make_async_copy(frames, raw, sems.at[0]),
        pltpu.make_async_copy(gain, one, sems.at[1]),
        pltpu.make_async_copy(mem, few.at[0], sems.at[2]),
        pltpu.make_async_copy(gm, few.at[1], sems.at[3]),
        pltpu.make_async_copy(gf, tokens.at[pl.ds(half, rows)], sems.at[4]),
    ]
    for i, block in enumerate(blocks):
        at = aligned(member_of() ^ i, width)
        for j, w in enumerate((wq, wk, wv)):
            into = block.at[:, pl.ds(j * width, width)]
            sem = sems.at[5 + 3 * i + j]
            copies.append(pltpu.make_async_copy(w.at[:, pl.ds(at, width)], into, sem))
    for copy in copies:
        copy.start()
    for copy in copies[:4]:
        copy.wait()
    normed = normed_rows(raw[...], one[...])
    tokens[:rows, :] = normed
    summary = jnp.sum(normed.astype(f32).reshape(segs, frame_count, model_width), axis=1)
    tokens[rows:half, :] = jnp.concatenate(
        [few[0], (summary / frame_count).astype(bf16)], axis=0
    )
    tokens[half + rows :, :] = jnp.concatenate([jnp.zeros_like(few[1]), few[1]], axis=0)
    for copy in copies[4:]:
        copy.wait()


def merge_kernel(group, *refs):
    parts, halo_a, halo_b, x_all, x_turned, u_all = refs[:group], *refs[group:]
    half = parts[0].shape[0] // 2
    halo = halo_a.shape[0]
    odd = (member_of() & 1) > 0
    x_all[:halo, :] = jnp.where(odd, halo_b[...], halo_a[...])
    for i in range(group):
        at = aligned(member_of() ^ i, half)
        x_all[pl.ds(pl.multiple_of(halo + at, 16), half), :] = parts[i][:half, :]
        u_all[pl.ds(at, half), :] = parts[i][half:, :]
    x_turned[...] = x_all[...].T


def assemble(pieces, whole, crossed):
    own = lax.axis_index("fsdp")
    rows = pieces[0].shape[0]
    flip = lax.axis_index("seg") & 1 if crossed else 0
    for j, piece in enumerate(pieces):
        apart = j ^ (3 * flip) if j in (1, 2) else j
        whole[pl.ds(aligned(own ^ apart, rows), rows), :] = piece[...]


def head_stack(array, heads):
    width = array.shape[1]
    head = lax.broadcasted_iota(jnp.int32, array.shape, 1) // (width // heads)
    zero = jnp.zeros_like(array)
    return jnp.concatenate([jnp.where(head == h, array, zero) for h in range(heads)], axis=0)


def weights_kernel(heads, frame_count, segs, crossed, x_all, *refs):
    soft, values, wqkv = refs[-3:]
    assemble(refs[:-3], wqkv, crossed)
    blocks, keys, lanes = soft.shape
    queries = lanes // heads
    halo = keys - queries
    frames = segs * frame_count
    block = values.shape[1]
    projected = jnp.dot(x_all[...], wqkv[...], preferred_element_type=f32).astype(bf16)
    q_all, k_all = projected[:, :block], projected[:, block : 2 * block]
    values[...] = projected[:, 2 * block :]
    key = lax.broadcasted_iota(jnp.int32, (keys, lanes), 0)
    row = lax.broadcasted_iota(jnp.int32, (keys, lanes), 1)
    for h in range(1, heads):
        row = jnp.where(row >= queries, row - queries, row)
    at = jnp.where(row < frames, row // frame_count, jnp.maximum(row - frames - segs, 0))
    own = key - halo
    own_seg = own // frame_count
    own_mem = own - frames
    valid_own = ((own >= 0) & (own < frames) & ((own_seg == at) | (own_seg == at - 1))) | (
        (own_mem >= 0) & (own_mem < segs) & (own_mem < at) & (own_mem >= at - MEMORY)
    )
    halo_mem = key - LEFT
    valid_halo = ((key < LEFT) & (at == 0)) | (
        (halo_mem >= 0) & (halo_mem < MEMORY) & (halo_mem >= at)
    )
    inside = lax.axis_index("seg") >= blocks
    scale = 1.0 / math.sqrt(block // heads)
    for b in range(blocks):
        valid = valid_own | (valid_halo & inside if b == 0 else valid_halo)
        start = b * queries
        q_b = head_stack(q_all[halo + start : halo + start + queries], heads)
        scores = (
            lax.dot_general(k_all[start : start + keys], q_b, NT, preferred_element_type=f32)
            * scale
        )
        scores = jnp.where(valid, scores, masked_score)
        exponent = jnp.exp(scores - jnp.max(scores, axis=0, keepdims=True))
        soft[b] = (exponent / jnp.sum(exponent, axis=0, keepdims=True)).astype(bf16)


def grad_kernel(count, heads, frame_count, segs, crossed, lengths, x_turned, u_all, soft, *refs):
    outputs = 2 if crossed else count
    wo_from, outs = refs[: -outputs - 3], refs[-outputs - 3 : -3]
    wo, values, whole = refs[-3:]
    blocks, keys, lanes = soft.shape
    queries = lanes // heads
    frames = segs * frame_count
    chosen = wo_from[0][...]
    if len(wo_from) > 1:
        apart = lax.axis_index("fsdp") ^ member_of()
        chosen = jnp.where(
            apart == 0, chosen, jnp.where(apart == 3, wo_from[2][...], wo_from[1][...])
        )
    wo[...] = chosen
    back = lax.dot_general(u_all[...], chosen, NT, preferred_element_type=f32)
    row = lax.broadcasted_iota(jnp.int32, (queries, wo.shape[0]), 0)
    seg_of = jnp.where(row < frames, row // frame_count, row - frames - segs)
    first = lax.axis_index("seg") - member_of()
    values[: keys - queries, :] = jnp.zeros((keys - queries, values.shape[1]), f32)
    for b in range(blocks):
        start = b * queries
        live = ((first + b) * segs + seg_of < lengths[0]).astype(f32)
        grad_attended = head_stack((live * back[start : start + queries]).astype(bf16), heads)
        term = jnp.dot(soft[b], grad_attended, preferred_element_type=f32)
        split = keys - queries
        values[start : start + split, :] += term[:split]
        values[start + split : start + keys, :] = term[split:]
    whole[...] = jnp.dot(
        x_turned[...], values[...].astype(bf16), preferred_element_type=f32
    )
    own = lax.axis_index("fsdp")
    rows = whole.shape[0] // count

    def part(apart, into):
        return whole[pl.ds(aligned(own ^ apart, rows), rows), :].astype(into.dtype)

    if crossed:
        keep, send = outs
        along = 1 + (lax.axis_index("seg") & 1)
        keep[0] = part(0, keep)
        keep[1] = part(along ^ 3, keep)
        send[0] = part(along, send)
        send[1] = part(3, send)
    else:
        for j in range(count):
            outs[j][...] = part(j, outs[j])


def out_kernel(heads, soft, values, wo, keep, send):
    blocks, keys, lanes = soft.shape
    queries = lanes // heads
    width = values.shape[1]
    head = lax.broadcasted_iota(jnp.int32, (queries, width), 1) // (width // heads)
    for i in range(blocks):
        b = member_of() ^ i
        stacked = lax.dot_general(
            soft[b],
            values[pl.ds(aligned(b, queries), keys), :],
            TN,
            preferred_element_type=f32,
        )
        attended = stacked[:queries]
        for h in range(1, heads):
            attended = jnp.where(head == h, stacked[h * queries : (h + 1) * queries], attended)
        projected = jnp.dot(attended.astype(bf16), wo[...], preferred_element_type=f32)
        into = send if i & 1 else keep
        into[i // 2] = projected.astype(into.dtype)


def gathered(piece):
    size = lax.axis_size("fsdp")
    pieces = {0: piece}
    bit = 1
    while bit < size:
        for have in sorted(pieces):
            pieces[have ^ bit] = swapped(pieces[have], "fsdp", bit)
        bit *= 2
    return [pieces[j] for j in range(size)]


def pairs(seg_size):
    straight, turned, beside, across = [], [], [], []
    for s in range(seg_size):
        along = 2 if s & 1 else 1
        for f in range(GROUP):
            straight.append((s * GROUP + f, s * GROUP + (f ^ along)))
            turned.append((s * GROUP + f, s * GROUP + (f ^ along ^ 3)))
        k = s % GROUP
        beside.append((s * GROUP + k, s * GROUP + (k ^ 1)))
        beside.append(((s ^ 1) * GROUP + k, s * GROUP + (k ^ 2)))
        across.append((s * GROUP + (k ^ 2), s * GROUP + (k ^ 3)))
    return straight, turned, beside, across


def on_device(
    frames, memory_in, lengths, ln_gain, w_query, w_key, w_value, w_out, grad_frames, grad_memory
):
    utterances, segs, frame_count, width = frames.shape
    seg_size = lax.axis_size("seg")
    fsdp_size = lax.axis_size("fsdp")
    group = GROUP
    assert utterances == 1 and segs == MEMORY and frame_count == LEFT and seg_size % group == 0
    heads = HEADS // group
    block = width // group
    rows = w_query.shape[0]
    frame_rows = segs * frame_count
    queries = frame_rows + 2 * segs
    halo_rows = LEFT + 2 * MEMORY
    keys = halo_rows + queries
    all_rows = halo_rows + group * queries
    seg = lax.axis_index("seg")
    member = seg % group

    crossed = fsdp_size == group
    *own_blocks, tokens = pl.pallas_call(
        functools.partial(pack_kernel, frame_count),
        in_specs=[hbm] * 8,
        out_specs=[vmem] * (2 + crossed),
        out_shape=[jax.ShapeDtypeStruct((rows, 3 * block), bf16)] * (1 + crossed)
        + [
            jax.ShapeDtypeStruct((2 * queries, width), bf16),
        ],
        scratch_shapes=[
            pltpu.VMEM((frame_rows, width), bf16),
            pltpu.VMEM((2, segs, width), bf16),
            pltpu.VMEM((1, width), f32),
            pltpu.SemaphoreType.DMA((11,)),
        ],
        compiler_params=params(60),
        name="pack",
    )(
        w_query, w_key, w_value, frames.reshape(frame_rows, width),
        grad_frames.reshape(frame_rows, width), memory_in.reshape(segs, width),
        grad_memory.reshape(segs, width), ln_gain.reshape(1, width),
    )
    w_out, own_blocks = lax.optimization_barrier((w_out, own_blocks))

    far = swapped(tokens, "seg", 2)
    near = swapped(tokens, "seg", 1)
    cut = slice(queries - halo_rows, queries)
    tail = jnp.where(member == group - 1, tokens[cut], near[cut])
    if crossed:
        both = ("seg", "fsdp")
        straight, turned, beside, across = pairs(seg_size)
        mine = lax.ppermute(own_blocks[0], both, straight)
        other = lax.ppermute(own_blocks[1], both, straight)
        wo_near = lax.ppermute(w_out, both, beside)
        wqkv_parts = [
            own_blocks[0], mine, swapped(other, "seg", 1), lax.ppermute(mine, both, turned)
        ]
        wo_from = [w_out, wo_near, lax.ppermute(wo_near, both, across)]
    else:
        wqkv_parts = gathered(own_blocks[0])
        wo_from = [
            lax.dynamic_slice_in_dim(
                lax.all_gather(w_out, "fsdp", axis=0, tiled=True), member * block, block, 0
            )
        ]
    ahead = []
    for s in range(group, seg_size, group):
        ahead += [(s - 1, s), (s - 2, s + 2)]
    halo_even = lax.ppermute(tail, "seg", ahead)
    halo_odd = lax.ppermute(halo_even, "seg", [(s, s + 1) for s in range(0, seg_size, 2)])
    parts = [tokens, near, far, swapped(far, "seg", 1)]

    x_all, x_turned, u_all = pl.pallas_call(
        functools.partial(merge_kernel, group),
        in_specs=[vmem] * (group + 2),
        out_specs=[vmem] * 3,
        out_shape=[
            jax.ShapeDtypeStruct((all_rows, width), bf16),
            jax.ShapeDtypeStruct((width, all_rows), bf16),
            jax.ShapeDtypeStruct((group * queries, width), bf16),
        ],
        compiler_params=params(),
        name="merge",
    )(*parts, halo_even, halo_odd)

    soft, values = pl.pallas_call(
        functools.partial(weights_kernel, heads, frame_count, segs, crossed),
        in_specs=[vmem] * (1 + fsdp_size),
        out_specs=[vmem] * 2,
        out_shape=[
            jax.ShapeDtypeStruct((group, keys, heads * queries), bf16),
            jax.ShapeDtypeStruct((all_rows, block), bf16),
        ],
        scratch_shapes=[pltpu.VMEM((width, 3 * block), bf16)],
        compiler_params=params(),
        name="soft_weights",
    )(x_all, *wqkv_parts)

    if crossed:
        grad_shapes = [jax.ShapeDtypeStruct((2, rows, block), dtype) for dtype in (f32, bf16)]
    else:
        grad_shapes = [jax.ShapeDtypeStruct((rows, block), bf16)] * fsdp_size
    *grad_chunks, wo_mine = pl.pallas_call(
        functools.partial(grad_kernel, fsdp_size, heads, frame_count, segs, crossed),
        in_specs=[smem] + [vmem] * (3 + len(wo_from)),
        out_specs=[vmem] * (len(grad_shapes) + 1),
        out_shape=grad_shapes + [jax.ShapeDtypeStruct((block, width), bf16)],
        scratch_shapes=[
            pltpu.VMEM((all_rows, block), f32),
            pltpu.VMEM((width, block), f32),
        ],
        compiler_params=params(),
        name="value_grad",
    )(lengths, x_turned, u_all, soft, *wo_from)

    keep, send = pl.pallas_call(
        functools.partial(out_kernel, heads),
        in_specs=[vmem] * 3,
        out_specs=[vmem] * 2,
        out_shape=[
            jax.ShapeDtypeStruct((group // 2, queries, width), f32),
            jax.ShapeDtypeStruct((group // 2, queries, width), bf16),
        ],
        compiler_params=params(),
        name="attend_project",
    )(soft, values, wo_mine)
    near = swapped(send, "seg", 1)
    onward = (keep[1] + near[1].astype(f32)).astype(bf16)
    if crossed:
        kept, sent = grad_chunks
        came = lax.ppermute(sent, both, straight)
        came, _ = lax.optimization_barrier((came, send))
        passing = (kept[1] + came[1].astype(f32)).astype(bf16)
        grad_sum = kept[0] + came[0].astype(f32)
        grad_sum = grad_sum + lax.ppermute(passing, both, turned).astype(f32)
    else:
        grad_sum = grad_chunks[0].astype(f32)
        for j in range(1, fsdp_size):
            grad_sum = grad_sum + swapped(grad_chunks[j], "fsdp", j).astype(f32)
    bit = group
    while bit < seg_size:
        mine = grad_sum.astype(bf16)
        grad_sum = mine.astype(f32) + swapped(mine, "seg", bit).astype(f32)
        bit *= 2
    mine = grad_sum.astype(bf16)
    projected = keep[0] + near[0].astype(f32) + swapped(onward, "seg", 2).astype(f32)

    live = (seg * segs + jnp.arange(segs) < lengths[0]).astype(f32)
    frames_out = (
        frames.astype(f32)
        + live[None, :, None, None]
        * projected[:frame_rows].reshape(1, segs, frame_count, width)
    ).astype(bf16)
    memory_out = (live[None, :, None] * projected[None, frame_rows + segs :]).astype(bf16)

    far = swapped(mine, "seg", 2)
    high = (member & 2) > 0
    pair = jnp.stack([jnp.where(high, far, mine), jnp.where(high, mine, far)])
    near = swapped(pair, "seg", 1)
    odd = (member & 1) > 0
    value_grad = jnp.concatenate(
        [
            part[j]
            for j in range(2)
            for part in (jnp.where(odd, near, pair), jnp.where(odd, pair, near))
        ],
        axis=1,
    ).astype(f32)
    return (frames_out, memory_out, value_grad)


def solution(mesh):
    return jax.shard_map(
        on_device,
        mesh=mesh,
        in_specs=(
            P("fsdp", "seg", None, None),
            P("fsdp", "seg", None),
            P("fsdp"),
            P(),
            P("fsdp", None),
            P("fsdp", None),
            P("fsdp", None),
            P("fsdp", None),
            P("fsdp", "seg", None, None),
            P("fsdp", "seg", None),
        ),
        out_specs=(P("fsdp", "seg", None, None), P("fsdp", "seg", None), P("fsdp", None)),
        check_vma=False,
    )
```

```python
import functools
import math

import jax
import jax.numpy as jnp
from jax import lax
from jax.experimental import pallas as pl
from jax.experimental.pallas import tpu as pltpu
from jax.sharding import PartitionSpec as P

HEADS = 16
LEFT = 16
MEMORY = 8
GROUP = 4


epsilon = 1e-05
masked_score = -1e30
bf16 = jnp.bfloat16
f32 = jnp.float32
vmem = pl.BlockSpec(memory_space=pltpu.VMEM)
smem = pl.BlockSpec(memory_space=pltpu.SMEM)
hbm = pl.BlockSpec(memory_space=pltpu.HBM)
NT = (((1,), (1,)), ((), ()))
TN = (((0,), (0,)), ((), ()))


def params(mib=40):
    return pltpu.CompilerParams(vmem_limit_bytes=mib * 1024 * 1024)


def swapped(array, axis, bit):
    size = lax.axis_size(axis)
    return lax.ppermute(array, axis, [(i, i ^ bit) for i in range(size)])


def halving_bits(size):
    return [1 << b for b in range(size.bit_length() - 1)]


def member_of():
    return lax.axis_index("seg") % GROUP


def aligned(start, step):
    return pl.multiple_of(start * step, step)


def normed_rows(rows, gain):
    wide = rows.astype(f32)
    centred = wide - jnp.mean(wide, axis=-1, keepdims=True)
    var = jnp.mean(centred * centred, axis=-1, keepdims=True)
    return (centred * lax.rsqrt(var + epsilon) * gain).astype(bf16)


def pack_kernel(frame_count, wq, wk, wv, frames, gf, mem, gm, gain, *refs):
    blocks, tokens, raw, few, one, sems = refs
    width = blocks.shape[2] // 3
    rows, model_width = gf.shape
    segs = mem.shape[0]
    half = tokens.shape[0] // 2
    copies = [
        pltpu.make_async_copy(frames, raw, sems.at[0]),
        pltpu.make_async_copy(gain, one, sems.at[1]),
        pltpu.make_async_copy(mem, few.at[0], sems.at[2]),
        pltpu.make_async_copy(gm, few.at[1], sems.at[3]),
        pltpu.make_async_copy(gf, tokens.at[pl.ds(half, rows)], sems.at[4]),
    ]
    for i in range(blocks.shape[0]):
        at = aligned(member_of() ^ i, width)
        for j, w in enumerate((wq, wk, wv)):
            into = blocks.at[i, :, pl.ds(j * width, width)]
            sem = sems.at[5 + 3 * i + j]
            copies.append(pltpu.make_async_copy(w.at[:, pl.ds(at, width)], into, sem))
    for copy in copies:
        copy.start()
    for copy in copies[:4]:
        copy.wait()
    normed = normed_rows(raw[...], one[...])
    tokens[:rows, :] = normed
    summary = jnp.sum(normed.astype(f32).reshape(segs, frame_count, model_width), axis=1)
    tokens[rows:half, :] = jnp.concatenate(
        [few[0], (summary / frame_count).astype(bf16)], axis=0
    )
    tokens[half + rows :, :] = jnp.concatenate([jnp.zeros_like(few[1]), few[1]], axis=0)
    for copy in copies[4:]:
        copy.wait()


def split_kernel(both, mine, other):
    mine[...] = both[0]
    other[...] = both[1]


def merge_kernel(group, *refs):
    parts, halo_a, halo_b, wo_from = refs[:group], *refs[group : group + 2], refs[group + 2 : -4]
    x_all, x_turned, u_all, wo = refs[-4:]
    half = parts[0].shape[0] // 2
    halo = halo_a.shape[0]
    odd = (member_of() & 1) > 0
    x_all[:halo, :] = jnp.where(odd, halo_b[...], halo_a[...])
    for i in range(group):
        at = aligned(member_of() ^ i, half)
        x_all[pl.ds(pl.multiple_of(halo + at, 16), half), :] = parts[i][:half, :]
        u_all[pl.ds(at, half), :] = parts[i][half:, :]
    x_turned[...] = x_all[...].T
    wo[...] = wo_from[0][...]
    if len(wo_from) > 1:
        wo[...] = jnp.where(lax.axis_index("fsdp") == member_of(), wo[...], wo_from[1][...])


def assemble(pieces, whole, crossed):
    own = lax.axis_index("fsdp")
    rows = pieces[0].shape[-2]
    flip = lax.axis_index("seg") & 1 if crossed else 0
    for j, piece in enumerate(pieces):
        apart = j ^ (3 * flip) if j in (1, 2) else j
        into = whole.at[pl.ds(aligned(own ^ apart, rows), rows), :]
        into[...] = piece[0] if len(piece.shape) == 3 else piece[...]


def head_stack(array, heads):
    width = array.shape[1]
    head = lax.broadcasted_iota(jnp.int32, array.shape, 1) // (width // heads)
    zero = jnp.zeros_like(array)
    return jnp.concatenate([jnp.where(head == h, array, zero) for h in range(heads)], axis=0)


def weights_kernel(heads, frame_count, segs, crossed, x_all, *refs):
    soft, values, wqkv = refs[-3:]
    assemble(refs[:-3], wqkv, crossed)
    blocks, keys, lanes = soft.shape
    queries = lanes // heads
    halo = keys - queries
    frames = segs * frame_count
    block = values.shape[1]
    projected = jnp.dot(x_all[...], wqkv[...], preferred_element_type=f32).astype(bf16)
    q_all, k_all = projected[:, :block], projected[:, block : 2 * block]
    values[...] = projected[:, 2 * block :]
    key = lax.broadcasted_iota(jnp.int32, (keys, lanes), 0)
    row = lax.broadcasted_iota(jnp.int32, (keys, lanes), 1)
    for h in range(1, heads):
        row = jnp.where(row >= queries, row - queries, row)
    at = jnp.where(row < frames, row // frame_count, jnp.maximum(row - frames - segs, 0))
    own = key - halo
    own_seg = own // frame_count
    own_mem = own - frames
    valid_own = ((own >= 0) & (own < frames) & ((own_seg == at) | (own_seg == at - 1))) | (
        (own_mem >= 0) & (own_mem < segs) & (own_mem < at) & (own_mem >= at - MEMORY)
    )
    halo_mem = key - LEFT
    valid_halo = ((key < LEFT) & (at == 0)) | (
        (halo_mem >= 0) & (halo_mem < MEMORY) & (halo_mem >= at)
    )
    inside = lax.axis_index("seg") >= blocks
    scale = 1.0 / math.sqrt(block // heads)
    for b in range(blocks):
        valid = valid_own | (valid_halo & inside if b == 0 else valid_halo)
        start = b * queries
        q_b = head_stack(q_all[halo + start : halo + start + queries], heads)
        scores = (
            lax.dot_general(k_all[start : start + keys], q_b, NT, preferred_element_type=f32)
            * scale
        )
        scores = jnp.where(valid, scores, masked_score)
        exponent = jnp.exp(scores - jnp.max(scores, axis=0, keepdims=True))
        soft[b] = (exponent / jnp.sum(exponent, axis=0, keepdims=True)).astype(bf16)


def grad_kernel(count, heads, frame_count, segs, crossed, lengths, x_turned, u_all, soft, *refs):
    outputs = 2 if crossed else count
    wo_from, outs = refs[: -outputs - 3], refs[-outputs - 3 : -3]
    wo, values, whole = refs[-3:]
    blocks, keys, lanes = soft.shape
    queries = lanes // heads
    frames = segs * frame_count
    wo[...] = wo_from[0][...]
    if len(wo_from) > 1:
        opposite = (lax.axis_index("fsdp") ^ member_of()) == 3
        wo[...] = jnp.where(opposite, wo_from[1][...], wo[...])
    back = lax.dot_general(u_all[...], wo[...], NT, preferred_element_type=f32)
    row = lax.broadcasted_iota(jnp.int32, (queries, wo.shape[0]), 0)
    seg_of = jnp.where(row < frames, row // frame_count, row - frames - segs)
    first = lax.axis_index("seg") - member_of()
    values[: keys - queries, :] = jnp.zeros((keys - queries, values.shape[1]), f32)
    for b in range(blocks):
        start = b * queries
        live = ((first + b) * segs + seg_of < lengths[0]).astype(f32)
        grad_attended = head_stack((live * back[start : start + queries]).astype(bf16), heads)
        term = jnp.dot(soft[b], grad_attended, preferred_element_type=f32)
        split = keys - queries
        values[start : start + split, :] += term[:split]
        values[start + split : start + keys, :] = term[split:]
    whole[...] = jnp.dot(
        x_turned[...], values[...].astype(bf16), preferred_element_type=f32
    )
    own = lax.axis_index("fsdp")
    rows = whole.shape[0] // count

    def part(apart, into):
        return whole[pl.ds(aligned(own ^ apart, rows), rows), :].astype(into.dtype)

    if crossed:
        keep, send = outs
        along = 1 + (lax.axis_index("seg") & 1)
        keep[0] = part(0, keep)
        keep[1] = part(along ^ 3, keep)
        send[0] = part(along, send)
        send[1] = part(3, send)
    else:
        for j in range(count):
            outs[j][...] = part(j, outs[j])


def out_kernel(heads, soft, values, wo, keep, send):
    blocks, keys, lanes = soft.shape
    queries = lanes // heads
    width = values.shape[1]
    head = lax.broadcasted_iota(jnp.int32, (queries, width), 1) // (width // heads)
    for i in range(blocks):
        b = member_of() ^ i
        stacked = lax.dot_general(
            soft[b],
            values[pl.ds(aligned(b, queries), keys), :],
            TN,
            preferred_element_type=f32,
        )
        attended = stacked[:queries]
        for h in range(1, heads):
            attended = jnp.where(head == h, stacked[h * queries : (h + 1) * queries], attended)
        projected = jnp.dot(attended.astype(bf16), wo[...], preferred_element_type=f32)
        into = send if i & 1 else keep
        into[i // 2] = projected.astype(into.dtype)


def gathered(piece):
    size = lax.axis_size("fsdp")
    pieces = {0: piece}
    bit = 1
    while bit < size:
        for have in sorted(pieces):
            pieces[have ^ bit] = swapped(pieces[have], "fsdp", bit)
        bit *= 2
    return [pieces[j] for j in range(size)]


def pairs(seg_size):
    straight, turned, first, last = [], [], [], []
    for s in range(seg_size):
        along = 2 if s & 1 else 1
        for f in range(GROUP):
            straight.append((s * GROUP + f, s * GROUP + (f ^ along)))
            turned.append((s * GROUP + f, s * GROUP + (f ^ along ^ 3)))
        k = s % GROUP
        first.append((s * GROUP + k, s * GROUP + (k ^ 1)))
        first.append(((s ^ 1) * GROUP + k, s * GROUP + (k ^ 2)))
        first.append(((s ^ 3) * GROUP + k, (s ^ 3) * GROUP + (k ^ 3)))
        last.append(((s ^ 3) * GROUP + (k ^ 3), s * GROUP + (k ^ 3)))
    return straight, turned, first, last


def on_device(
    frames, memory_in, lengths, ln_gain, w_query, w_key, w_value, w_out, grad_frames, grad_memory
):
    utterances, segs, frame_count, width = frames.shape
    seg_size = lax.axis_size("seg")
    fsdp_size = lax.axis_size("fsdp")
    group = GROUP
    assert utterances == 1 and segs == MEMORY and frame_count == LEFT and seg_size % group == 0
    heads = HEADS // group
    block = width // group
    rows = w_query.shape[0]
    frame_rows = segs * frame_count
    queries = frame_rows + 2 * segs
    halo_rows = LEFT + 2 * MEMORY
    keys = halo_rows + queries
    all_rows = halo_rows + group * queries
    seg = lax.axis_index("seg")
    member = seg % group

    crossed = fsdp_size == group
    own_blocks, tokens = pl.pallas_call(
        functools.partial(pack_kernel, frame_count),
        in_specs=[hbm] * 8,
        out_specs=[vmem] * 2,
        out_shape=[
            jax.ShapeDtypeStruct((1 + crossed, rows, 3 * block), bf16),
            jax.ShapeDtypeStruct((2 * queries, width), bf16),
        ],
        scratch_shapes=[
            pltpu.VMEM((frame_rows, width), bf16),
            pltpu.VMEM((2, segs, width), bf16),
            pltpu.VMEM((1, width), f32),
            pltpu.SemaphoreType.DMA((11,)),
        ],
        compiler_params=params(60),
        name="pack",
    )(
        w_query, w_key, w_value, frames.reshape(frame_rows, width),
        grad_frames.reshape(frame_rows, width), memory_in.reshape(segs, width),
        grad_memory.reshape(segs, width), ln_gain.reshape(1, width),
    )
    w_out, own_blocks = lax.optimization_barrier((w_out, own_blocks))

    far = swapped(tokens, "seg", 2)
    near = swapped(tokens, "seg", 1)
    cut = slice(queries - halo_rows, queries)
    tail = jnp.where(member == group - 1, tokens[cut], near[cut])
    ahead = []
    for s in range(group, seg_size, group):
        ahead += [(s - 1, s), (s - 2, s + 2)]
    halo_even = lax.ppermute(tail, "seg", ahead)
    if crossed:
        both = ("seg", "fsdp")
        straight, turned, first, last = pairs(seg_size)
        came = lax.ppermute(own_blocks, both, straight)
        wo_came = lax.ppermute(w_out, both, first)
        came, far, near, halo_even, wo_came = lax.optimization_barrier(
            (came, far, near, halo_even, wo_came)
        )
        mine, other = pl.pallas_call(
            split_kernel,
            in_specs=[vmem],
            out_specs=[vmem] * 2,
            out_shape=[jax.ShapeDtypeStruct(came.shape[1:], bf16)] * 2,
            compiler_params=params(),
            name="split",
        )(came)
        wqkv_parts = [
            own_blocks, mine, swapped(other, "seg", 1), lax.ppermute(mine, both, turned)
        ]
        wo_from, wo_last = [w_out, wo_came], [lax.ppermute(wo_came, both, last)]
    else:
        wqkv_parts = gathered(own_blocks)
        wo_from = [
            lax.dynamic_slice_in_dim(
                lax.all_gather(w_out, "fsdp", axis=0, tiled=True), member * block, block, 0
            )
        ]
        wo_last = []
    halo_odd = lax.ppermute(halo_even, "seg", [(s, s + 1) for s in range(0, seg_size, 2)])
    parts = [tokens, near, far, swapped(far, "seg", 1)]

    x_all, x_turned, u_all, wo_near = pl.pallas_call(
        functools.partial(merge_kernel, group),
        in_specs=[vmem] * (group + 2 + len(wo_from)),
        out_specs=[vmem] * 4,
        out_shape=[
            jax.ShapeDtypeStruct((all_rows, width), bf16),
            jax.ShapeDtypeStruct((width, all_rows), bf16),
            jax.ShapeDtypeStruct((group * queries, width), bf16),
            jax.ShapeDtypeStruct((block, width), bf16),
        ],
        compiler_params=params(),
        name="merge",
    )(*parts, halo_even, halo_odd, *wo_from)

    soft, values = pl.pallas_call(
        functools.partial(weights_kernel, heads, frame_count, segs, crossed),
        in_specs=[vmem] * (1 + fsdp_size),
        out_specs=[vmem] * 2,
        out_shape=[
            jax.ShapeDtypeStruct((group, keys, heads * queries), bf16),
            jax.ShapeDtypeStruct((all_rows, block), bf16),
        ],
        scratch_shapes=[pltpu.VMEM((width, 3 * block), bf16)],
        compiler_params=params(),
        name="soft_weights",
    )(x_all, *wqkv_parts)

    if crossed:
        grad_shapes = [jax.ShapeDtypeStruct((2, rows, block), dtype) for dtype in (f32, bf16)]
    else:
        grad_shapes = [jax.ShapeDtypeStruct((rows, block), bf16)] * fsdp_size
    *grad_chunks, wo_mine = pl.pallas_call(
        functools.partial(grad_kernel, fsdp_size, heads, frame_count, segs, crossed),
        in_specs=[smem] + [vmem] * (4 + len(wo_last)),
        out_specs=[vmem] * (len(grad_shapes) + 1),
        out_shape=grad_shapes + [jax.ShapeDtypeStruct((block, width), bf16)],
        scratch_shapes=[
            pltpu.VMEM((all_rows, block), f32),
            pltpu.VMEM((width, block), f32),
        ],
        compiler_params=params(),
        name="value_grad",
    )(lengths, x_turned, u_all, soft, wo_near, *wo_last)

    keep, send = pl.pallas_call(
        functools.partial(out_kernel, heads),
        in_specs=[vmem] * 3,
        out_specs=[vmem] * 2,
        out_shape=[
            jax.ShapeDtypeStruct((group // 2, queries, width), f32),
            jax.ShapeDtypeStruct((group // 2, queries, width), bf16),
        ],
        compiler_params=params(),
        name="attend_project",
    )(soft, values, wo_mine)
    near = swapped(send, "seg", 1)
    onward = (keep[1] + near[1].astype(f32)).astype(bf16)
    back = swapped(onward, "seg", 2)
    if crossed:
        kept, sent = grad_chunks
        came, _ = lax.optimization_barrier((lax.ppermute(sent, both, straight), send))
        passing = (kept[1] + came[1].astype(f32)).astype(bf16)
        passing, onward = lax.optimization_barrier((passing, onward))
        last = lax.ppermute(passing, both, turned)
        grad_sum = kept[0] + came[0].astype(f32) + last.astype(f32)
    else:
        grad_sum = grad_chunks[0].astype(f32)
        for j in range(1, fsdp_size):
            grad_sum = grad_sum + swapped(grad_chunks[j], "fsdp", j).astype(f32)
    bit = group
    while bit < seg_size:
        mine = grad_sum.astype(bf16)
        grad_sum = mine.astype(f32) + swapped(mine, "seg", bit).astype(f32)
        bit *= 2
    mine = grad_sum.astype(bf16)
    projected = keep[0] + near[0].astype(f32) + back.astype(f32)

    live = (seg * segs + jnp.arange(segs) < lengths[0]).astype(f32)
    frames_out = (
        frames.astype(f32)
        + live[None, :, None, None]
        * projected[:frame_rows].reshape(1, segs, frame_count, width)
    ).astype(bf16)
    memory_out = (live[None, :, None] * projected[None, frame_rows + segs :]).astype(bf16)

    far = swapped(mine, "seg", 2)
    high = (member & 2) > 0
    pair = jnp.stack([jnp.where(high, far, mine), jnp.where(high, mine, far)])
    near = swapped(pair, "seg", 1)
    odd = (member & 1) > 0
    value_grad = jnp.concatenate(
        [
            part[j]
            for j in range(2)
            for part in (jnp.where(odd, near, pair), jnp.where(odd, pair, near))
        ],
        axis=1,
    ).astype(f32)
    return (frames_out, memory_out, value_grad)


def solution(mesh):
    return jax.shard_map(
        on_device,
        mesh=mesh,
        in_specs=(
            P("fsdp", "seg", None, None),
            P("fsdp", "seg", None),
            P("fsdp"),
            P(),
            P("fsdp", None),
            P("fsdp", None),
            P("fsdp", None),
            P("fsdp", None),
            P("fsdp", "seg", None, None),
            P("fsdp", "seg", None),
        ),
        out_specs=(P("fsdp", "seg", None, None), P("fsdp", "seg", None), P("fsdp", None)),
        check_vma=False,
    )
```

```python
import functools
import math

import jax
import jax.numpy as jnp
from jax import lax
from jax.experimental import pallas as pl
from jax.experimental.pallas import tpu as pltpu
from jax.sharding import PartitionSpec as P

HEADS = 16
LEFT = 16
MEMORY = 8
GROUP = 4
PIECES = 2


epsilon = 1e-05
masked_score = -1e30
bf16 = jnp.bfloat16
f32 = jnp.float32
vmem = pl.BlockSpec(memory_space=pltpu.VMEM)
smem = pl.BlockSpec(memory_space=pltpu.SMEM)
hbm = pl.BlockSpec(memory_space=pltpu.HBM)
NT = (((1,), (1,)), ((), ()))
TN = (((0,), (0,)), ((), ()))


def params(mib=40):
    return pltpu.CompilerParams(vmem_limit_bytes=mib * 1024 * 1024)


def swapped(array, axis, bit):
    size = lax.axis_size(axis)
    return lax.ppermute(array, axis, [(i, i ^ bit) for i in range(size)])


def halving_bits(size):
    return [1 << b for b in range(size.bit_length() - 1)]


def member_of():
    return lax.axis_index("seg") % GROUP


def aligned(start, step):
    return pl.multiple_of(start * step, step)


def normed_rows(rows, gain):
    wide = rows.astype(f32)
    centred = wide - jnp.mean(wide, axis=-1, keepdims=True)
    var = jnp.mean(centred * centred, axis=-1, keepdims=True)
    return (centred * lax.rsqrt(var + epsilon) * gain).astype(bf16)


def pack_kernel(frame_count, wq, wk, wv, frames, gf, mem, gm, gain, *refs):
    blocks, tokens, raw, few, one, sems = refs
    width = blocks.shape[2] // 3
    rows, model_width = gf.shape
    segs = mem.shape[0]
    half = tokens.shape[0] // 2
    copies = [
        pltpu.make_async_copy(frames, raw, sems.at[0]),
        pltpu.make_async_copy(gain, one, sems.at[1]),
        pltpu.make_async_copy(mem, few.at[0], sems.at[2]),
        pltpu.make_async_copy(gm, few.at[1], sems.at[3]),
        pltpu.make_async_copy(gf, tokens.at[pl.ds(half, rows)], sems.at[4]),
    ]
    for i in range(blocks.shape[0]):
        at = aligned(member_of() ^ i, width)
        for j, w in enumerate((wq, wk, wv)):
            into = blocks.at[i, :, pl.ds(j * width, width)]
            sem = sems.at[5 + 3 * i + j]
            copies.append(pltpu.make_async_copy(w.at[:, pl.ds(at, width)], into, sem))
    for copy in copies:
        copy.start()
    for copy in copies[:4]:
        copy.wait()
    normed = normed_rows(raw[...], one[...])
    tokens[:rows, :] = normed
    summary = jnp.sum(normed.astype(f32).reshape(segs, frame_count, model_width), axis=1)
    tokens[rows:half, :] = jnp.concatenate(
        [few[0], (summary / frame_count).astype(bf16)], axis=0
    )
    tokens[half + rows :, :] = jnp.concatenate([jnp.zeros_like(few[1]), few[1]], axis=0)
    for copy in copies[4:]:
        copy.wait()


def split_kernel(both, far, halo, mine, other, far_tokens, far_grads):
    mine[...] = both[0]
    other[...] = both[1]
    half = far_grads.shape[0]
    far_tokens[:half, :] = far[:half, :]
    far_tokens[half:, :] = halo[...]
    far_grads[...] = far[half:, :]


def merge_kernel(tokens, near, far, far_grads, last, last_grads, x_all, x_turned, u_all):
    half = far_grads.shape[0]
    parts = [
        (tokens[:half, :], tokens[half:, :]),
        (near[:half, :], near[half:, :]),
        (far[:half, :], far_grads[...]),
        (last[:half, :], last_grads[...]),
    ]
    halo = far.shape[0] - half
    odd = (member_of() & 1) > 0
    x_all[:halo, :] = jnp.where(odd, last[half:, :], far[half:, :])
    for i, (x_part, u_part) in enumerate(parts):
        at = aligned(member_of() ^ i, half)
        x_all[pl.ds(pl.multiple_of(halo + at, 16), half), :] = x_part
        u_all[pl.ds(at, half), :] = u_part
    x_turned[...] = x_all[...].T


def pick_kernel(own, came, wo):
    wo[...] = jnp.where(lax.axis_index("fsdp") == member_of(), own[...], came[...])


def assemble(pieces, whole, crossed):
    own = lax.axis_index("fsdp")
    rows = pieces[0].shape[-2]
    flip = lax.axis_index("seg") & 1 if crossed else 0
    for j, piece in enumerate(pieces):
        apart = j ^ (3 * flip) if j in (1, 2) else j
        into = whole.at[pl.ds(aligned(own ^ apart, rows), rows), :]
        into[...] = piece[0] if len(piece.shape) == 3 else piece[...]


def head_stack(array, heads):
    width = array.shape[1]
    head = lax.broadcasted_iota(jnp.int32, array.shape, 1) // (width // heads)
    zero = jnp.zeros_like(array)
    return jnp.concatenate([jnp.where(head == h, array, zero) for h in range(heads)], axis=0)


def weights_kernel(heads, frame_count, segs, crossed, x_all, *refs):
    soft, values, wqkv = refs[-3:]
    assemble(refs[:-3], wqkv, crossed)
    blocks, keys, lanes = soft.shape
    queries = lanes // heads
    halo = keys - queries
    frames = segs * frame_count
    block = values.shape[1]
    projected = jnp.dot(x_all[...], wqkv[...], preferred_element_type=f32).astype(bf16)
    q_all, k_all = projected[:, :block], projected[:, block : 2 * block]
    values[...] = projected[:, 2 * block :]
    key = lax.broadcasted_iota(jnp.int32, (keys, lanes), 0)
    row = lax.broadcasted_iota(jnp.int32, (keys, lanes), 1)
    for h in range(1, heads):
        row = jnp.where(row >= queries, row - queries, row)
    at = jnp.where(row < frames, row // frame_count, jnp.maximum(row - frames - segs, 0))
    own = key - halo
    own_seg = own // frame_count
    own_mem = own - frames
    valid_own = ((own >= 0) & (own < frames) & ((own_seg == at) | (own_seg == at - 1))) | (
        (own_mem >= 0) & (own_mem < segs) & (own_mem < at) & (own_mem >= at - MEMORY)
    )
    halo_mem = key - LEFT
    valid_halo = ((key < LEFT) & (at == 0)) | (
        (halo_mem >= 0) & (halo_mem < MEMORY) & (halo_mem >= at)
    )
    inside = lax.axis_index("seg") >= blocks
    scale = 1.0 / math.sqrt(block // heads)
    for b in range(blocks):
        valid = valid_own | (valid_halo & inside if b == 0 else valid_halo)
        start = b * queries
        q_b = head_stack(q_all[halo + start : halo + start + queries], heads)
        scores = (
            lax.dot_general(k_all[start : start + keys], q_b, NT, preferred_element_type=f32)
            * scale
        )
        scores = jnp.where(valid, scores, masked_score)
        exponent = jnp.exp(scores - jnp.max(scores, axis=0, keepdims=True))
        soft[b] = (exponent / jnp.sum(exponent, axis=0, keepdims=True)).astype(bf16)


def grad_kernel(count, heads, frame_count, segs, crossed, lengths, x_turned, u_all, soft, *refs):
    outputs = 2 if crossed else count
    wo, outs = refs[0], refs[1 : 1 + outputs]
    values, whole = refs[-2:]
    blocks, keys, lanes = soft.shape
    queries = lanes // heads
    frames = segs * frame_count
    back = lax.dot_general(u_all[...], wo[...], NT, preferred_element_type=f32)
    row = lax.broadcasted_iota(jnp.int32, (queries, wo.shape[0]), 0)
    seg_of = jnp.where(row < frames, row // frame_count, row - frames - segs)
    first = lax.axis_index("seg") - member_of()
    values[: keys - queries, :] = jnp.zeros((keys - queries, values.shape[1]), f32)
    for b in range(blocks):
        start = b * queries
        live = ((first + b) * segs + seg_of < lengths[0]).astype(f32)
        grad_attended = head_stack((live * back[start : start + queries]).astype(bf16), heads)
        term = jnp.dot(soft[b], grad_attended, preferred_element_type=f32)
        split = keys - queries
        values[start : start + split, :] += term[:split]
        values[start + split : start + keys, :] = term[split:]
    whole[...] = jnp.dot(
        x_turned[...], values[...].astype(bf16), preferred_element_type=f32
    )
    own = lax.axis_index("fsdp")
    rows = whole.shape[0] // count

    def part(apart, into):
        return whole[pl.ds(aligned(own ^ apart, rows), rows), :].astype(into.dtype)

    if crossed:
        keep, send = outs
        along = 1 + (lax.axis_index("seg") & 1)
        keep[0] = part(0, keep)
        keep[1] = part(along ^ 3, keep)
        send[0] = part(along, send)
        send[1] = part(3, send)
    else:
        for j in range(count):
            outs[j][...] = part(j, outs[j])


def out_kernel(heads, first, soft, values, *refs):
    wo_from, (keep, *send) = refs[: -1 - PIECES], refs[-1 - PIECES :]
    if len(wo_from) == 3:
        wo_from, wo = wo_from[:2], wo_from[2]
        opposite = (lax.axis_index("fsdp") ^ member_of()) == 3
        wo[...] = jnp.where(opposite, wo_from[1][...], wo_from[0][...])
    else:
        wo = wo_from[0]
    blocks, keys, lanes = soft.shape
    queries = lanes // heads
    width = values.shape[1]
    head = lax.broadcasted_iota(jnp.int32, (queries, width), 1) // (width // heads)
    for i in (first, first + 1):
        b = member_of() ^ i
        stacked = lax.dot_general(
            soft[b],
            values[pl.ds(aligned(b, queries), keys), :],
            TN,
            preferred_element_type=f32,
        )
        attended = stacked[:queries]
        for h in range(1, heads):
            attended = jnp.where(head == h, stacked[h * queries : (h + 1) * queries], attended)
        projected = jnp.dot(attended.astype(bf16), wo[...], preferred_element_type=f32)
        if i == first:
            keep[...] = projected
        else:
            start = 0
            for into in send:
                into[...] = projected[start : start + into.shape[0]].astype(into.dtype)
                start += into.shape[0]


def onward_kernel(keep, *refs):
    pieces, onward = refs[:-1], refs[-1]
    start = 0
    for piece in pieces:
        part = slice(start, start + piece.shape[0])
        onward[part, :] = (keep[part, :] + piece[...].astype(f32)).astype(bf16)
        start += piece.shape[0]


def finish_kernel(frame_count, lengths, frames, keep, back, *refs):
    pieces, frames_out, memory_out = refs[:-2], refs[-2], refs[-1]
    segs = memory_out.shape[0]
    count = frames.shape[0]
    near = jnp.concatenate([piece[...].astype(f32) for piece in pieces], axis=0)
    projected = keep[...] + near + back[...].astype(f32)
    first = lax.axis_index("seg") * segs

    def live(array, step):
        at = lax.broadcasted_iota(jnp.int32, array.shape, 0) // step
        return jnp.where(first + at < lengths[0], array, 0.0)

    frames_out[...] = (
        frames[...].astype(f32) + live(projected[:count], frame_count)
    ).astype(bf16)
    memory_out[...] = live(projected[count + segs :], 1).astype(bf16)


def columns_kernel(mine, far, near_mine, near_far, out):
    width = mine.shape[1]
    for i, part in enumerate((mine, near_mine, far, near_far)):
        out[:, pl.ds(aligned(member_of() ^ i, width), width)] = part[...].astype(f32)


def gathered(piece):
    size = lax.axis_size("fsdp")
    pieces = {0: piece}
    bit = 1
    while bit < size:
        for have in sorted(pieces):
            pieces[have ^ bit] = swapped(pieces[have], "fsdp", bit)
        bit *= 2
    return [pieces[j] for j in range(size)]


def pairs(seg_size):
    straight, turned, first, last = [], [], [], []
    for s in range(seg_size):
        along = 2 if s & 1 else 1
        for f in range(GROUP):
            straight.append((s * GROUP + f, s * GROUP + (f ^ along)))
            turned.append((s * GROUP + f, s * GROUP + (f ^ along ^ 3)))
        k = s % GROUP
        first.append((s * GROUP + k, s * GROUP + (k ^ 1)))
        first.append(((s ^ 1) * GROUP + k, s * GROUP + (k ^ 2)))
        first.append(((s ^ 3) * GROUP + k, (s ^ 3) * GROUP + (k ^ 3)))
        last.append(((s ^ 3) * GROUP + (k ^ 3), s * GROUP + (k ^ 3)))
    return straight, turned, first, last


def on_device(
    frames, memory_in, lengths, ln_gain, w_query, w_key, w_value, w_out, grad_frames, grad_memory
):
    utterances, segs, frame_count, width = frames.shape
    seg_size = lax.axis_size("seg")
    fsdp_size = lax.axis_size("fsdp")
    group = GROUP
    assert utterances == 1 and segs == MEMORY and frame_count == LEFT and seg_size % group == 0
    heads = HEADS // group
    block = width // group
    rows = w_query.shape[0]
    frame_rows = segs * frame_count
    queries = frame_rows + 2 * segs
    halo_rows = LEFT + 2 * MEMORY
    keys = halo_rows + queries
    all_rows = halo_rows + group * queries
    seg = lax.axis_index("seg")
    member = seg % group

    crossed = fsdp_size == group
    own_blocks, tokens = pl.pallas_call(
        functools.partial(pack_kernel, frame_count),
        in_specs=[hbm] * 8,
        out_specs=[vmem] * 2,
        out_shape=[
            jax.ShapeDtypeStruct((1 + crossed, rows, 3 * block), bf16),
            jax.ShapeDtypeStruct((2 * queries, width), bf16),
        ],
        scratch_shapes=[
            pltpu.VMEM((frame_rows, width), bf16),
            pltpu.VMEM((2, segs, width), bf16),
            pltpu.VMEM((1, width), f32),
            pltpu.SemaphoreType.DMA((11,)),
        ],
        compiler_params=params(60),
        name="pack",
    )(
        w_query, w_key, w_value, frames.reshape(frame_rows, width),
        grad_frames.reshape(frame_rows, width), memory_in.reshape(segs, width),
        grad_memory.reshape(segs, width), ln_gain.reshape(1, width),
    )
    w_out, own_blocks = lax.optimization_barrier((w_out, own_blocks))

    far = swapped(tokens, "seg", 2)
    near = swapped(tokens, "seg", 1)
    cut = slice(queries - halo_rows, queries)
    tail = jnp.where(member == group - 1, tokens[cut], near[cut])
    ahead = []
    for s in range(group, seg_size, group):
        ahead += [(s - 1, s), (s - 2, s + 2)]
    halo = lax.ppermute(tail, "seg", ahead)
    if crossed:
        both = ("seg", "fsdp")
        straight, turned, first, last = pairs(seg_size)
        came = lax.ppermute(own_blocks, both, straight)
        wo_came = lax.ppermute(w_out, both, first)
        came, far, near, halo, wo_came = lax.optimization_barrier(
            (came, far, near, halo, wo_came)
        )
        wo_last = lax.ppermute(wo_came, both, last)
    else:
        came = own_blocks
        wo_near = lax.dynamic_slice_in_dim(
            lax.all_gather(w_out, "fsdp", axis=0, tiled=True), member * block, block, 0
        )
    mine, other, far, far_grads = pl.pallas_call(
        split_kernel,
        in_specs=[vmem] * 3,
        out_specs=[vmem] * 4,
        out_shape=[jax.ShapeDtypeStruct(came.shape[1:], bf16)] * 2
        + [
            jax.ShapeDtypeStruct((queries + halo_rows, width), bf16),
            jax.ShapeDtypeStruct((queries, width), bf16),
        ],
        compiler_params=params(),
        name="split",
    )(came, far, halo)
    if crossed:
        wqkv_parts = [
            own_blocks, mine, swapped(other, "seg", 1), lax.ppermute(mine, both, turned)
        ]
        wo_near = pl.pallas_call(
            pick_kernel,
            in_specs=[vmem] * 2,
            out_specs=vmem,
            out_shape=jax.ShapeDtypeStruct((block, width), bf16),
            compiler_params=params(),
            name="pick",
        )(w_out, wo_came)
    else:
        wqkv_parts = gathered(own_blocks)
    parts = [tokens, near, far, far_grads, swapped(far, "seg", 1), swapped(far_grads, "seg", 1)]

    x_all, x_turned, u_all = pl.pallas_call(
        merge_kernel,
        in_specs=[vmem] * len(parts),
        out_specs=[vmem] * 3,
        out_shape=[
            jax.ShapeDtypeStruct((all_rows, width), bf16),
            jax.ShapeDtypeStruct((width, all_rows), bf16),
            jax.ShapeDtypeStruct((group * queries, width), bf16),
        ],
        compiler_params=params(),
        name="merge",
    )(*parts)
    x_all, wo_near = lax.optimization_barrier((x_all, wo_near))

    soft, values = pl.pallas_call(
        functools.partial(weights_kernel, heads, frame_count, segs, crossed),
        in_specs=[vmem] * (1 + fsdp_size),
        out_specs=[vmem] * 2,
        out_shape=[
            jax.ShapeDtypeStruct((group, keys, heads * queries), bf16),
            jax.ShapeDtypeStruct((all_rows, block), bf16),
        ],
        scratch_shapes=[pltpu.VMEM((width, 3 * block), bf16)],
        compiler_params=params(),
        name="soft_weights",
    )(x_all, *wqkv_parts)

    def attend(start, wo_from, name):
        wo_shape = [jax.ShapeDtypeStruct((block, width), bf16)] * (len(wo_from) - 1)
        cut = queries // PIECES // 16 * 16
        sizes = [cut] * (PIECES - 1) + [queries - cut * (PIECES - 1)]
        outs = pl.pallas_call(
            functools.partial(out_kernel, heads, start),
            in_specs=[vmem] * (2 + len(wo_from)),
            out_specs=[vmem] * (len(wo_shape) + 1 + PIECES),
            out_shape=wo_shape
            + [jax.ShapeDtypeStruct((queries, width), f32)]
            + [jax.ShapeDtypeStruct((size, width), bf16) for size in sizes],
            compiler_params=params(),
            name=name,
        )(soft, values, *wo_from)
        return outs[: len(wo_shape)], outs[len(wo_shape)], outs[len(wo_shape) + 1 :]

    picked, keep_far, send_far = attend(2, [wo_near] + ([wo_last] if crossed else []), "attend_far")
    wo_mine = picked[0] if crossed else wo_near
    if crossed:
        grad_shapes = [jax.ShapeDtypeStruct((2, rows, block), dtype) for dtype in (f32, bf16)]
    else:
        grad_shapes = [jax.ShapeDtypeStruct((rows, block), bf16)] * fsdp_size
    grad_chunks = pl.pallas_call(
        functools.partial(grad_kernel, fsdp_size, heads, frame_count, segs, crossed),
        in_specs=[smem] + [vmem] * 4,
        out_specs=[vmem] * len(grad_shapes),
        out_shape=grad_shapes,
        scratch_shapes=[
            pltpu.VMEM((all_rows, block), f32),
            pltpu.VMEM((width, block), f32),
        ],
        compiler_params=params(),
        name="value_grad",
    )(lengths, x_turned, u_all, soft, wo_mine)

    _, keep, send = attend(0, [wo_mine], "attend_near")
    near = [swapped(piece, "seg", 1) for piece in send]
    near_far = [swapped(piece, "seg", 1) for piece in send_far]
    onward = pl.pallas_call(
        onward_kernel,
        in_specs=[vmem] * (1 + PIECES),
        out_specs=vmem,
        out_shape=jax.ShapeDtypeStruct((queries, width), bf16),
        compiler_params=params(),
        name="onward",
    )(keep_far, *near_far)
    if crossed:
        kept, sent = grad_chunks
        came = lax.ppermute(sent, both, straight)
        passing = (kept[1] + came[1].astype(f32)).astype(bf16)
        passing, onward = lax.optimization_barrier((passing, onward))
        last = lax.ppermute(passing, both, turned)
        grad_sum = kept[0] + came[0].astype(f32) + last.astype(f32)
    else:
        grad_sum = grad_chunks[0].astype(f32)
        for j in range(1, fsdp_size):
            grad_sum = grad_sum + swapped(grad_chunks[j], "fsdp", j).astype(f32)
    back = swapped(onward, "seg", 2)
    back = swapped(onward, "seg", 2)
    bit = group
    while bit < seg_size:
        mine = grad_sum.astype(bf16)
        other, back = lax.optimization_barrier((swapped(mine, "seg", bit), back))
        grad_sum = mine.astype(f32) + other.astype(f32)
        bit *= 2
    mine, near = lax.optimization_barrier((grad_sum.astype(bf16), near))
    frames_out, memory_out = pl.pallas_call(
        functools.partial(finish_kernel, frame_count),
        in_specs=[smem] + [vmem] * (3 + PIECES),
        out_specs=[vmem] * 2,
        out_shape=[
            jax.ShapeDtypeStruct((frame_rows, width), bf16),
            jax.ShapeDtypeStruct((segs, width), bf16),
        ],
        compiler_params=params(),
        name="finish",
    )(lengths, frames.reshape(frame_rows, width), keep, back, *near)
    far = swapped(mine, "seg", 2)
    value_grad = pl.pallas_call(
        columns_kernel,
        in_specs=[vmem] * 4,
        out_specs=vmem,
        out_shape=jax.ShapeDtypeStruct((rows, width), f32),
        compiler_params=params(),
        name="columns",
    )(mine, far, swapped(mine, "seg", 1), swapped(far, "seg", 1))
    frames_out = frames_out.reshape(frames.shape)
    memory_out = memory_out.reshape(memory_in.shape)
    return (frames_out, memory_out, value_grad)


def solution(mesh):
    return jax.shard_map(
        on_device,
        mesh=mesh,
        in_specs=(
            P("fsdp", "seg", None, None),
            P("fsdp", "seg", None),
            P("fsdp"),
            P(),
            P("fsdp", None),
            P("fsdp", None),
            P("fsdp", None),
            P("fsdp", None),
            P("fsdp", "seg", None, None),
            P("fsdp", "seg", None),
        ),
        out_specs=(P("fsdp", "seg", None, None), P("fsdp", "seg", None), P("fsdp", None)),
        check_vma=False,
    )
```

```python
import functools
import math

import jax
import jax.numpy as jnp
from jax import lax
from jax.experimental import pallas as pl
from jax.experimental.pallas import tpu as pltpu
from jax.sharding import PartitionSpec as P

HEADS = 16
LEFT = 16
MEMORY = 8
GROUP = 4
PIECES = 2


epsilon = 1e-05
masked_score = -1e30
bf16 = jnp.bfloat16
f32 = jnp.float32
vmem = pl.BlockSpec(memory_space=pltpu.VMEM)
smem = pl.BlockSpec(memory_space=pltpu.SMEM)
hbm = pl.BlockSpec(memory_space=pltpu.HBM)
NT = (((1,), (1,)), ((), ()))
TN = (((0,), (0,)), ((), ()))


def params(mib=40):
    return pltpu.CompilerParams(vmem_limit_bytes=mib * 1024 * 1024)


def swapped(array, axis, bit):
    size = lax.axis_size(axis)
    return lax.ppermute(array, axis, [(i, i ^ bit) for i in range(size)])


def halving_bits(size):
    return [1 << b for b in range(size.bit_length() - 1)]


def member_of():
    return lax.axis_index("seg") % GROUP


def aligned(start, step):
    return pl.multiple_of(start * step, step)


def normed_rows(rows, gain):
    wide = rows.astype(f32)
    centred = wide - jnp.mean(wide, axis=-1, keepdims=True)
    var = jnp.mean(centred * centred, axis=-1, keepdims=True)
    return (centred * lax.rsqrt(var + epsilon) * gain).astype(bf16)


def pack_kernel(frame_count, wq, wk, wv, frames, gf, mem, gm, gain, *refs):
    blocks, tokens, raw, few, one, sems = refs
    width = blocks.shape[2] // 3
    rows, model_width = gf.shape
    segs = mem.shape[0]
    half = tokens.shape[0] // 2
    copies = [
        pltpu.make_async_copy(frames, raw, sems.at[0]),
        pltpu.make_async_copy(gain, one, sems.at[1]),
        pltpu.make_async_copy(mem, few.at[0], sems.at[2]),
        pltpu.make_async_copy(gm, few.at[1], sems.at[3]),
        pltpu.make_async_copy(gf, tokens.at[pl.ds(half, rows)], sems.at[4]),
    ]
    for i in range(blocks.shape[0]):
        at = aligned(member_of() ^ i, width)
        for j, w in enumerate((wq, wk, wv)):
            into = blocks.at[i, :, pl.ds(j * width, width)]
            sem = sems.at[5 + 3 * i + j]
            copies.append(pltpu.make_async_copy(w.at[:, pl.ds(at, width)], into, sem))
    for copy in copies:
        copy.start()
    for copy in copies[:4]:
        copy.wait()
    normed = normed_rows(raw[...], one[...])
    tokens[:rows, :] = normed
    summary = jnp.sum(normed.astype(f32).reshape(segs, frame_count, model_width), axis=1)
    tokens[rows:half, :] = jnp.concatenate(
        [few[0], (summary / frame_count).astype(bf16)], axis=0
    )
    tokens[half + rows :, :] = jnp.concatenate([jnp.zeros_like(few[1]), few[1]], axis=0)
    for copy in copies[4:]:
        copy.wait()


def split_kernel(both, far, halo, mine, other, far_tokens, far_grads):
    mine[...] = both[0]
    other[...] = both[1]
    half = far_grads.shape[0]
    far_tokens[:half, :] = far[:half, :]
    far_tokens[half:, :] = halo[...]
    far_grads[...] = far[half:, :]


def merge_kernel(tokens, near, far, far_grads, last, last_grads, x_all, x_turned, u_all):
    half = far_grads.shape[0]
    parts = [
        (tokens[:half, :], tokens[half:, :]),
        (near[:half, :], near[half:, :]),
        (far[:half, :], far_grads[...]),
        (last[:half, :], last_grads[...]),
    ]
    halo = far.shape[0] - half
    odd = (member_of() & 1) > 0
    x_all[:halo, :] = jnp.where(odd, last[half:, :], far[half:, :])
    for i, (x_part, u_part) in enumerate(parts):
        at = aligned(member_of() ^ i, half)
        x_all[pl.ds(pl.multiple_of(halo + at, 16), half), :] = x_part
        u_all[pl.ds(at, half), :] = u_part
    x_turned[...] = x_all[...].T


def pick_kernel(own, came, wo):
    wo[...] = jnp.where(lax.axis_index("fsdp") == member_of(), own[...], came[...])


def assemble(pieces, whole):
    own = lax.axis_index("fsdp")
    rows = pieces[0].shape[-2]
    for j, piece in enumerate(pieces):
        into = whole.at[pl.ds(aligned(own ^ j, rows), rows), :]
        into[...] = piece[0] if len(piece.shape) == 3 else piece[...]


def head_stack(array, heads):
    width = array.shape[1]
    head = lax.broadcasted_iota(jnp.int32, array.shape, 1) // (width // heads)
    zero = jnp.zeros_like(array)
    return jnp.concatenate([jnp.where(head == h, array, zero) for h in range(heads)], axis=0)


def early_kernel(x_all, mine, beside, swapped_in, total):
    own = lax.axis_index("fsdp")
    along = 1 + (lax.axis_index("seg") & 1)
    rows = beside.shape[0]
    columns = lambda j: x_all[:, pl.ds(aligned(own ^ j, rows), rows)]
    total[...] = (
        jnp.dot(columns(0), mine[0], preferred_element_type=f32)
        + jnp.dot(columns(along), beside[...], preferred_element_type=f32)
        + jnp.dot(columns(along ^ 3), swapped_in[...], preferred_element_type=f32)
    )


def weights_kernel(heads, frame_count, segs, crossed, x_all, *refs):
    soft, values = refs[-3:-1] if not crossed else refs[-2:]
    if crossed:
        total, last = refs[:2]
        rows = last.shape[0]
        at = aligned(lax.axis_index("fsdp") ^ 3, rows)
        product = total[...] + jnp.dot(
            x_all[:, pl.ds(at, rows)], last[...], preferred_element_type=f32
        )
    else:
        assemble(refs[:-3], refs[-1])
        product = jnp.dot(x_all[...], refs[-1][...], preferred_element_type=f32)
    projected = product.astype(bf16)
    blocks, keys, lanes = soft.shape
    queries = lanes // heads
    halo = keys - queries
    frames = segs * frame_count
    block = values.shape[1]
    q_all, k_all = projected[:, :block], projected[:, block : 2 * block]
    values[...] = projected[:, 2 * block :]
    key = lax.broadcasted_iota(jnp.int32, (keys, lanes), 0)
    row = lax.broadcasted_iota(jnp.int32, (keys, lanes), 1)
    for h in range(1, heads):
        row = jnp.where(row >= queries, row - queries, row)
    at = jnp.where(row < frames, row // frame_count, jnp.maximum(row - frames - segs, 0))
    own = key - halo
    own_seg = own // frame_count
    own_mem = own - frames
    valid_own = ((own >= 0) & (own < frames) & ((own_seg == at) | (own_seg == at - 1))) | (
        (own_mem >= 0) & (own_mem < segs) & (own_mem < at) & (own_mem >= at - MEMORY)
    )
    halo_mem = key - LEFT
    valid_halo = ((key < LEFT) & (at == 0)) | (
        (halo_mem >= 0) & (halo_mem < MEMORY) & (halo_mem >= at)
    )
    inside = lax.axis_index("seg") >= blocks
    scale = 1.0 / math.sqrt(block // heads)
    for b in range(blocks):
        valid = valid_own | (valid_halo & inside if b == 0 else valid_halo)
        start = b * queries
        q_b = head_stack(q_all[halo + start : halo + start + queries], heads)
        scores = (
            lax.dot_general(k_all[start : start + keys], q_b, NT, preferred_element_type=f32)
            * scale
        )
        scores = jnp.where(valid, scores, masked_score)
        exponent = jnp.exp(scores - jnp.max(scores, axis=0, keepdims=True))
        soft[b] = (exponent / jnp.sum(exponent, axis=0, keepdims=True)).astype(bf16)


def grad_kernel(heads, frame_count, segs, lengths, u_all, soft, *refs):
    wo_from, (wo, values, total) = refs[:-3], refs[-3:]
    blocks, keys, lanes = soft.shape
    queries = lanes // heads
    frames = segs * frame_count
    wo[...] = wo_from[0][...]
    if len(wo_from) > 1:
        opposite = (lax.axis_index("fsdp") ^ member_of()) == 3
        wo[...] = jnp.where(opposite, wo_from[1][...], wo[...])
    back = lax.dot_general(u_all[...], wo[...], NT, preferred_element_type=f32)
    row = lax.broadcasted_iota(jnp.int32, (queries, wo.shape[0]), 0)
    seg_of = jnp.where(row < frames, row // frame_count, row - frames - segs)
    first = lax.axis_index("seg") - member_of()
    split = keys - queries
    total[:split, :] = jnp.zeros((split, total.shape[1]), f32)
    for b in range(blocks):
        start = b * queries
        live = ((first + b) * segs + seg_of < lengths[0]).astype(f32)
        grad_attended = head_stack((live * back[start : start + queries]).astype(bf16), heads)
        term = jnp.dot(soft[b], grad_attended, preferred_element_type=f32)
        total[start : start + split, :] += term[:split]
        total[start + split : start + keys, :] = term[split:]
    values[...] = total[...].astype(bf16)


def rows_kernel(which, x_turned, values, *outs):
    own = lax.axis_index("fsdp")
    along = 1 + (lax.axis_index("seg") & 1)
    parts = {"kept": (0, along ^ 3), "sent": (along, 3)}
    if which in parts:
        into = [outs[0].at[i] for i in range(2)]
        apart = parts[which]
    else:
        into, apart = outs, range(len(outs))
    rows = into[0].shape[0]
    for out, j in zip(into, apart, strict=True):
        at = pl.ds(aligned(own ^ j, rows), rows)
        out[...] = jnp.dot(
            x_turned[at, :], values[...], preferred_element_type=f32
        ).astype(out.dtype)


def out_kernel(heads, first, soft, values, *refs):
    wo, keep, *send = refs
    blocks, keys, lanes = soft.shape
    queries = lanes // heads
    width = values.shape[1]
    head = lax.broadcasted_iota(jnp.int32, (queries, width), 1) // (width // heads)
    for i in (first, first + 1):
        b = member_of() ^ i
        stacked = lax.dot_general(
            soft[b],
            values[pl.ds(aligned(b, queries), keys), :],
            TN,
            preferred_element_type=f32,
        )
        attended = stacked[:queries]
        for h in range(1, heads):
            attended = jnp.where(head == h, stacked[h * queries : (h + 1) * queries], attended)
        projected = jnp.dot(attended.astype(bf16), wo[...], preferred_element_type=f32)
        if i == first:
            keep[...] = projected
        else:
            start = 0
            for into in send:
                into[...] = projected[start : start + into.shape[0]].astype(into.dtype)
                start += into.shape[0]


def onward_kernel(keep, *refs):
    pieces, onward = refs[:-1], refs[-1]
    start = 0
    for piece in pieces:
        part = slice(start, start + piece.shape[0])
        onward[part, :] = (keep[part, :] + piece[...].astype(f32)).astype(bf16)
        start += piece.shape[0]


def finish_kernel(frame_count, lengths, frames, keep, back, *refs):
    pieces, frames_out, memory_out = refs[:-2], refs[-2], refs[-1]
    segs = memory_out.shape[0]
    count = frames.shape[0]
    near = jnp.concatenate([piece[...].astype(f32) for piece in pieces], axis=0)
    projected = keep[...] + near + back[...].astype(f32)
    first = lax.axis_index("seg") * segs

    def live(array, step):
        at = lax.broadcasted_iota(jnp.int32, array.shape, 0) // step
        return jnp.where(first + at < lengths[0], array, 0.0)

    frames_out[...] = (
        frames[...].astype(f32) + live(projected[:count], frame_count)
    ).astype(bf16)
    memory_out[...] = live(projected[count + segs :], 1).astype(bf16)


def columns_kernel(mine, far, near_mine, near_far, out):
    width = mine.shape[1]
    for i, part in enumerate((mine, near_mine, far, near_far)):
        out[:, pl.ds(aligned(member_of() ^ i, width), width)] = part[...].astype(f32)


def gathered(piece):
    size = lax.axis_size("fsdp")
    pieces = {0: piece}
    bit = 1
    while bit < size:
        for have in sorted(pieces):
            pieces[have ^ bit] = swapped(pieces[have], "fsdp", bit)
        bit *= 2
    return [pieces[j] for j in range(size)]


def pairs(seg_size):
    straight, turned, first, last = [], [], [], []
    for s in range(seg_size):
        along = 2 if s & 1 else 1
        for f in range(GROUP):
            straight.append((s * GROUP + f, s * GROUP + (f ^ along)))
            turned.append((s * GROUP + f, s * GROUP + (f ^ along ^ 3)))
        k = s % GROUP
        first.append((s * GROUP + k, s * GROUP + (k ^ 1)))
        first.append(((s ^ 1) * GROUP + k, s * GROUP + (k ^ 2)))
        first.append(((s ^ 3) * GROUP + k, (s ^ 3) * GROUP + (k ^ 3)))
        last.append(((s ^ 3) * GROUP + (k ^ 3), s * GROUP + (k ^ 3)))
    return straight, turned, first, last


def on_device(
    frames, memory_in, lengths, ln_gain, w_query, w_key, w_value, w_out, grad_frames, grad_memory
):
    utterances, segs, frame_count, width = frames.shape
    seg_size = lax.axis_size("seg")
    fsdp_size = lax.axis_size("fsdp")
    group = GROUP
    assert utterances == 1 and segs == MEMORY and frame_count == LEFT and seg_size % group == 0
    heads = HEADS // group
    block = width // group
    rows = w_query.shape[0]
    frame_rows = segs * frame_count
    queries = frame_rows + 2 * segs
    halo_rows = LEFT + 2 * MEMORY
    keys = halo_rows + queries
    all_rows = halo_rows + group * queries
    seg = lax.axis_index("seg")
    member = seg % group

    crossed = fsdp_size == group
    own_blocks, tokens = pl.pallas_call(
        functools.partial(pack_kernel, frame_count),
        in_specs=[hbm] * 8,
        out_specs=[vmem] * 2,
        out_shape=[
            jax.ShapeDtypeStruct((1 + crossed, rows, 3 * block), bf16),
            jax.ShapeDtypeStruct((2 * queries, width), bf16),
        ],
        scratch_shapes=[
            pltpu.VMEM((frame_rows, width), bf16),
            pltpu.VMEM((2, segs, width), bf16),
            pltpu.VMEM((1, width), f32),
            pltpu.SemaphoreType.DMA((11,)),
        ],
        compiler_params=params(60),
        name="pack",
    )(
        w_query, w_key, w_value, frames.reshape(frame_rows, width),
        grad_frames.reshape(frame_rows, width), memory_in.reshape(segs, width),
        grad_memory.reshape(segs, width), ln_gain.reshape(1, width),
    )
    w_out, own_blocks = lax.optimization_barrier((w_out, own_blocks))

    far = swapped(tokens, "seg", 2)
    near = swapped(tokens, "seg", 1)
    cut = slice(queries - halo_rows, queries)
    tail = jnp.where(member == group - 1, tokens[cut], near[cut])
    ahead = []
    for s in range(group, seg_size, group):
        ahead += [(s - 1, s), (s - 2, s + 2)]
    halo = lax.ppermute(tail, "seg", ahead)
    if crossed:
        both = ("seg", "fsdp")
        straight, turned, first, last = pairs(seg_size)
        came = lax.ppermute(own_blocks, both, straight)
        wo_came = lax.ppermute(w_out, both, first)
        came, far, near, halo, wo_came = lax.optimization_barrier(
            (came, far, near, halo, wo_came)
        )
        wo_last = lax.ppermute(wo_came, both, last)
    else:
        came = own_blocks
        wo_near = lax.dynamic_slice_in_dim(
            lax.all_gather(w_out, "fsdp", axis=0, tiled=True), member * block, block, 0
        )
    mine, other, far, far_grads = pl.pallas_call(
        split_kernel,
        in_specs=[vmem] * 3,
        out_specs=[vmem] * 4,
        out_shape=[jax.ShapeDtypeStruct(came.shape[1:], bf16)] * 2
        + [
            jax.ShapeDtypeStruct((queries + halo_rows, width), bf16),
            jax.ShapeDtypeStruct((queries, width), bf16),
        ],
        compiler_params=params(),
        name="split",
    )(came, far, halo)
    if crossed:
        other = swapped(other, "seg", 1)
        forwarded = lax.ppermute(mine, both, turned)
        wo_near = pl.pallas_call(
            pick_kernel,
            in_specs=[vmem] * 2,
            out_specs=vmem,
            out_shape=jax.ShapeDtypeStruct((block, width), bf16),
            compiler_params=params(),
            name="pick",
        )(w_out, wo_came)
    else:
        wqkv_parts = gathered(own_blocks)
    parts = [tokens, near, far, far_grads, swapped(far, "seg", 1), swapped(far_grads, "seg", 1)]

    x_all, x_turned, u_all = pl.pallas_call(
        merge_kernel,
        in_specs=[vmem] * len(parts),
        out_specs=[vmem] * 3,
        out_shape=[
            jax.ShapeDtypeStruct((all_rows, width), bf16),
            jax.ShapeDtypeStruct((width, all_rows), bf16),
            jax.ShapeDtypeStruct((group * queries, width), bf16),
        ],
        compiler_params=params(),
        name="merge",
    )(*parts)
    x_all, wo_near = lax.optimization_barrier((x_all, wo_near))

    if crossed:
        early = pl.pallas_call(
            early_kernel,
            in_specs=[vmem] * 4,
            out_specs=vmem,
            out_shape=jax.ShapeDtypeStruct((all_rows, 3 * block), f32),
            compiler_params=params(),
            name="early",
        )(x_all, own_blocks, mine, other)
        wqkv_parts = [early, forwarded]
    soft, values = pl.pallas_call(
        functools.partial(weights_kernel, heads, frame_count, segs, crossed),
        in_specs=[vmem] * (1 + len(wqkv_parts)),
        out_specs=[vmem] * 2,
        out_shape=[
            jax.ShapeDtypeStruct((group, keys, heads * queries), bf16),
            jax.ShapeDtypeStruct((all_rows, block), bf16),
        ],
        scratch_shapes=[] if crossed else [pltpu.VMEM((width, 3 * block), bf16)],
        compiler_params=params(),
        name="soft_weights",
    )(x_all, *wqkv_parts)

    values_grad_shape = jax.ShapeDtypeStruct((all_rows, block), bf16)
    wo_from = [wo_near] + ([wo_last] if crossed else [])
    wo_mine, values_grad = pl.pallas_call(
        functools.partial(grad_kernel, heads, frame_count, segs),
        in_specs=[smem] + [vmem] * (2 + len(wo_from)),
        out_specs=[vmem] * 2,
        out_shape=[jax.ShapeDtypeStruct((block, width), bf16), values_grad_shape],
        scratch_shapes=[pltpu.VMEM((all_rows, block), f32)],
        compiler_params=params(),
        name="values_grad",
    )(lengths, u_all, soft, *wo_from)

    def grad_rows(which, shapes):
        return pl.pallas_call(
            functools.partial(rows_kernel, which),
            in_specs=[vmem] * 2,
            out_specs=[vmem] * len(shapes),
            out_shape=shapes,
            compiler_params=params(),
            name="grad_rows_" + which,
        )(x_turned, values_grad)

    if crossed:
        (sent,) = grad_rows("sent", [jax.ShapeDtypeStruct((2, rows, block), bf16)])
        (kept,) = grad_rows("kept", [jax.ShapeDtypeStruct((2, rows, block), f32)])
    else:
        grad_chunks = grad_rows(
            "all", [jax.ShapeDtypeStruct((rows, block), bf16)] * fsdp_size
        )

    def attend(start, name):
        cut = queries // PIECES // 16 * 16
        sizes = [cut] * (PIECES - 1) + [queries - cut * (PIECES - 1)]
        keep, *send = pl.pallas_call(
            functools.partial(out_kernel, heads, start),
            in_specs=[vmem] * 3,
            out_specs=[vmem] * (1 + PIECES),
            out_shape=[jax.ShapeDtypeStruct((queries, width), f32)]
            + [jax.ShapeDtypeStruct((size, width), bf16) for size in sizes],
            compiler_params=params(),
            name=name,
        )(soft, values, wo_mine)
        return keep, send

    keep_far, send_far = attend(2, "attend_far")
    keep, send = attend(0, "attend_near")
    near = [swapped(piece, "seg", 1) for piece in send]
    near_far = [swapped(piece, "seg", 1) for piece in send_far]
    onward = pl.pallas_call(
        onward_kernel,
        in_specs=[vmem] * (1 + PIECES),
        out_specs=vmem,
        out_shape=jax.ShapeDtypeStruct((queries, width), bf16),
        compiler_params=params(),
        name="onward",
    )(keep_far, *near_far)
    if crossed:
        came = lax.ppermute(sent, both, straight)
        passing = (kept[1] + came[1].astype(f32)).astype(bf16)
        passing, onward = lax.optimization_barrier((passing, onward))
        last = lax.ppermute(passing, both, turned)
        grad_sum = kept[0] + came[0].astype(f32) + last.astype(f32)
    else:
        grad_sum = grad_chunks[0].astype(f32)
        for j in range(1, fsdp_size):
            grad_sum = grad_sum + swapped(grad_chunks[j], "fsdp", j).astype(f32)
    back = swapped(onward, "seg", 2)
    back = swapped(onward, "seg", 2)
    bit = group
    while bit < seg_size:
        mine = grad_sum.astype(bf16)
        other, back = lax.optimization_barrier((swapped(mine, "seg", bit), back))
        grad_sum = mine.astype(f32) + other.astype(f32)
        bit *= 2
    mine, near = lax.optimization_barrier((grad_sum.astype(bf16), near))
    frames_out, memory_out = pl.pallas_call(
        functools.partial(finish_kernel, frame_count),
        in_specs=[smem] + [vmem] * (3 + PIECES),
        out_specs=[vmem] * 2,
        out_shape=[
            jax.ShapeDtypeStruct((frame_rows, width), bf16),
            jax.ShapeDtypeStruct((segs, width), bf16),
        ],
        compiler_params=params(),
        name="finish",
    )(lengths, frames.reshape(frame_rows, width), keep, back, *near)
    far = swapped(mine, "seg", 2)
    value_grad = pl.pallas_call(
        columns_kernel,
        in_specs=[vmem] * 4,
        out_specs=vmem,
        out_shape=jax.ShapeDtypeStruct((rows, width), f32),
        compiler_params=params(),
        name="columns",
    )(mine, far, swapped(mine, "seg", 1), swapped(far, "seg", 1))
    frames_out = frames_out.reshape(frames.shape)
    memory_out = memory_out.reshape(memory_in.shape)
    return (frames_out, memory_out, value_grad)


def solution(mesh):
    return jax.shard_map(
        on_device,
        mesh=mesh,
        in_specs=(
            P("fsdp", "seg", None, None),
            P("fsdp", "seg", None),
            P("fsdp"),
            P(),
            P("fsdp", None),
            P("fsdp", None),
            P("fsdp", None),
            P("fsdp", None),
            P("fsdp", "seg", None, None),
            P("fsdp", "seg", None),
        ),
        out_specs=(P("fsdp", "seg", None, None), P("fsdp", "seg", None), P("fsdp", None)),
        check_vma=False,
    )
```

```python
import functools
import math

import jax
import jax.numpy as jnp
from jax import lax
from jax.experimental import pallas as pl
from jax.experimental.pallas import tpu as pltpu
from jax.sharding import PartitionSpec as P

HEADS = 16
LEFT = 16
MEMORY = 8
GROUP = 4
PIECES = 2


epsilon = 1e-05
masked_score = -1e30
bf16 = jnp.bfloat16
f32 = jnp.float32
vmem = pl.BlockSpec(memory_space=pltpu.VMEM)
smem = pl.BlockSpec(memory_space=pltpu.SMEM)
hbm = pl.BlockSpec(memory_space=pltpu.HBM)
NT = (((1,), (1,)), ((), ()))
TN = (((0,), (0,)), ((), ()))


def params(mib=40):
    return pltpu.CompilerParams(vmem_limit_bytes=mib * 1024 * 1024)


def swapped(array, axis, bit):
    size = lax.axis_size(axis)
    return lax.ppermute(array, axis, [(i, i ^ bit) for i in range(size)])


def halving_bits(size):
    return [1 << b for b in range(size.bit_length() - 1)]


def member_of():
    return lax.axis_index("seg") % GROUP


def aligned(start, step):
    return pl.multiple_of(start * step, step)


def normed_rows(rows, gain):
    wide = rows.astype(f32)
    centred = wide - jnp.mean(wide, axis=-1, keepdims=True)
    var = jnp.mean(centred * centred, axis=-1, keepdims=True)
    return (centred * lax.rsqrt(var + epsilon) * gain).astype(bf16)


def pack_kernel(frame_count, wq, wk, wv, frames, gf, mem, gm, gain, *refs):
    blocks, tokens, tail, raw, few, one, sems = refs
    width = blocks.shape[2] // 3
    rows, model_width = gf.shape
    segs = mem.shape[0]
    half = tokens.shape[0] // 2
    copies = [
        pltpu.make_async_copy(frames, raw, sems.at[0]),
        pltpu.make_async_copy(gain, one, sems.at[1]),
        pltpu.make_async_copy(mem, few.at[0], sems.at[2]),
        pltpu.make_async_copy(gm, few.at[1], sems.at[3]),
        pltpu.make_async_copy(gf, tokens.at[pl.ds(half, rows)], sems.at[4]),
    ]
    for i in range(blocks.shape[0]):
        at = aligned(member_of() ^ i, width)
        for j, w in enumerate((wq, wk, wv)):
            into = blocks.at[i, :, pl.ds(j * width, width)]
            sem = sems.at[5 + 3 * i + j]
            copies.append(pltpu.make_async_copy(w.at[:, pl.ds(at, width)], into, sem))
    for copy in copies:
        copy.start()
    for copy in copies[:4]:
        copy.wait()
    normed = normed_rows(raw[...], one[...])
    tokens[:rows, :] = normed
    summary = jnp.sum(normed.astype(f32).reshape(segs, frame_count, model_width), axis=1)
    tokens[rows:half, :] = jnp.concatenate(
        [few[0], (summary / frame_count).astype(bf16)], axis=0
    )
    tokens[half + rows :, :] = jnp.concatenate([jnp.zeros_like(few[1]), few[1]], axis=0)
    tail[...] = tokens[half - tail.shape[0] : half, :]
    for copy in copies[4:]:
        copy.wait()


def split_kernel(both, far, halo_first, halo_third, mine, mine_values, other, far_tokens, far_grads):
    width = mine.shape[1]
    mine[...] = both[0, :, :width]
    mine_values[...] = both[0, :, width:]
    other[...] = both[1]
    half = far_grads.shape[0]
    far_tokens[:half, :] = far[:half, :]
    far_tokens[half:, :] = jnp.where(member_of() == 0, halo_first[...], halo_third[...])
    far_grads[...] = far[half:, :]


def merge_kernel(tokens, near, far, far_grads, last, last_grads, x_all, x_turned, u_all):
    half = far_grads.shape[0]
    parts = [
        (tokens[:half, :], tokens[half:, :]),
        (near[:half, :], near[half:, :]),
        (far[:half, :], far_grads[...]),
        (last[:half, :], last_grads[...]),
    ]
    halo = far.shape[0] - half
    odd = (member_of() & 1) > 0
    x_all[:halo, :] = jnp.where(odd, last[half:, :], far[half:, :])
    for i, (x_part, u_part) in enumerate(parts):
        at = aligned(member_of() ^ i, half)
        x_all[pl.ds(pl.multiple_of(halo + at, 16), half), :] = x_part
        u_all[pl.ds(at, half), :] = u_part
    x_turned[...] = x_all[...].T


def pick_kernel(own, came, wo):
    wo[...] = jnp.where(lax.axis_index("fsdp") == member_of(), own[...], came[...])


def assemble(pieces, whole):
    own = lax.axis_index("fsdp")
    rows = pieces[0].shape[-2]
    for j, piece in enumerate(pieces):
        into = whole.at[pl.ds(aligned(own ^ j, rows), rows), :]
        into[...] = piece[0] if len(piece.shape) == 3 else piece[...]


def head_stack(array, heads):
    width = array.shape[1]
    head = lax.broadcasted_iota(jnp.int32, array.shape, 1) // (width // heads)
    zero = jnp.zeros_like(array)
    return jnp.concatenate([jnp.where(head == h, array, zero) for h in range(heads)], axis=0)


def early_kernel(x_all, mine, beside, beside_values, swapped_in, total, total_values):
    own = lax.axis_index("fsdp")
    along = 1 + (lax.axis_index("seg") & 1)
    rows, width = beside.shape
    columns = lambda j: x_all[:, pl.ds(aligned(own ^ j, rows), rows)]
    product = jnp.dot(columns(0), mine[0], preferred_element_type=f32) + jnp.dot(
        columns(along ^ 3), swapped_in[...], preferred_element_type=f32
    )
    total[...] = product[:, :width] + jnp.dot(
        columns(along), beside[...], preferred_element_type=f32
    )
    total_values[...] = product[:, width:] + jnp.dot(
        columns(along), beside_values[...], preferred_element_type=f32
    )


def values_kernel(x_all, total, last, values):
    rows = last.shape[0]
    at = aligned(lax.axis_index("fsdp") ^ 3, rows)
    columns = x_all[:, pl.ds(at, rows)]
    values[...] = (
        total[...] + jnp.dot(columns, last[...], preferred_element_type=f32)
    ).astype(bf16)


def weights_kernel(heads, frame_count, segs, crossed, x_all, *refs):
    if crossed:
        total, last, soft = refs
        rows = last.shape[0]
        at = aligned(lax.axis_index("fsdp") ^ 3, rows)
        product = total[...] + jnp.dot(
            x_all[:, pl.ds(at, rows)], last[...], preferred_element_type=f32
        )
    else:
        soft, values, whole = refs[-3:]
        assemble(refs[:-3], whole)
        product = jnp.dot(x_all[...], whole[...], preferred_element_type=f32)
    projected = product.astype(bf16)
    blocks, keys, lanes = soft.shape
    queries = lanes // heads
    halo = keys - queries
    frames = segs * frame_count
    block = projected.shape[1] // (2 if crossed else 3)
    q_all, k_all = projected[:, :block], projected[:, block : 2 * block]
    if not crossed:
        values[...] = projected[:, 2 * block :]
    key = lax.broadcasted_iota(jnp.int32, (keys, lanes), 0)
    row = lax.broadcasted_iota(jnp.int32, (keys, lanes), 1)
    for h in range(1, heads):
        row = jnp.where(row >= queries, row - queries, row)
    at = jnp.where(row < frames, row // frame_count, jnp.maximum(row - frames - segs, 0))
    own = key - halo
    own_seg = own // frame_count
    own_mem = own - frames
    valid_own = ((own >= 0) & (own < frames) & ((own_seg == at) | (own_seg == at - 1))) | (
        (own_mem >= 0) & (own_mem < segs) & (own_mem < at) & (own_mem >= at - MEMORY)
    )
    halo_mem = key - LEFT
    valid_halo = ((key < LEFT) & (at == 0)) | (
        (halo_mem >= 0) & (halo_mem < MEMORY) & (halo_mem >= at)
    )
    inside = lax.axis_index("seg") >= blocks
    scale = 1.0 / math.sqrt(block // heads)
    for b in range(blocks):
        valid = valid_own | (valid_halo & inside if b == 0 else valid_halo)
        start = b * queries
        q_b = head_stack(q_all[halo + start : halo + start + queries], heads)
        scores = (
            lax.dot_general(k_all[start : start + keys], q_b, NT, preferred_element_type=f32)
            * scale
        )
        scores = jnp.where(valid, scores, masked_score)
        exponent = jnp.exp(scores - jnp.max(scores, axis=0, keepdims=True))
        soft[b] = (exponent / jnp.sum(exponent, axis=0, keepdims=True)).astype(bf16)


def grad_kernel(heads, frame_count, segs, lengths, u_all, soft, *refs):
    wo_from, (wo, values, total) = refs[:-3], refs[-3:]
    blocks, keys, lanes = soft.shape
    queries = lanes // heads
    frames = segs * frame_count
    wo[...] = wo_from[0][...]
    if len(wo_from) > 1:
        opposite = (lax.axis_index("fsdp") ^ member_of()) == 3
        wo[...] = jnp.where(opposite, wo_from[1][...], wo[...])
    back = lax.dot_general(u_all[...], wo[...], NT, preferred_element_type=f32)
    row = lax.broadcasted_iota(jnp.int32, (queries, wo.shape[0]), 0)
    seg_of = jnp.where(row < frames, row // frame_count, row - frames - segs)
    first = lax.axis_index("seg") - member_of()
    split = keys - queries
    total[:split, :] = jnp.zeros((split, total.shape[1]), f32)
    for b in range(blocks):
        start = b * queries
        live = ((first + b) * segs + seg_of < lengths[0]).astype(f32)
        grad_attended = head_stack((live * back[start : start + queries]).astype(bf16), heads)
        term = jnp.dot(soft[b], grad_attended, preferred_element_type=f32)
        total[start : start + split, :] += term[:split]
        total[start + split : start + keys, :] = term[split:]
    values[...] = total[...].astype(bf16)


def rows_kernel(which, x_turned, values, *outs):
    own = lax.axis_index("fsdp")
    along = 1 + (lax.axis_index("seg") & 1)
    parts = {"kept": (0, along ^ 3), "sent": (along, 3)}
    if which in parts:
        into = [outs[0].at[i] for i in range(2)]
        apart = parts[which]
    else:
        into, apart = outs, range(len(outs))
    rows = into[0].shape[0]
    for out, j in zip(into, apart, strict=True):
        at = pl.ds(aligned(own ^ j, rows), rows)
        out[...] = jnp.dot(
            x_turned[at, :], values[...], preferred_element_type=f32
        ).astype(out.dtype)


def out_kernel(heads, first, soft, values, *refs):
    wo, keep, *send = refs
    blocks, keys, lanes = soft.shape
    queries = lanes // heads
    width = values.shape[1]
    head = lax.broadcasted_iota(jnp.int32, (queries, width), 1) // (width // heads)
    for i in (first, first + 1):
        b = member_of() ^ i
        stacked = lax.dot_general(
            soft[b],
            values[pl.ds(aligned(b, queries), keys), :],
            TN,
            preferred_element_type=f32,
        )
        attended = stacked[:queries]
        for h in range(1, heads):
            attended = jnp.where(head == h, stacked[h * queries : (h + 1) * queries], attended)
        projected = jnp.dot(attended.astype(bf16), wo[...], preferred_element_type=f32)
        if i == first:
            keep[...] = projected
        else:
            start = 0
            for into in send:
                into[...] = projected[start : start + into.shape[0]].astype(into.dtype)
                start += into.shape[0]


def onward_kernel(keep, *refs):
    pieces, onward = refs[:-1], refs[-1]
    start = 0
    for piece in pieces:
        part = slice(start, start + piece.shape[0])
        onward[part, :] = (keep[part, :] + piece[...].astype(f32)).astype(bf16)
        start += piece.shape[0]


def finish_kernel(frame_count, lengths, frames, keep, back, *refs):
    pieces, frames_out, memory_out = refs[:-2], refs[-2], refs[-1]
    segs = memory_out.shape[0]
    count = frames.shape[0]
    near = jnp.concatenate([piece[...].astype(f32) for piece in pieces], axis=0)
    projected = keep[...] + near + back[...].astype(f32)
    first = lax.axis_index("seg") * segs

    def live(array, step):
        at = lax.broadcasted_iota(jnp.int32, array.shape, 0) // step
        return jnp.where(first + at < lengths[0], array, 0.0)

    frames_out[...] = (
        frames[...].astype(f32) + live(projected[:count], frame_count)
    ).astype(bf16)
    memory_out[...] = live(projected[count + segs :], 1).astype(bf16)


def columns_kernel(mine, far, near_mine, near_far, out):
    width = mine.shape[1]
    for i, part in enumerate((mine, near_mine, far, near_far)):
        out[:, pl.ds(aligned(member_of() ^ i, width), width)] = part[...].astype(f32)


def gathered(piece):
    size = lax.axis_size("fsdp")
    pieces = {0: piece}
    bit = 1
    while bit < size:
        for have in sorted(pieces):
            pieces[have ^ bit] = swapped(pieces[have], "fsdp", bit)
        bit *= 2
    return [pieces[j] for j in range(size)]


def pairs(seg_size):
    straight, turned, first, last = [], [], [], []
    for s in range(seg_size):
        along = 2 if s & 1 else 1
        for f in range(GROUP):
            straight.append((s * GROUP + f, s * GROUP + (f ^ along)))
            turned.append((s * GROUP + f, s * GROUP + (f ^ along ^ 3)))
        k = s % GROUP
        first.append((s * GROUP + k, s * GROUP + (k ^ 1)))
        first.append(((s ^ 1) * GROUP + k, s * GROUP + (k ^ 2)))
        first.append(((s ^ 3) * GROUP + k, (s ^ 3) * GROUP + (k ^ 3)))
        last.append(((s ^ 3) * GROUP + (k ^ 3), s * GROUP + (k ^ 3)))
    return straight, turned, first, last


def on_device(
    frames, memory_in, lengths, ln_gain, w_query, w_key, w_value, w_out, grad_frames, grad_memory
):
    utterances, segs, frame_count, width = frames.shape
    seg_size = lax.axis_size("seg")
    fsdp_size = lax.axis_size("fsdp")
    group = GROUP
    assert utterances == 1 and segs == MEMORY and frame_count == LEFT and seg_size % group == 0
    heads = HEADS // group
    block = width // group
    rows = w_query.shape[0]
    frame_rows = segs * frame_count
    queries = frame_rows + 2 * segs
    halo_rows = LEFT + 2 * MEMORY
    keys = halo_rows + queries
    all_rows = halo_rows + group * queries
    seg = lax.axis_index("seg")
    member = seg % group

    crossed = fsdp_size == group
    own_blocks, tokens, tail = pl.pallas_call(
        functools.partial(pack_kernel, frame_count),
        in_specs=[hbm] * 8,
        out_specs=[vmem] * 3,
        out_shape=[
            jax.ShapeDtypeStruct((1 + crossed, rows, 3 * block), bf16),
            jax.ShapeDtypeStruct((2 * queries, width), bf16),
            jax.ShapeDtypeStruct((halo_rows, width), bf16),
        ],
        scratch_shapes=[
            pltpu.VMEM((frame_rows, width), bf16),
            pltpu.VMEM((2, segs, width), bf16),
            pltpu.VMEM((1, width), f32),
            pltpu.SemaphoreType.DMA((11,)),
        ],
        compiler_params=params(60),
        name="pack",
    )(
        w_query, w_key, w_value, frames.reshape(frame_rows, width),
        grad_frames.reshape(frame_rows, width), memory_in.reshape(segs, width),
        grad_memory.reshape(segs, width), ln_gain.reshape(1, width),
    )
    w_out, own_blocks = lax.optimization_barrier((w_out, own_blocks))

    far = swapped(tokens, "seg", 2)
    near = swapped(tokens, "seg", 1)
    starts = range(group, seg_size, group)
    halo = [
        lax.ppermute(tail, "seg", [(s - 1, s + ahead) for s in starts]) for ahead in (0, 2)
    ]
    if crossed:
        both = ("seg", "fsdp")
        straight, turned, first, last = pairs(seg_size)
        came = lax.ppermute(own_blocks, both, straight)
        wo_came = lax.ppermute(w_out, both, first)
        came, far, near, halo, wo_came = lax.optimization_barrier(
            (came, far, near, halo, wo_came)
        )
        wo_last = lax.ppermute(wo_came, both, last)
    else:
        came = jnp.concatenate([own_blocks, own_blocks])
        wo_near = lax.dynamic_slice_in_dim(
            lax.all_gather(w_out, "fsdp", axis=0, tiled=True), member * block, block, 0
        )
    mine, mine_values, other, far, far_grads = pl.pallas_call(
        split_kernel,
        in_specs=[vmem] * 4,
        out_specs=[vmem] * 5,
        out_shape=[jax.ShapeDtypeStruct((rows, 2 * block), bf16)]
        + [jax.ShapeDtypeStruct((rows, block), bf16)]
        + [jax.ShapeDtypeStruct(came.shape[1:], bf16)]
        + [
            jax.ShapeDtypeStruct((queries + halo_rows, width), bf16),
            jax.ShapeDtypeStruct((queries, width), bf16),
        ],
        compiler_params=params(),
        name="split",
    )(came, far, *halo)
    if crossed:
        other = swapped(other, "seg", 1)
        forwarded = lax.ppermute(mine, both, turned)
        wo_near = pl.pallas_call(
            pick_kernel,
            in_specs=[vmem] * 2,
            out_specs=vmem,
            out_shape=jax.ShapeDtypeStruct((block, width), bf16),
            compiler_params=params(),
            name="pick",
        )(w_out, wo_came)
    else:
        wqkv_parts = gathered(own_blocks)
    parts = [tokens, near, far, far_grads, swapped(far, "seg", 1), swapped(far_grads, "seg", 1)]

    x_all, x_turned, u_all = pl.pallas_call(
        merge_kernel,
        in_specs=[vmem] * len(parts),
        out_specs=[vmem] * 3,
        out_shape=[
            jax.ShapeDtypeStruct((all_rows, width), bf16),
            jax.ShapeDtypeStruct((width, all_rows), bf16),
            jax.ShapeDtypeStruct((group * queries, width), bf16),
        ],
        compiler_params=params(),
        name="merge",
    )(*parts)
    x_all, wo_near, mine_values = lax.optimization_barrier((x_all, wo_near, mine_values))
    if crossed:
        forwarded_values = lax.ppermute(mine_values, both, turned)

    soft_shape = jax.ShapeDtypeStruct((group, keys, heads * queries), bf16)
    values_shape = jax.ShapeDtypeStruct((all_rows, block), bf16)
    if crossed:
        early, early_values = pl.pallas_call(
            early_kernel,
            in_specs=[vmem] * 5,
            out_specs=[vmem] * 2,
            out_shape=[
                jax.ShapeDtypeStruct((all_rows, 2 * block), f32),
                jax.ShapeDtypeStruct((all_rows, block), f32),
            ],
            compiler_params=params(),
            name="early",
        )(x_all, own_blocks, mine, mine_values, other)
        wqkv_parts = [early, forwarded]
    soft, *values = pl.pallas_call(
        functools.partial(weights_kernel, heads, frame_count, segs, crossed),
        in_specs=[vmem] * (1 + len(wqkv_parts)),
        out_specs=[vmem] * (2 - crossed),
        out_shape=[soft_shape] + [values_shape] * (1 - crossed),
        scratch_shapes=[] if crossed else [pltpu.VMEM((width, 3 * block), bf16)],
        compiler_params=params(),
        name="soft_weights",
    )(x_all, *wqkv_parts)
    if crossed:
        values = pl.pallas_call(
            values_kernel,
            in_specs=[vmem] * 3,
            out_specs=vmem,
            out_shape=values_shape,
            compiler_params=params(),
            name="values",
        )(x_all, early_values, forwarded_values)
    else:
        (values,) = values

    values_grad_shape = jax.ShapeDtypeStruct((all_rows, block), bf16)
    wo_from = [wo_near] + ([wo_last] if crossed else [])
    wo_mine, values_grad = pl.pallas_call(
        functools.partial(grad_kernel, heads, frame_count, segs),
        in_specs=[smem] + [vmem] * (2 + len(wo_from)),
        out_specs=[vmem] * 2,
        out_shape=[jax.ShapeDtypeStruct((block, width), bf16), values_grad_shape],
        scratch_shapes=[pltpu.VMEM((all_rows, block), f32)],
        compiler_params=params(),
        name="values_grad",
    )(lengths, u_all, soft, *wo_from)

    def grad_rows(which, shapes):
        return pl.pallas_call(
            functools.partial(rows_kernel, which),
            in_specs=[vmem] * 2,
            out_specs=[vmem] * len(shapes),
            out_shape=shapes,
            compiler_params=params(),
            name="grad_rows_" + which,
        )(x_turned, values_grad)

    if crossed:
        (sent,) = grad_rows("sent", [jax.ShapeDtypeStruct((2, rows, block), bf16)])
        (kept,) = grad_rows("kept", [jax.ShapeDtypeStruct((2, rows, block), f32)])
    else:
        grad_chunks = grad_rows(
            "all", [jax.ShapeDtypeStruct((rows, block), bf16)] * fsdp_size
        )

    def attend(start, name):
        cut = queries // PIECES // 16 * 16
        sizes = [cut] * (PIECES - 1) + [queries - cut * (PIECES - 1)]
        keep, *send = pl.pallas_call(
            functools.partial(out_kernel, heads, start),
            in_specs=[vmem] * 3,
            out_specs=[vmem] * (1 + PIECES),
            out_shape=[jax.ShapeDtypeStruct((queries, width), f32)]
            + [jax.ShapeDtypeStruct((size, width), bf16) for size in sizes],
            compiler_params=params(),
            name=name,
        )(soft, values, wo_mine)
        return keep, send

    keep_far, send_far = attend(2, "attend_far")
    keep, send = attend(0, "attend_near")
    near = [swapped(piece, "seg", 1) for piece in send]
    near_far = [swapped(piece, "seg", 1) for piece in send_far]
    onward = pl.pallas_call(
        onward_kernel,
        in_specs=[vmem] * (1 + PIECES),
        out_specs=vmem,
        out_shape=jax.ShapeDtypeStruct((queries, width), bf16),
        compiler_params=params(),
        name="onward",
    )(keep_far, *near_far)
    if crossed:
        came = lax.ppermute(sent, both, straight)
        passing = (kept[1] + came[1].astype(f32)).astype(bf16)
        passing, onward = lax.optimization_barrier((passing, onward))
        last = lax.ppermute(passing, both, turned)
        grad_sum = kept[0] + came[0].astype(f32) + last.astype(f32)
    else:
        grad_sum = grad_chunks[0].astype(f32)
        for j in range(1, fsdp_size):
            grad_sum = grad_sum + swapped(grad_chunks[j], "fsdp", j).astype(f32)
    back = swapped(onward, "seg", 2)
    back = swapped(onward, "seg", 2)
    bit = group
    while bit < seg_size:
        mine = grad_sum.astype(bf16)
        other, back = lax.optimization_barrier((swapped(mine, "seg", bit), back))
        grad_sum = mine.astype(f32) + other.astype(f32)
        bit *= 2
    mine, near = lax.optimization_barrier((grad_sum.astype(bf16), near))
    frames_out, memory_out = pl.pallas_call(
        functools.partial(finish_kernel, frame_count),
        in_specs=[smem] + [vmem] * (3 + PIECES),
        out_specs=[vmem] * 2,
        out_shape=[
            jax.ShapeDtypeStruct((frame_rows, width), bf16),
            jax.ShapeDtypeStruct((segs, width), bf16),
        ],
        compiler_params=params(),
        name="finish",
    )(lengths, frames.reshape(frame_rows, width), keep, back, *near)
    far = swapped(mine, "seg", 2)
    value_grad = pl.pallas_call(
        columns_kernel,
        in_specs=[vmem] * 4,
        out_specs=vmem,
        out_shape=jax.ShapeDtypeStruct((rows, width), f32),
        compiler_params=params(),
        name="columns",
    )(mine, far, swapped(mine, "seg", 1), swapped(far, "seg", 1))
    frames_out = frames_out.reshape(frames.shape)
    memory_out = memory_out.reshape(memory_in.shape)
    return (frames_out, memory_out, value_grad)


def solution(mesh):
    return jax.shard_map(
        on_device,
        mesh=mesh,
        in_specs=(
            P("fsdp", "seg", None, None),
            P("fsdp", "seg", None),
            P("fsdp"),
            P(),
            P("fsdp", None),
            P("fsdp", None),
            P("fsdp", None),
            P("fsdp", None),
            P("fsdp", "seg", None, None),
            P("fsdp", "seg", None),
        ),
        out_specs=(P("fsdp", "seg", None, None), P("fsdp", "seg", None), P("fsdp", None)),
        check_vma=False,
    )
```

```python
import functools
import math

import jax
import jax.numpy as jnp
from jax import lax
from jax.experimental import pallas as pl
from jax.experimental.pallas import tpu as pltpu
from jax.sharding import PartitionSpec as P

HEADS = 16
LEFT = 16
MEMORY = 8
GROUP = 4
PIECES = 2


epsilon = 1e-05
masked_score = -1e30
bf16 = jnp.bfloat16
f32 = jnp.float32
vmem = pl.BlockSpec(memory_space=pltpu.VMEM)
smem = pl.BlockSpec(memory_space=pltpu.SMEM)
hbm = pl.BlockSpec(memory_space=pltpu.HBM)
NT = (((1,), (1,)), ((), ()))
TN = (((0,), (0,)), ((), ()))


def params(mib=40):
    return pltpu.CompilerParams(vmem_limit_bytes=mib * 1024 * 1024)


def swapped(array, axis, bit):
    size = lax.axis_size(axis)
    return lax.ppermute(array, axis, [(i, i ^ bit) for i in range(size)])


def halving_bits(size):
    return [1 << b for b in range(size.bit_length() - 1)]


def member_of():
    return lax.axis_index("seg") % GROUP


def aligned(start, step):
    return pl.multiple_of(start * step, step)


def normed_rows(rows, gain):
    wide = rows.astype(f32)
    centred = wide - jnp.mean(wide, axis=-1, keepdims=True)
    var = jnp.mean(centred * centred, axis=-1, keepdims=True)
    return (centred * lax.rsqrt(var + epsilon) * gain).astype(bf16)


def pack_kernel(frame_count, wq, wk, wv, frames, gf, mem, gm, gain, *refs):
    blocks, tokens, tail, raw, few, one, sems = refs
    width = blocks.shape[2] // 3
    rows, model_width = gf.shape
    segs = mem.shape[0]
    half = tokens.shape[0] // 2
    copies = [
        pltpu.make_async_copy(frames, raw, sems.at[0]),
        pltpu.make_async_copy(gain, one, sems.at[1]),
        pltpu.make_async_copy(mem, few.at[0], sems.at[2]),
        pltpu.make_async_copy(gm, few.at[1], sems.at[3]),
        pltpu.make_async_copy(gf, tokens.at[pl.ds(half, rows)], sems.at[4]),
    ]
    for i in range(blocks.shape[0]):
        at = aligned(member_of() ^ i, width)
        for j, w in enumerate((wq, wk, wv)):
            into = blocks.at[i, :, pl.ds(j * width, width)]
            sem = sems.at[5 + 3 * i + j]
            copies.append(pltpu.make_async_copy(w.at[:, pl.ds(at, width)], into, sem))
    for copy in copies:
        copy.start()
    for copy in copies[:4]:
        copy.wait()
    normed = normed_rows(raw[...], one[...])
    tokens[:rows, :] = normed
    summary = jnp.sum(normed.astype(f32).reshape(segs, frame_count, model_width), axis=1)
    tokens[rows:half, :] = jnp.concatenate(
        [few[0], (summary / frame_count).astype(bf16)], axis=0
    )
    tokens[half + rows :, :] = jnp.concatenate([jnp.zeros_like(few[1]), few[1]], axis=0)
    tail[...] = tokens[half - tail.shape[0] : half, :]
    for copy in copies[4:]:
        copy.wait()


def split_kernel(both, far, halo_first, halo_third, mine, mine_values, other, far_tokens, far_grads):
    width = mine.shape[1]
    mine[...] = both[0, :, :width]
    mine_values[...] = both[0, :, width:]
    other[...] = both[1]
    half = far_grads.shape[0]
    far_tokens[:half, :] = far[:half, :]
    far_tokens[half:, :] = jnp.where(member_of() == 0, halo_first[...], halo_third[...])
    far_grads[...] = far[half:, :]


def merge_kernel(tokens, near, far, far_grads, last, last_grads, x_all, x_turned, u_all):
    half = far_grads.shape[0]
    parts = [
        (tokens[:half, :], tokens[half:, :]),
        (near[:half, :], near[half:, :]),
        (far[:half, :], far_grads[...]),
        (last[:half, :], last_grads[...]),
    ]
    halo = far.shape[0] - half
    odd = (member_of() & 1) > 0
    x_all[:halo, :] = jnp.where(odd, last[half:, :], far[half:, :])
    for i, (x_part, u_part) in enumerate(parts):
        at = aligned(member_of() ^ i, half)
        x_all[pl.ds(pl.multiple_of(halo + at, 16), half), :] = x_part
        u_all[pl.ds(at, half), :] = u_part
    x_turned[...] = x_all[...].T


def pick_kernel(own, came, wo):
    wo[...] = jnp.where(lax.axis_index("fsdp") == member_of(), own[...], came[...])


def assemble(pieces, whole):
    own = lax.axis_index("fsdp")
    rows = pieces[0].shape[-2]
    for j, piece in enumerate(pieces):
        into = whole.at[pl.ds(aligned(own ^ j, rows), rows), :]
        into[...] = piece[0] if len(piece.shape) == 3 else piece[...]


def head_stack(array, heads):
    width = array.shape[1]
    head = lax.broadcasted_iota(jnp.int32, array.shape, 1) // (width // heads)
    zero = jnp.zeros_like(array)
    return jnp.concatenate([jnp.where(head == h, array, zero) for h in range(heads)], axis=0)


def early_kernel(x_all, mine, beside, beside_values, swapped_in, total, total_values):
    own = lax.axis_index("fsdp")
    along = 1 + (lax.axis_index("seg") & 1)
    rows, width = beside.shape
    columns = lambda j: x_all[:, pl.ds(aligned(own ^ j, rows), rows)]
    product = jnp.dot(columns(0), mine[0], preferred_element_type=f32) + jnp.dot(
        columns(along ^ 3), swapped_in[...], preferred_element_type=f32
    )
    total[...] = product[:, :width] + jnp.dot(
        columns(along), beside[...], preferred_element_type=f32
    )
    total_values[...] = product[:, width:] + jnp.dot(
        columns(along), beside_values[...], preferred_element_type=f32
    )


def values_kernel(x_all, total, last, values):
    rows = last.shape[0]
    at = aligned(lax.axis_index("fsdp") ^ 3, rows)
    columns = x_all[:, pl.ds(at, rows)]
    values[...] = (
        total[...] + jnp.dot(columns, last[...], preferred_element_type=f32)
    ).astype(bf16)


def weights_kernel(heads, frame_count, segs, crossed, x_all, *refs):
    if crossed:
        total, last, soft = refs
        rows = last.shape[0]
        at = aligned(lax.axis_index("fsdp") ^ 3, rows)
        product = total[...] + jnp.dot(
            x_all[:, pl.ds(at, rows)], last[...], preferred_element_type=f32
        )
    else:
        soft, values, whole = refs[-3:]
        assemble(refs[:-3], whole)
        product = jnp.dot(x_all[...], whole[...], preferred_element_type=f32)
    projected = product.astype(bf16)
    blocks, keys, lanes = soft.shape
    queries = lanes // heads
    halo = keys - queries
    frames = segs * frame_count
    block = projected.shape[1] // (2 if crossed else 3)
    q_all, k_all = projected[:, :block], projected[:, block : 2 * block]
    if not crossed:
        values[...] = projected[:, 2 * block :]
    key = lax.broadcasted_iota(jnp.int32, (keys, lanes), 0)
    row = lax.broadcasted_iota(jnp.int32, (keys, lanes), 1)
    for h in range(1, heads):
        row = jnp.where(row >= queries, row - queries, row)
    at = jnp.where(row < frames, row // frame_count, jnp.maximum(row - frames - segs, 0))
    own = key - halo
    own_seg = own // frame_count
    own_mem = own - frames
    valid_own = ((own >= 0) & (own < frames) & ((own_seg == at) | (own_seg == at - 1))) | (
        (own_mem >= 0) & (own_mem < segs) & (own_mem < at) & (own_mem >= at - MEMORY)
    )
    halo_mem = key - LEFT
    valid_halo = ((key < LEFT) & (at == 0)) | (
        (halo_mem >= 0) & (halo_mem < MEMORY) & (halo_mem >= at)
    )
    inside = lax.axis_index("seg") >= blocks
    scale = 1.0 / math.sqrt(block // heads)
    for b in range(blocks):
        valid = valid_own | (valid_halo & inside if b == 0 else valid_halo)
        start = b * queries
        q_b = head_stack(q_all[halo + start : halo + start + queries], heads)
        scores = (
            lax.dot_general(k_all[start : start + keys], q_b, NT, preferred_element_type=f32)
            * scale
        )
        scores = jnp.where(valid, scores, masked_score)
        exponent = jnp.exp(scores - jnp.max(scores, axis=0, keepdims=True))
        soft[b] = (exponent / jnp.sum(exponent, axis=0, keepdims=True)).astype(bf16)


def grad_kernel(heads, frame_count, segs, crossed, lengths, u_all, soft, x_turned, *refs):
    outputs = 3 + crossed
    wo_from, (wo, values, *sent, total) = refs[:-outputs], refs[-outputs:]
    blocks, keys, lanes = soft.shape
    queries = lanes // heads
    frames = segs * frame_count
    wo[...] = wo_from[0][...]
    if len(wo_from) > 1:
        opposite = (lax.axis_index("fsdp") ^ member_of()) == 3
        wo[...] = jnp.where(opposite, wo_from[1][...], wo[...])
    back = lax.dot_general(u_all[...], wo[...], NT, preferred_element_type=f32)
    row = lax.broadcasted_iota(jnp.int32, (queries, wo.shape[0]), 0)
    seg_of = jnp.where(row < frames, row // frame_count, row - frames - segs)
    first = lax.axis_index("seg") - member_of()
    split = keys - queries
    total[:split, :] = jnp.zeros((split, total.shape[1]), f32)
    for b in range(blocks):
        start = b * queries
        live = ((first + b) * segs + seg_of < lengths[0]).astype(f32)
        grad_attended = head_stack((live * back[start : start + queries]).astype(bf16), heads)
        term = jnp.dot(soft[b], grad_attended, preferred_element_type=f32)
        total[start : start + split, :] += term[:split]
        total[start + split : start + keys, :] = term[split:]
    values[...] = total[...].astype(bf16)
    if crossed:
        rows_kernel("sent", x_turned, values, *sent)


def rows_kernel(which, x_turned, values, *outs):
    own = lax.axis_index("fsdp")
    along = 1 + (lax.axis_index("seg") & 1)
    parts = {"kept": (0, along ^ 3), "sent": (along, 3)}
    if which in parts:
        into = [outs[0].at[i] for i in range(2)]
        apart = parts[which]
    else:
        into, apart = outs, range(len(outs))
    rows = into[0].shape[0]
    for out, j in zip(into, apart, strict=True):
        at = pl.ds(aligned(own ^ j, rows), rows)
        out[...] = jnp.dot(
            x_turned[at, :], values[...], preferred_element_type=f32
        ).astype(out.dtype)


def out_kernel(heads, first, soft, values, *refs):
    wo, keep, *send = refs
    blocks, keys, lanes = soft.shape
    queries = lanes // heads
    width = values.shape[1]
    head = lax.broadcasted_iota(jnp.int32, (queries, width), 1) // (width // heads)
    for i in (first, first + 1):
        b = member_of() ^ i
        stacked = lax.dot_general(
            soft[b],
            values[pl.ds(aligned(b, queries), keys), :],
            TN,
            preferred_element_type=f32,
        )
        attended = stacked[:queries]
        for h in range(1, heads):
            attended = jnp.where(head == h, stacked[h * queries : (h + 1) * queries], attended)
        projected = jnp.dot(attended.astype(bf16), wo[...], preferred_element_type=f32)
        if i == first:
            keep[...] = projected
        else:
            start = 0
            for into in send:
                into[...] = projected[start : start + into.shape[0]].astype(into.dtype)
                start += into.shape[0]


def onward_kernel(keep, *refs):
    pieces, onward = refs[:-1], refs[-1]
    start = 0
    for piece in pieces:
        part = slice(start, start + piece.shape[0])
        onward[part, :] = (keep[part, :] + piece[...].astype(f32)).astype(bf16)
        start += piece.shape[0]


def finish_kernel(frame_count, lengths, frames, keep, back, *refs):
    pieces, frames_out, memory_out = refs[:-2], refs[-2], refs[-1]
    segs = memory_out.shape[0]
    count = frames.shape[0]
    near = jnp.concatenate([piece[...].astype(f32) for piece in pieces], axis=0)
    projected = keep[...] + near + back[...].astype(f32)
    first = lax.axis_index("seg") * segs

    def live(array, step):
        at = lax.broadcasted_iota(jnp.int32, array.shape, 0) // step
        return jnp.where(first + at < lengths[0], array, 0.0)

    frames_out[...] = (
        frames[...].astype(f32) + live(projected[:count], frame_count)
    ).astype(bf16)
    memory_out[...] = live(projected[count + segs :], 1).astype(bf16)


def columns_kernel(apart, *refs):
    count = len(apart)
    blocks, (out, wide, sems) = refs[:count], refs[-3:]
    width = blocks[0].shape[1]
    copies = []
    for i, block in enumerate(blocks):
        wide[i] = block[...].astype(f32)
        at = pl.ds(aligned(member_of() ^ apart[i], width), width)
        copies.append(pltpu.make_async_copy(wide.at[i], out.at[:, at], sems.at[i]))
        copies[-1].start()
    for copy in copies:
        copy.wait()


def gathered(piece):
    size = lax.axis_size("fsdp")
    pieces = {0: piece}
    bit = 1
    while bit < size:
        for have in sorted(pieces):
            pieces[have ^ bit] = swapped(pieces[have], "fsdp", bit)
        bit *= 2
    return [pieces[j] for j in range(size)]


def pairs(seg_size):
    straight, turned, first, last = [], [], [], []
    for s in range(seg_size):
        along = 2 if s & 1 else 1
        for f in range(GROUP):
            straight.append((s * GROUP + f, s * GROUP + (f ^ along)))
            turned.append((s * GROUP + f, s * GROUP + (f ^ along ^ 3)))
        k = s % GROUP
        first.append((s * GROUP + k, s * GROUP + (k ^ 1)))
        first.append(((s ^ 1) * GROUP + k, s * GROUP + (k ^ 2)))
        first.append(((s ^ 3) * GROUP + k, (s ^ 3) * GROUP + (k ^ 3)))
        last.append(((s ^ 3) * GROUP + (k ^ 3), s * GROUP + (k ^ 3)))
    return straight, turned, first, last


def on_device(
    frames, memory_in, lengths, ln_gain, w_query, w_key, w_value, w_out, grad_frames, grad_memory
):
    utterances, segs, frame_count, width = frames.shape
    seg_size = lax.axis_size("seg")
    fsdp_size = lax.axis_size("fsdp")
    group = GROUP
    assert utterances == 1 and segs == MEMORY and frame_count == LEFT and seg_size % group == 0
    heads = HEADS // group
    block = width // group
    rows = w_query.shape[0]
    frame_rows = segs * frame_count
    queries = frame_rows + 2 * segs
    halo_rows = LEFT + 2 * MEMORY
    keys = halo_rows + queries
    all_rows = halo_rows + group * queries
    seg = lax.axis_index("seg")
    member = seg % group

    crossed = fsdp_size == group
    own_blocks, tokens, tail = pl.pallas_call(
        functools.partial(pack_kernel, frame_count),
        in_specs=[hbm] * 8,
        out_specs=[vmem] * 3,
        out_shape=[
            jax.ShapeDtypeStruct((1 + crossed, rows, 3 * block), bf16),
            jax.ShapeDtypeStruct((2 * queries, width), bf16),
            jax.ShapeDtypeStruct((halo_rows, width), bf16),
        ],
        scratch_shapes=[
            pltpu.VMEM((frame_rows, width), bf16),
            pltpu.VMEM((2, segs, width), bf16),
            pltpu.VMEM((1, width), f32),
            pltpu.SemaphoreType.DMA((11,)),
        ],
        compiler_params=params(60),
        name="pack",
    )(
        w_query, w_key, w_value, frames.reshape(frame_rows, width),
        grad_frames.reshape(frame_rows, width), memory_in.reshape(segs, width),
        grad_memory.reshape(segs, width), ln_gain.reshape(1, width),
    )
    w_out, own_blocks = lax.optimization_barrier((w_out, own_blocks))

    far = swapped(tokens, "seg", 2)
    near = swapped(tokens, "seg", 1)
    starts = range(group, seg_size, group)
    halo = [
        lax.ppermute(tail, "seg", [(s - 1, s + ahead) for s in starts]) for ahead in (0, 2)
    ]
    if crossed:
        both = ("seg", "fsdp")
        straight, turned, first, last = pairs(seg_size)
        came = lax.ppermute(own_blocks, both, straight)
        wo_came = lax.ppermute(w_out, both, first)
        came, far, near, halo, wo_came = lax.optimization_barrier(
            (came, far, near, halo, wo_came)
        )
        wo_last = lax.ppermute(wo_came, both, last)
    else:
        came = jnp.concatenate([own_blocks, own_blocks])
        wo_near = lax.dynamic_slice_in_dim(
            lax.all_gather(w_out, "fsdp", axis=0, tiled=True), member * block, block, 0
        )
    mine, mine_values, other, far, far_grads = pl.pallas_call(
        split_kernel,
        in_specs=[vmem] * 4,
        out_specs=[vmem] * 5,
        out_shape=[jax.ShapeDtypeStruct((rows, 2 * block), bf16)]
        + [jax.ShapeDtypeStruct((rows, block), bf16)]
        + [jax.ShapeDtypeStruct(came.shape[1:], bf16)]
        + [
            jax.ShapeDtypeStruct((queries + halo_rows, width), bf16),
            jax.ShapeDtypeStruct((queries, width), bf16),
        ],
        compiler_params=params(),
        name="split",
    )(came, far, *halo)
    if crossed:
        other = swapped(other, "seg", 1)
        forwarded = lax.ppermute(mine, both, turned)
        wo_near = pl.pallas_call(
            pick_kernel,
            in_specs=[vmem] * 2,
            out_specs=vmem,
            out_shape=jax.ShapeDtypeStruct((block, width), bf16),
            compiler_params=params(),
            name="pick",
        )(w_out, wo_came)
    else:
        wqkv_parts = gathered(own_blocks)
    parts = [tokens, near, far, far_grads, swapped(far, "seg", 1), swapped(far_grads, "seg", 1)]

    x_all, x_turned, u_all = pl.pallas_call(
        merge_kernel,
        in_specs=[vmem] * len(parts),
        out_specs=[vmem] * 3,
        out_shape=[
            jax.ShapeDtypeStruct((all_rows, width), bf16),
            jax.ShapeDtypeStruct((width, all_rows), bf16),
            jax.ShapeDtypeStruct((group * queries, width), bf16),
        ],
        compiler_params=params(),
        name="merge",
    )(*parts)
    x_all, wo_near, mine_values = lax.optimization_barrier((x_all, wo_near, mine_values))
    if crossed:
        forwarded_values = lax.ppermute(mine_values, both, turned)

    soft_shape = jax.ShapeDtypeStruct((group, keys, heads * queries), bf16)
    values_shape = jax.ShapeDtypeStruct((all_rows, block), bf16)
    if crossed:
        early, early_values = pl.pallas_call(
            early_kernel,
            in_specs=[vmem] * 5,
            out_specs=[vmem] * 2,
            out_shape=[
                jax.ShapeDtypeStruct((all_rows, 2 * block), f32),
                jax.ShapeDtypeStruct((all_rows, block), f32),
            ],
            compiler_params=params(),
            name="early",
        )(x_all, own_blocks, mine, mine_values, other)
        wqkv_parts = [early, forwarded]
    soft, *values = pl.pallas_call(
        functools.partial(weights_kernel, heads, frame_count, segs, crossed),
        in_specs=[vmem] * (1 + len(wqkv_parts)),
        out_specs=[vmem] * (2 - crossed),
        out_shape=[soft_shape] + [values_shape] * (1 - crossed),
        scratch_shapes=[] if crossed else [pltpu.VMEM((width, 3 * block), bf16)],
        compiler_params=params(),
        name="soft_weights",
    )(x_all, *wqkv_parts)
    if crossed:
        values = pl.pallas_call(
            values_kernel,
            in_specs=[vmem] * 3,
            out_specs=vmem,
            out_shape=values_shape,
            compiler_params=params(),
            name="values",
        )(x_all, early_values, forwarded_values)
    else:
        (values,) = values

    values_grad_shape = jax.ShapeDtypeStruct((all_rows, block), bf16)
    wo_from = [wo_near] + ([wo_last] if crossed else [])
    sent_shape = [jax.ShapeDtypeStruct((2, rows, block), bf16)] * crossed
    wo_mine, values_grad, *sent = pl.pallas_call(
        functools.partial(grad_kernel, heads, frame_count, segs, crossed),
        in_specs=[smem] + [vmem] * (3 + len(wo_from)),
        out_specs=[vmem] * (2 + crossed),
        out_shape=[jax.ShapeDtypeStruct((block, width), bf16), values_grad_shape] + sent_shape,
        scratch_shapes=[pltpu.VMEM((all_rows, block), f32)],
        compiler_params=params(),
        name="values_grad",
    )(lengths, u_all, soft, x_turned, *wo_from)

    def grad_rows(which, shapes):
        return pl.pallas_call(
            functools.partial(rows_kernel, which),
            in_specs=[vmem] * 2,
            out_specs=[vmem] * len(shapes),
            out_shape=shapes,
            compiler_params=params(),
            name="grad_rows_" + which,
        )(x_turned, values_grad)

    if crossed:
        (sent,) = sent
        (kept,) = grad_rows("kept", [jax.ShapeDtypeStruct((2, rows, block), f32)])
    else:
        grad_chunks = grad_rows(
            "all", [jax.ShapeDtypeStruct((rows, block), bf16)] * fsdp_size
        )

    def attend(start, name, pieces):
        cut = queries // pieces // 16 * 16
        sizes = [cut] * (pieces - 1) + [queries - cut * (pieces - 1)]
        keep, *send = pl.pallas_call(
            functools.partial(out_kernel, heads, start),
            in_specs=[vmem] * 3,
            out_specs=[vmem] * (1 + pieces),
            out_shape=[jax.ShapeDtypeStruct((queries, width), f32)]
            + [jax.ShapeDtypeStruct((size, width), bf16) for size in sizes],
            compiler_params=params(),
            name=name,
        )(soft, values, wo_mine)
        return keep, send

    keep_far, send_far = attend(2, "attend_far", PIECES)
    keep, send = attend(0, "attend_near", 1)
    near = [swapped(piece, "seg", 1) for piece in send]
    near_far = [swapped(piece, "seg", 1) for piece in send_far]
    onward = pl.pallas_call(
        onward_kernel,
        in_specs=[vmem] * (1 + PIECES),
        out_specs=vmem,
        out_shape=jax.ShapeDtypeStruct((queries, width), bf16),
        compiler_params=params(),
        name="onward",
    )(keep_far, *near_far)
    if crossed:
        came = lax.ppermute(sent, both, straight)
        passing = (kept[1] + came[1].astype(f32)).astype(bf16)
        passing, onward = lax.optimization_barrier((passing, onward))
        last = lax.ppermute(passing, both, turned)
        grad_sum = kept[0] + came[0].astype(f32) + last.astype(f32)
    else:
        grad_sum = grad_chunks[0].astype(f32)
        for j in range(1, fsdp_size):
            grad_sum = grad_sum + swapped(grad_chunks[j], "fsdp", j).astype(f32)
    back = swapped(onward, "seg", 2)
    back = swapped(onward, "seg", 2)
    bit = group
    while bit < seg_size:
        mine = grad_sum.astype(bf16)
        other, back = lax.optimization_barrier((swapped(mine, "seg", bit), back))
        grad_sum = mine.astype(f32) + other.astype(f32)
        bit *= 2
    mine = grad_sum.astype(bf16)
    frames_out, memory_out = pl.pallas_call(
        functools.partial(finish_kernel, frame_count),
        in_specs=[smem] + [vmem] * 4,
        out_specs=[vmem] * 2,
        out_shape=[
            jax.ShapeDtypeStruct((frame_rows, width), bf16),
            jax.ShapeDtypeStruct((segs, width), bf16),
        ],
        compiler_params=params(),
        name="finish",
    )(lengths, frames.reshape(frame_rows, width), keep, back, *near)
    far, frames_out, memory_out = lax.optimization_barrier(
        (swapped(mine, "seg", 2), frames_out, memory_out)
    )

    def columns(apart, blocks, *onto):
        count = len(blocks)
        return pl.pallas_call(
            functools.partial(columns_kernel, apart),
            in_specs=[vmem] * count + [hbm] * len(onto),
            out_specs=hbm,
            out_shape=jax.ShapeDtypeStruct((rows, width), f32),
            scratch_shapes=[
                pltpu.VMEM((count, rows, block), f32),
                pltpu.SemaphoreType.DMA((count,)),
            ],
            input_output_aliases={count: 0} if onto else {},
            compiler_params=params(),
            name="columns" + "_rest" * len(onto),
        )(*blocks, *onto)

    begun = columns((0, 2, 1), (mine, far, swapped(mine, "seg", 1)))
    value_grad = columns((3,), (swapped(far, "seg", 1),), begun)
    frames_out = frames_out.reshape(frames.shape)
    memory_out = memory_out.reshape(memory_in.shape)
    return (frames_out, memory_out, value_grad)


def solution(mesh):
    return jax.shard_map(
        on_device,
        mesh=mesh,
        in_specs=(
            P("fsdp", "seg", None, None),
            P("fsdp", "seg", None),
            P("fsdp"),
            P(),
            P("fsdp", None),
            P("fsdp", None),
            P("fsdp", None),
            P("fsdp", None),
            P("fsdp", "seg", None, None),
            P("fsdp", "seg", None),
        ),
        out_specs=(P("fsdp", "seg", None, None), P("fsdp", "seg", None), P("fsdp", None)),
        check_vma=False,
    )
```

```python
import functools
import math

import jax
import jax.numpy as jnp
from jax import lax
from jax.experimental import pallas as pl
from jax.experimental.pallas import tpu as pltpu
from jax.sharding import PartitionSpec as P

HEADS = 16
LEFT = 16
MEMORY = 8
GROUP = 4
PIECES = 2


epsilon = 1e-05
masked_score = -1e30
bf16 = jnp.bfloat16
f32 = jnp.float32
vmem = pl.BlockSpec(memory_space=pltpu.VMEM)
smem = pl.BlockSpec(memory_space=pltpu.SMEM)
hbm = pl.BlockSpec(memory_space=pltpu.HBM)
NT = (((1,), (1,)), ((), ()))
TN = (((0,), (0,)), ((), ()))


def params(mib=40):
    return pltpu.CompilerParams(vmem_limit_bytes=mib * 1024 * 1024)


def swapped(array, axis, bit):
    size = lax.axis_size(axis)
    return lax.ppermute(array, axis, [(i, i ^ bit) for i in range(size)])


def halving_bits(size):
    return [1 << b for b in range(size.bit_length() - 1)]


def member_of():
    return lax.axis_index("seg") % GROUP


def aligned(start, step):
    return pl.multiple_of(start * step, step)


def normed_rows(rows, gain):
    wide = rows.astype(f32)
    centred = wide - jnp.mean(wide, axis=-1, keepdims=True)
    var = jnp.mean(centred * centred, axis=-1, keepdims=True)
    return (centred * lax.rsqrt(var + epsilon) * gain).astype(bf16)


def pack_kernel(frame_count, wq, wk, wv, frames, gf, mem, gm, gain, *refs):
    blocks, tokens, tail, raw, few, one, sems = refs
    width = blocks.shape[2] // 3
    rows, model_width = gf.shape
    segs = mem.shape[0]
    half = tokens.shape[0] // 2
    copies = [
        pltpu.make_async_copy(frames, raw, sems.at[0]),
        pltpu.make_async_copy(gain, one, sems.at[1]),
        pltpu.make_async_copy(mem, few.at[0], sems.at[2]),
        pltpu.make_async_copy(gm, few.at[1], sems.at[3]),
        pltpu.make_async_copy(gf, tokens.at[pl.ds(half, rows)], sems.at[4]),
    ]
    for i in range(blocks.shape[0]):
        at = aligned(member_of() ^ i, width)
        for j, w in enumerate((wq, wk, wv)):
            into = blocks.at[i, :, pl.ds(j * width, width)]
            sem = sems.at[5 + 3 * i + j]
            copies.append(pltpu.make_async_copy(w.at[:, pl.ds(at, width)], into, sem))
    for copy in copies:
        copy.start()
    for copy in copies[:4]:
        copy.wait()
    normed = normed_rows(raw[...], one[...])
    tokens[:rows, :] = normed
    summary = jnp.sum(normed.astype(f32).reshape(segs, frame_count, model_width), axis=1)
    tokens[rows:half, :] = jnp.concatenate(
        [few[0], (summary / frame_count).astype(bf16)], axis=0
    )
    tokens[half + rows :, :] = jnp.concatenate([jnp.zeros_like(few[1]), few[1]], axis=0)
    tail[...] = tokens[half - tail.shape[0] : half, :]
    for copy in copies[4:]:
        copy.wait()


def split_kernel(both, far, halo_first, halo_third, mine, mine_values, other, far_tokens, far_grads):
    width = mine.shape[1]
    mine[...] = both[0, :, :width]
    mine_values[...] = both[0, :, width:]
    other[...] = both[1]
    half = far_grads.shape[0]
    far_tokens[:half, :] = far[:half, :]
    far_tokens[half:, :] = jnp.where(member_of() == 0, halo_first[...], halo_third[...])
    far_grads[...] = far[half:, :]


def merge_kernel(tokens, near, far, far_grads, last, last_grads, x_all, x_turned, u_all):
    half = far_grads.shape[0]
    parts = [
        (tokens[:half, :], tokens[half:, :]),
        (near[:half, :], near[half:, :]),
        (far[:half, :], far_grads[...]),
        (last[:half, :], last_grads[...]),
    ]
    halo = far.shape[0] - half
    odd = (member_of() & 1) > 0
    x_all[:halo, :] = jnp.where(odd, last[half:, :], far[half:, :])
    for i, (x_part, u_part) in enumerate(parts):
        at = aligned(member_of() ^ i, half)
        x_all[pl.ds(pl.multiple_of(halo + at, 16), half), :] = x_part
        u_all[pl.ds(at, half), :] = u_part
    x_turned[...] = x_all[...].T


def pick_kernel(own, came, wo):
    wo[...] = jnp.where(lax.axis_index("fsdp") == member_of(), own[...], came[...])


def assemble(pieces, whole):
    own = lax.axis_index("fsdp")
    rows = pieces[0].shape[-2]
    for j, piece in enumerate(pieces):
        into = whole.at[pl.ds(aligned(own ^ j, rows), rows), :]
        into[...] = piece[0] if len(piece.shape) == 3 else piece[...]


def head_stack(array, heads):
    width = array.shape[1]
    head = lax.broadcasted_iota(jnp.int32, array.shape, 1) // (width // heads)
    zero = jnp.zeros_like(array)
    return jnp.concatenate([jnp.where(head == h, array, zero) for h in range(heads)], axis=0)


def early_kernel(x_all, mine, beside, beside_values, swapped_in, total, total_values):
    own = lax.axis_index("fsdp")
    along = 1 + (lax.axis_index("seg") & 1)
    rows, width = beside.shape
    columns = lambda j: x_all[:, pl.ds(aligned(own ^ j, rows), rows)]
    product = jnp.dot(columns(0), mine[0], preferred_element_type=f32) + jnp.dot(
        columns(along ^ 3), swapped_in[...], preferred_element_type=f32
    )
    total[...] = product[:, :width] + jnp.dot(
        columns(along), beside[...], preferred_element_type=f32
    )
    total_values[...] = product[:, width:] + jnp.dot(
        columns(along), beside_values[...], preferred_element_type=f32
    )


def values_kernel(x_all, total, last, values):
    rows = last.shape[0]
    at = aligned(lax.axis_index("fsdp") ^ 3, rows)
    columns = x_all[:, pl.ds(at, rows)]
    values[...] = (
        total[...] + jnp.dot(columns, last[...], preferred_element_type=f32)
    ).astype(bf16)


def weights_kernel(heads, crossed, x_all, bias, *refs):
    if crossed:
        total, last, soft = refs
        rows = last.shape[0]
        at = aligned(lax.axis_index("fsdp") ^ 3, rows)
        product = total[...] + jnp.dot(
            x_all[:, pl.ds(at, rows)], last[...], preferred_element_type=f32
        )
    else:
        soft, values, whole = refs[-3:]
        assemble(refs[:-3], whole)
        product = jnp.dot(x_all[...], whole[...], preferred_element_type=f32)
    projected = product.astype(bf16)
    blocks, keys, lanes = soft.shape
    queries = lanes // heads
    halo = keys - queries
    block = projected.shape[1] // (2 if crossed else 3)
    q_all, k_all = projected[:, :block], projected[:, block : 2 * block]
    if not crossed:
        values[...] = projected[:, 2 * block :]
    scale = 1.0 / math.sqrt(block // heads)
    for b in range(blocks):
        start = b * queries
        q_b = head_stack(q_all[halo + start : halo + start + queries], heads)
        scores = (
            lax.dot_general(k_all[start : start + keys], q_b, NT, preferred_element_type=f32)
            * scale
            + bias[min(b, 1)]
        )
        exponent = jnp.exp(scores - jnp.max(scores, axis=0, keepdims=True))
        inverse = 1.0 / jnp.sum(exponent, axis=0, keepdims=True)
        soft[b] = (exponent * inverse).astype(bf16)


def mask_kernel(heads, frame_count, segs, group, bias):
    _, keys, lanes = bias.shape
    queries = lanes // heads
    halo = keys - queries
    frames = segs * frame_count
    key = lax.broadcasted_iota(jnp.int32, (keys, lanes), 0)
    row = lax.broadcasted_iota(jnp.int32, (keys, lanes), 1)
    for h in range(1, heads):
        row = jnp.where(row >= queries, row - queries, row)
    at = jnp.where(row < frames, row // frame_count, jnp.maximum(row - frames - segs, 0))
    own = key - halo
    own_seg = own // frame_count
    own_mem = own - frames
    valid_own = ((own >= 0) & (own < frames) & ((own_seg == at) | (own_seg == at - 1))) | (
        (own_mem >= 0) & (own_mem < segs) & (own_mem < at) & (own_mem >= at - MEMORY)
    )
    halo_mem = key - LEFT
    valid_halo = ((key < LEFT) & (at == 0)) | (
        (halo_mem >= 0) & (halo_mem < MEMORY) & (halo_mem >= at)
    )
    inside = lax.axis_index("seg") >= group
    bias[0] = jnp.where(valid_own | (valid_halo & inside), 0.0, masked_score)
    bias[1] = jnp.where(valid_own | valid_halo, 0.0, masked_score)


def back_kernel(u_all, wo, back):
    back[...] = lax.dot_general(u_all[...], wo[...], NT, preferred_element_type=f32)


def grad_kernel(heads, frame_count, segs, crossed, lengths, u_all, soft, x_turned, early, *refs):
    outputs = 4 + crossed
    wo_from, (wo, values, *sent, total, back) = refs[:-outputs], refs[-outputs:]
    blocks, keys, lanes = soft.shape
    queries = lanes // heads
    frames = segs * frame_count
    wo[...] = wo_from[0][...]
    back[...] = early[...]
    if len(wo_from) > 1:

        @pl.when((lax.axis_index("fsdp") ^ member_of()) == 3)
        def _():
            wo[...] = wo_from[1][...]
            back[...] = lax.dot_general(u_all[...], wo[...], NT, preferred_element_type=f32)

    row = lax.broadcasted_iota(jnp.int32, (queries, wo.shape[0]), 0)
    seg_of = jnp.where(row < frames, row // frame_count, row - frames - segs)
    first = lax.axis_index("seg") - member_of()
    split = keys - queries
    total[:split, :] = jnp.zeros((split, total.shape[1]), f32)
    for b in range(blocks):
        start = b * queries
        live = ((first + b) * segs + seg_of < lengths[0]).astype(f32)
        grad_attended = head_stack((live * back[start : start + queries]).astype(bf16), heads)
        term = jnp.dot(soft[b], grad_attended, preferred_element_type=f32)
        total[start : start + split, :] += term[:split]
        total[start + split : start + keys, :] = term[split:]
    values[...] = total[...].astype(bf16)
    if crossed:
        rows_kernel("sent", x_turned, values, *sent)


def rows_kernel(which, x_turned, values, *outs):
    own = lax.axis_index("fsdp")
    along = 1 + (lax.axis_index("seg") & 1)
    parts = {"kept": (0, along ^ 3), "sent": (along, 3)}
    if which in parts:
        into = [outs[0].at[i] for i in range(2)]
        apart = parts[which]
    else:
        into, apart = outs, range(len(outs))
    rows = into[0].shape[0]
    for out, j in zip(into, apart, strict=True):
        at = pl.ds(aligned(own ^ j, rows), rows)
        out[...] = jnp.dot(
            x_turned[at, :], values[...], preferred_element_type=f32
        ).astype(out.dtype)


def out_kernel(heads, first, soft, values, *refs):
    wo, keep, *send = refs
    blocks, keys, lanes = soft.shape
    queries = lanes // heads
    width = values.shape[1]
    head = lax.broadcasted_iota(jnp.int32, (queries, width), 1) // (width // heads)
    for i in (first, first + 1):
        b = member_of() ^ i
        stacked = lax.dot_general(
            soft[b],
            values[pl.ds(aligned(b, queries), keys), :],
            TN,
            preferred_element_type=f32,
        )
        attended = stacked[:queries]
        for h in range(1, heads):
            attended = jnp.where(head == h, stacked[h * queries : (h + 1) * queries], attended)
        projected = jnp.dot(attended.astype(bf16), wo[...], preferred_element_type=f32)
        if i == first:
            keep[...] = projected
        else:
            start = 0
            for into in send:
                into[...] = projected[start : start + into.shape[0]].astype(into.dtype)
                start += into.shape[0]


def onward_kernel(keep, *refs):
    pieces, onward = refs[:-1], refs[-1]
    start = 0
    for piece in pieces:
        part = slice(start, start + piece.shape[0])
        onward[part, :] = (keep[part, :] + piece[...].astype(f32)).astype(bf16)
        start += piece.shape[0]


def finish_kernel(frame_count, lengths, frames, keep, back, *refs):
    pieces, frames_out, memory_out = refs[:-2], refs[-2], refs[-1]
    segs = memory_out.shape[0]
    count = frames.shape[0]
    near = jnp.concatenate([piece[...].astype(f32) for piece in pieces], axis=0)
    projected = keep[...] + near + back[...].astype(f32)
    first = lax.axis_index("seg") * segs

    def live(array, step):
        at = lax.broadcasted_iota(jnp.int32, array.shape, 0) // step
        return jnp.where(first + at < lengths[0], array, 0.0)

    frames_out[...] = (
        frames[...].astype(f32) + live(projected[:count], frame_count)
    ).astype(bf16)
    memory_out[...] = live(projected[count + segs :], 1).astype(bf16)


def columns_kernel(apart, *refs):
    count = len(apart)
    blocks, (out, wide, sems) = refs[:count], refs[-3:]
    width = blocks[0].shape[1]
    copies = []
    for i, block in enumerate(blocks):
        wide[i] = block[...].astype(f32)
        at = pl.ds(aligned(member_of() ^ apart[i], width), width)
        copies.append(pltpu.make_async_copy(wide.at[i], out.at[:, at], sems.at[i]))
        copies[-1].start()
    for copy in copies:
        copy.wait()


def gathered(piece):
    size = lax.axis_size("fsdp")
    pieces = {0: piece}
    bit = 1
    while bit < size:
        for have in sorted(pieces):
            pieces[have ^ bit] = swapped(pieces[have], "fsdp", bit)
        bit *= 2
    return [pieces[j] for j in range(size)]


def pairs(seg_size):
    straight, turned, first, last = [], [], [], []
    for s in range(seg_size):
        along = 2 if s & 1 else 1
        for f in range(GROUP):
            straight.append((s * GROUP + f, s * GROUP + (f ^ along)))
            turned.append((s * GROUP + f, s * GROUP + (f ^ along ^ 3)))
        k = s % GROUP
        first.append((s * GROUP + k, s * GROUP + (k ^ 1)))
        first.append(((s ^ 1) * GROUP + k, s * GROUP + (k ^ 2)))
        first.append(((s ^ 3) * GROUP + k, (s ^ 3) * GROUP + (k ^ 3)))
        last.append(((s ^ 3) * GROUP + (k ^ 3), s * GROUP + (k ^ 3)))
    return straight, turned, first, last


def on_device(
    frames, memory_in, lengths, ln_gain, w_query, w_key, w_value, w_out, grad_frames, grad_memory
):
    utterances, segs, frame_count, width = frames.shape
    seg_size = lax.axis_size("seg")
    fsdp_size = lax.axis_size("fsdp")
    group = GROUP
    assert utterances == 1 and segs == MEMORY and frame_count == LEFT and seg_size % group == 0
    heads = HEADS // group
    block = width // group
    rows = w_query.shape[0]
    frame_rows = segs * frame_count
    queries = frame_rows + 2 * segs
    halo_rows = LEFT + 2 * MEMORY
    keys = halo_rows + queries
    all_rows = halo_rows + group * queries
    seg = lax.axis_index("seg")
    member = seg % group

    crossed = fsdp_size == group
    own_blocks, tokens, tail = pl.pallas_call(
        functools.partial(pack_kernel, frame_count),
        in_specs=[hbm] * 8,
        out_specs=[vmem] * 3,
        out_shape=[
            jax.ShapeDtypeStruct((1 + crossed, rows, 3 * block), bf16),
            jax.ShapeDtypeStruct((2 * queries, width), bf16),
            jax.ShapeDtypeStruct((halo_rows, width), bf16),
        ],
        scratch_shapes=[
            pltpu.VMEM((frame_rows, width), bf16),
            pltpu.VMEM((2, segs, width), bf16),
            pltpu.VMEM((1, width), f32),
            pltpu.SemaphoreType.DMA((11,)),
        ],
        compiler_params=params(60),
        name="pack",
    )(
        w_query, w_key, w_value, frames.reshape(frame_rows, width),
        grad_frames.reshape(frame_rows, width), memory_in.reshape(segs, width),
        grad_memory.reshape(segs, width), ln_gain.reshape(1, width),
    )
    w_out, own_blocks = lax.optimization_barrier((w_out, own_blocks))

    far = swapped(tokens, "seg", 2)
    near = swapped(tokens, "seg", 1)
    starts = range(group, seg_size, group)
    halo = [
        lax.ppermute(tail, "seg", [(s - 1, s + ahead) for s in starts]) for ahead in (0, 2)
    ]
    if crossed:
        both = ("seg", "fsdp")
        straight, turned, first, last = pairs(seg_size)
        came = lax.ppermute(own_blocks, both, straight)
        wo_came = lax.ppermute(w_out, both, first)
        came, far, near, halo, wo_came = lax.optimization_barrier(
            (came, far, near, halo, wo_came)
        )
        wo_last = lax.ppermute(wo_came, both, last)
    else:
        came = jnp.concatenate([own_blocks, own_blocks])
        wo_near = lax.dynamic_slice_in_dim(
            lax.all_gather(w_out, "fsdp", axis=0, tiled=True), member * block, block, 0
        )
    mine, mine_values, other, far, far_grads = pl.pallas_call(
        split_kernel,
        in_specs=[vmem] * 4,
        out_specs=[vmem] * 5,
        out_shape=[jax.ShapeDtypeStruct((rows, 2 * block), bf16)]
        + [jax.ShapeDtypeStruct((rows, block), bf16)]
        + [jax.ShapeDtypeStruct(came.shape[1:], bf16)]
        + [
            jax.ShapeDtypeStruct((queries + halo_rows, width), bf16),
            jax.ShapeDtypeStruct((queries, width), bf16),
        ],
        compiler_params=params(),
        name="split",
    )(came, far, *halo)
    if crossed:
        other = swapped(other, "seg", 1)
        forwarded = lax.ppermute(mine, both, turned)
        wo_near = pl.pallas_call(
            pick_kernel,
            in_specs=[vmem] * 2,
            out_specs=vmem,
            out_shape=jax.ShapeDtypeStruct((block, width), bf16),
            compiler_params=params(),
            name="pick",
        )(w_out, wo_came)
    else:
        wqkv_parts = gathered(own_blocks)
    parts = [tokens, near, far, far_grads, swapped(far, "seg", 1), swapped(far_grads, "seg", 1)]

    x_all, x_turned, u_all = pl.pallas_call(
        merge_kernel,
        in_specs=[vmem] * len(parts),
        out_specs=[vmem] * 3,
        out_shape=[
            jax.ShapeDtypeStruct((all_rows, width), bf16),
            jax.ShapeDtypeStruct((width, all_rows), bf16),
            jax.ShapeDtypeStruct((group * queries, width), bf16),
        ],
        compiler_params=params(),
        name="merge",
    )(*parts)
    x_all, wo_near, mine_values = lax.optimization_barrier((x_all, wo_near, mine_values))
    if crossed:
        forwarded_values = lax.ppermute(mine_values, both, turned)

    back = pl.pallas_call(
        back_kernel,
        in_specs=[vmem] * 2,
        out_specs=vmem,
        out_shape=jax.ShapeDtypeStruct((group * queries, block), f32),
        compiler_params=params(),
        name="back",
    )(u_all, wo_near)
    bias = pl.pallas_call(
        functools.partial(mask_kernel, heads, frame_count, segs, group),
        out_specs=vmem,
        out_shape=jax.ShapeDtypeStruct((2, keys, heads * queries), f32),
        compiler_params=params(),
        name="mask",
    )()
    back, bias, x_all = lax.optimization_barrier((back, bias, x_all))
    soft_shape = jax.ShapeDtypeStruct((group, keys, heads * queries), bf16)
    values_shape = jax.ShapeDtypeStruct((all_rows, block), bf16)
    if crossed:
        early, early_values = pl.pallas_call(
            early_kernel,
            in_specs=[vmem] * 5,
            out_specs=[vmem] * 2,
            out_shape=[
                jax.ShapeDtypeStruct((all_rows, 2 * block), f32),
                jax.ShapeDtypeStruct((all_rows, block), f32),
            ],
            compiler_params=params(),
            name="early",
        )(x_all, own_blocks, mine, mine_values, other)
        wqkv_parts = [early, forwarded]
    soft, *values = pl.pallas_call(
        functools.partial(weights_kernel, heads, crossed),
        in_specs=[vmem] * (2 + len(wqkv_parts)),
        out_specs=[vmem] * (2 - crossed),
        out_shape=[soft_shape] + [values_shape] * (1 - crossed),
        scratch_shapes=[] if crossed else [pltpu.VMEM((width, 3 * block), bf16)],
        compiler_params=params(),
        name="soft_weights",
    )(x_all, bias, *wqkv_parts)
    if crossed:
        values = pl.pallas_call(
            values_kernel,
            in_specs=[vmem] * 3,
            out_specs=vmem,
            out_shape=values_shape,
            compiler_params=params(),
            name="values",
        )(x_all, early_values, forwarded_values)
    else:
        (values,) = values

    values_grad_shape = jax.ShapeDtypeStruct((all_rows, block), bf16)
    wo_from = [wo_near] + ([wo_last] if crossed else [])
    sent_shape = [jax.ShapeDtypeStruct((2, rows, block), bf16)] * crossed
    wo_mine, values_grad, *sent = pl.pallas_call(
        functools.partial(grad_kernel, heads, frame_count, segs, crossed),
        in_specs=[smem] + [vmem] * (4 + len(wo_from)),
        out_specs=[vmem] * (2 + crossed),
        out_shape=[jax.ShapeDtypeStruct((block, width), bf16), values_grad_shape] + sent_shape,
        scratch_shapes=[
            pltpu.VMEM((all_rows, block), f32),
            pltpu.VMEM((group * queries, block), f32),
        ],
        compiler_params=params(),
        name="values_grad",
    )(lengths, u_all, soft, x_turned, back, *wo_from)

    def grad_rows(which, shapes):
        return pl.pallas_call(
            functools.partial(rows_kernel, which),
            in_specs=[vmem] * 2,
            out_specs=[vmem] * len(shapes),
            out_shape=shapes,
            compiler_params=params(),
            name="grad_rows_" + which,
        )(x_turned, values_grad)

    if crossed:
        (sent,) = sent
        (kept,) = grad_rows("kept", [jax.ShapeDtypeStruct((2, rows, block), f32)])
    else:
        grad_chunks = grad_rows(
            "all", [jax.ShapeDtypeStruct((rows, block), bf16)] * fsdp_size
        )

    def attend(start, name, pieces):
        cut = queries // pieces // 16 * 16
        sizes = [cut] * (pieces - 1) + [queries - cut * (pieces - 1)]
        keep, *send = pl.pallas_call(
            functools.partial(out_kernel, heads, start),
            in_specs=[vmem] * 3,
            out_specs=[vmem] * (1 + pieces),
            out_shape=[jax.ShapeDtypeStruct((queries, width), f32)]
            + [jax.ShapeDtypeStruct((size, width), bf16) for size in sizes],
            compiler_params=params(),
            name=name,
        )(soft, values, wo_mine)
        return keep, send

    keep_far, send_far = attend(2, "attend_far", PIECES)
    keep, send = attend(0, "attend_near", 1)
    near = [swapped(piece, "seg", 1) for piece in send]
    near_far = [swapped(piece, "seg", 1) for piece in send_far]
    onward = pl.pallas_call(
        onward_kernel,
        in_specs=[vmem] * (1 + PIECES),
        out_specs=vmem,
        out_shape=jax.ShapeDtypeStruct((queries, width), bf16),
        compiler_params=params(),
        name="onward",
    )(keep_far, *near_far)
    if crossed:
        came = lax.ppermute(sent, both, straight)
        passing = (kept[1] + came[1].astype(f32)).astype(bf16)
        passing, onward = lax.optimization_barrier((passing, onward))
        last = lax.ppermute(passing, both, turned)
        grad_sum = kept[0] + came[0].astype(f32) + last.astype(f32)
    else:
        grad_sum = grad_chunks[0].astype(f32)
        for j in range(1, fsdp_size):
            grad_sum = grad_sum + swapped(grad_chunks[j], "fsdp", j).astype(f32)
    back = swapped(onward, "seg", 2)
    back = swapped(onward, "seg", 2)
    bit = group
    while bit < seg_size:
        mine = grad_sum.astype(bf16)
        other, back = lax.optimization_barrier((swapped(mine, "seg", bit), back))
        grad_sum = mine.astype(f32) + other.astype(f32)
        bit *= 2
    mine = grad_sum.astype(bf16)
    frames_out, memory_out = pl.pallas_call(
        functools.partial(finish_kernel, frame_count),
        in_specs=[smem] + [vmem] * 4,
        out_specs=[vmem] * 2,
        out_shape=[
            jax.ShapeDtypeStruct((frame_rows, width), bf16),
            jax.ShapeDtypeStruct((segs, width), bf16),
        ],
        compiler_params=params(),
        name="finish",
    )(lengths, frames.reshape(frame_rows, width), keep, back, *near)
    far, frames_out, memory_out = lax.optimization_barrier(
        (swapped(mine, "seg", 2), frames_out, memory_out)
    )

    def columns(apart, blocks, *onto):
        count = len(blocks)
        return pl.pallas_call(
            functools.partial(columns_kernel, apart),
            in_specs=[vmem] * count + [hbm] * len(onto),
            out_specs=hbm,
            out_shape=jax.ShapeDtypeStruct((rows, width), f32),
            scratch_shapes=[
                pltpu.VMEM((count, rows, block), f32),
                pltpu.SemaphoreType.DMA((count,)),
            ],
            input_output_aliases={count: 0} if onto else {},
            compiler_params=params(),
            name="columns" + "_rest" * len(onto),
        )(*blocks, *onto)

    begun = columns((0, 2, 1), (mine, far, swapped(mine, "seg", 1)))
    value_grad = columns((3,), (swapped(far, "seg", 1),), begun)
    frames_out = frames_out.reshape(frames.shape)
    memory_out = memory_out.reshape(memory_in.shape)
    return (frames_out, memory_out, value_grad)


def solution(mesh):
    return jax.shard_map(
        on_device,
        mesh=mesh,
        in_specs=(
            P("fsdp", "seg", None, None),
            P("fsdp", "seg", None),
            P("fsdp"),
            P(),
            P("fsdp", None),
            P("fsdp", None),
            P("fsdp", None),
            P("fsdp", None),
            P("fsdp", "seg", None, None),
            P("fsdp", "seg", None),
        ),
        out_specs=(P("fsdp", "seg", None, None), P("fsdp", "seg", None), P("fsdp", None)),
        check_vma=False,
    )
```

```python
import functools
import math

import jax
import jax.numpy as jnp
from jax import lax
from jax.experimental import pallas as pl
from jax.experimental.pallas import tpu as pltpu
from jax.sharding import PartitionSpec as P

HEADS = 16
LEFT = 16
MEMORY = 8
GROUP = 4
PIECES = 2


epsilon = 1e-05
masked_score = -1e30
bf16 = jnp.bfloat16
f32 = jnp.float32
vmem = pl.BlockSpec(memory_space=pltpu.VMEM)
smem = pl.BlockSpec(memory_space=pltpu.SMEM)
hbm = pl.BlockSpec(memory_space=pltpu.HBM)
NT = (((1,), (1,)), ((), ()))
TN = (((0,), (0,)), ((), ()))


def params(mib=40):
    return pltpu.CompilerParams(vmem_limit_bytes=mib * 1024 * 1024)


def swapped(array, axis, bit):
    size = lax.axis_size(axis)
    return lax.ppermute(array, axis, [(i, i ^ bit) for i in range(size)])


def halving_bits(size):
    return [1 << b for b in range(size.bit_length() - 1)]


def member_of():
    return lax.axis_index("seg") % GROUP


def aligned(start, step):
    return pl.multiple_of(start * step, step)


def normed_rows(rows, gain):
    wide = rows.astype(f32)
    centred = wide - jnp.mean(wide, axis=-1, keepdims=True)
    var = jnp.mean(centred * centred, axis=-1, keepdims=True)
    return (centred * lax.rsqrt(var + epsilon) * gain).astype(bf16)


def pack_kernel(frame_count, wq, wk, wv, frames, gf, mem, gm, gain, *refs):
    blocks, tokens, tail, raw, few, one, sems = refs
    width = blocks.shape[2] // 3
    rows, model_width = gf.shape
    segs = mem.shape[0]
    half = tokens.shape[0] // 2
    copies = [
        pltpu.make_async_copy(frames, raw, sems.at[0]),
        pltpu.make_async_copy(gain, one, sems.at[1]),
        pltpu.make_async_copy(mem, few.at[0], sems.at[2]),
        pltpu.make_async_copy(gm, few.at[1], sems.at[3]),
        pltpu.make_async_copy(gf, tokens.at[pl.ds(half, rows)], sems.at[4]),
    ]
    for i in range(blocks.shape[0]):
        at = aligned(member_of() ^ i, width)
        for j, w in enumerate((wq, wk, wv)):
            into = blocks.at[i, :, pl.ds(j * width, width)]
            sem = sems.at[5 + 3 * i + j]
            copies.append(pltpu.make_async_copy(w.at[:, pl.ds(at, width)], into, sem))
    for copy in copies:
        copy.start()
    for copy in copies[:4]:
        copy.wait()
    normed = normed_rows(raw[...], one[...])
    tokens[:rows, :] = normed
    summary = jnp.sum(normed.astype(f32).reshape(segs, frame_count, model_width), axis=1)
    tokens[rows:half, :] = jnp.concatenate(
        [few[0], (summary / frame_count).astype(bf16)], axis=0
    )
    tokens[half + rows :, :] = jnp.concatenate([jnp.zeros_like(few[1]), few[1]], axis=0)
    tail[...] = tokens[half - tail.shape[0] : half, :]
    for copy in copies[4:]:
        copy.wait()


def split_kernel(both, far, halo_first, halo_third, mine, mine_values, other, far_tokens, far_grads):
    width = mine.shape[1]
    mine[...] = both[0, :, :width]
    mine_values[...] = both[0, :, width:]
    other[...] = both[1]
    half = far_grads.shape[0]
    far_tokens[:half, :] = far[:half, :]
    far_tokens[half:, :] = jnp.where(member_of() == 0, halo_first[...], halo_third[...])
    far_grads[...] = far[half:, :]


def merge_kernel(tokens, near, far, far_grads, last, last_grads, x_all, x_turned, u_all):
    half = far_grads.shape[0]
    parts = [
        (tokens[:half, :], tokens[half:, :]),
        (near[:half, :], near[half:, :]),
        (far[:half, :], far_grads[...]),
        (last[:half, :], last_grads[...]),
    ]
    halo = far.shape[0] - half
    odd = (member_of() & 1) > 0
    x_all[:halo, :] = jnp.where(odd, last[half:, :], far[half:, :])
    for i, (x_part, u_part) in enumerate(parts):
        at = aligned(member_of() ^ i, half)
        x_all[pl.ds(pl.multiple_of(halo + at, 16), half), :] = x_part
        u_all[pl.ds(at, half), :] = u_part
    x_turned[...] = x_all[...].T


def pick_kernel(own, came, wo):
    wo[...] = jnp.where(lax.axis_index("fsdp") == member_of(), own[...], came[...])


def assemble(pieces, whole):
    own = lax.axis_index("fsdp")
    rows = pieces[0].shape[-2]
    for j, piece in enumerate(pieces):
        into = whole.at[pl.ds(aligned(own ^ j, rows), rows), :]
        into[...] = piece[0] if len(piece.shape) == 3 else piece[...]


def head_stack(array, heads):
    width = array.shape[1]
    head = lax.broadcasted_iota(jnp.int32, array.shape, 1) // (width // heads)
    zero = jnp.zeros_like(array)
    return jnp.concatenate([jnp.where(head == h, array, zero) for h in range(heads)], axis=0)


def early_kernel(x_all, mine, beside, swapped_in, total):
    own = lax.axis_index("fsdp")
    along = 2 - (lax.axis_index("seg") & 1)
    rows, width = beside.shape
    product = 0.0
    for j, piece in ((0, mine.at[0]), (along, beside), (along ^ 3, swapped_in)):
        columns = x_all[:, pl.ds(aligned(own ^ j, rows), rows)]
        product = product + jnp.dot(columns, piece[:, :width], preferred_element_type=f32)
    total[...] = product


def values_kernel(x_all, mine, beside, swapped_in, across, values):
    own = lax.axis_index("fsdp")
    along = 2 - (lax.axis_index("seg") & 1)
    rows, width = beside.shape
    total = 0.0
    for j, piece in ((0, mine.at[0]), (along, beside), (along ^ 3, swapped_in), (3, across)):
        columns = x_all[:, pl.ds(aligned(own ^ j, rows), rows)]
        start = piece.shape[1] - width
        total = total + jnp.dot(columns, piece[:, start:], preferred_element_type=f32)
    values[...] = total.astype(bf16)


def weights_kernel(heads, crossed, x_all, bias, *refs):
    if crossed:
        total, last, soft = refs
        rows = last.shape[0]
        at = aligned(lax.axis_index("fsdp") ^ 3, rows)
        product = total[...] + jnp.dot(
            x_all[:, pl.ds(at, rows)], last[...], preferred_element_type=f32
        )
    else:
        soft, values, whole = refs[-3:]
        assemble(refs[:-3], whole)
        product = jnp.dot(x_all[...], whole[...], preferred_element_type=f32)
    projected = product.astype(bf16)
    blocks, keys, lanes = soft.shape
    queries = lanes // heads
    halo = keys - queries
    block = projected.shape[1] // (2 if crossed else 3)
    q_all, k_all = projected[:, :block], projected[:, block : 2 * block]
    if not crossed:
        values[...] = projected[:, 2 * block :]
    scale = 1.0 / math.sqrt(block // heads)
    for b in range(blocks):
        start = b * queries
        q_b = head_stack(q_all[halo + start : halo + start + queries], heads)
        scores = (
            lax.dot_general(k_all[start : start + keys], q_b, NT, preferred_element_type=f32)
            * scale
            + bias[min(b, 1)]
        )
        exponent = jnp.exp(scores - jnp.max(scores, axis=0, keepdims=True))
        inverse = 1.0 / jnp.sum(exponent, axis=0, keepdims=True)
        soft[b] = (exponent * inverse).astype(bf16)


def mask_kernel(heads, frame_count, segs, group, bias):
    _, keys, lanes = bias.shape
    queries = lanes // heads
    halo = keys - queries
    frames = segs * frame_count
    key = lax.broadcasted_iota(jnp.int32, (keys, lanes), 0)
    row = lax.broadcasted_iota(jnp.int32, (keys, lanes), 1)
    for h in range(1, heads):
        row = jnp.where(row >= queries, row - queries, row)
    at = jnp.where(row < frames, row // frame_count, jnp.maximum(row - frames - segs, 0))
    own = key - halo
    own_seg = own // frame_count
    own_mem = own - frames
    valid_own = ((own >= 0) & (own < frames) & ((own_seg == at) | (own_seg == at - 1))) | (
        (own_mem >= 0) & (own_mem < segs) & (own_mem < at) & (own_mem >= at - MEMORY)
    )
    halo_mem = key - LEFT
    valid_halo = ((key < LEFT) & (at == 0)) | (
        (halo_mem >= 0) & (halo_mem < MEMORY) & (halo_mem >= at)
    )
    inside = lax.axis_index("seg") >= group
    bias[0] = jnp.where(valid_own | (valid_halo & inside), 0.0, masked_score)
    bias[1] = jnp.where(valid_own | valid_halo, 0.0, masked_score)


def back_kernel(u_all, wo, back):
    back[...] = lax.dot_general(u_all[...], wo[...], NT, preferred_element_type=f32)


def grad_kernel(heads, frame_count, segs, crossed, lengths, u_all, soft, x_turned, early, *refs):
    outputs = 4 + crossed
    wo_from, (wo, values, *sent, total, back) = refs[:-outputs], refs[-outputs:]
    blocks, keys, lanes = soft.shape
    queries = lanes // heads
    frames = segs * frame_count

    def here():
        wo[...] = wo_from[0][...]
        back[...] = early[...]

    def late():
        wo[...] = wo_from[1][...]
        back[...] = lax.dot_general(u_all[...], wo[...], NT, preferred_element_type=f32)

    if len(wo_from) > 1:
        opposite = (lax.axis_index("fsdp") ^ member_of()) == 3
        pl.when(opposite)(late)
        pl.when(jnp.logical_not(opposite))(here)
    else:
        here()
    row = lax.broadcasted_iota(jnp.int32, (queries, wo.shape[0]), 0)
    seg_of = jnp.where(row < frames, row // frame_count, row - frames - segs)
    first = lax.axis_index("seg") - member_of()
    split = keys - queries
    total[:split, :] = jnp.zeros((split, total.shape[1]), f32)
    for b in range(blocks):
        start = b * queries
        live = ((first + b) * segs + seg_of < lengths[0]).astype(f32)
        grad_attended = head_stack((live * back[start : start + queries]).astype(bf16), heads)
        term = jnp.dot(soft[b], grad_attended, preferred_element_type=f32)
        total[start : start + split, :] += term[:split]
        total[start + split : start + keys, :] = term[split:]
    values[...] = total[...].astype(bf16)
    if crossed:
        rows_kernel("sent", x_turned, values, *sent)


def rows_kernel(which, x_turned, values, *outs):
    own = lax.axis_index("fsdp")
    along = 2 - (lax.axis_index("seg") & 1)
    parts = {"kept": (0, along ^ 3), "sent": (along, 3)}
    if which in parts:
        into = [outs[0].at[i] for i in range(2)]
        apart = parts[which]
    else:
        into, apart = outs, range(len(outs))
    rows = into[0].shape[0]
    for out, j in zip(into, apart, strict=True):
        at = pl.ds(aligned(own ^ j, rows), rows)
        out[...] = jnp.dot(
            x_turned[at, :], values[...], preferred_element_type=f32
        ).astype(out.dtype)


def out_kernel(heads, first, soft, values, *refs):
    wo, keep, *send = refs
    blocks, keys, lanes = soft.shape
    queries = lanes // heads
    width = values.shape[1]
    head = lax.broadcasted_iota(jnp.int32, (queries, width), 1) // (width // heads)
    for i in (first, first + 1):
        b = member_of() ^ i
        stacked = lax.dot_general(
            soft[b],
            values[pl.ds(aligned(b, queries), keys), :],
            TN,
            preferred_element_type=f32,
        )
        attended = stacked[:queries]
        for h in range(1, heads):
            attended = jnp.where(head == h, stacked[h * queries : (h + 1) * queries], attended)
        projected = jnp.dot(attended.astype(bf16), wo[...], preferred_element_type=f32)
        if i == first:
            keep[...] = projected
        else:
            start = 0
            for into in send:
                into[...] = projected[start : start + into.shape[0]].astype(into.dtype)
                start += into.shape[0]


def onward_kernel(keep, *refs):
    pieces, onward = refs[:-1], refs[-1]
    start = 0
    for piece in pieces:
        part = slice(start, start + piece.shape[0])
        onward[part, :] = (keep[part, :] + piece[...].astype(f32)).astype(bf16)
        start += piece.shape[0]


def finish_kernel(frame_count, lengths, frames, keep, back, *refs):
    pieces, frames_out, memory_out = refs[:-2], refs[-2], refs[-1]
    segs = memory_out.shape[0]
    count = frames.shape[0]
    near = jnp.concatenate([piece[...].astype(f32) for piece in pieces], axis=0)
    projected = keep[...] + near + back[...].astype(f32)
    first = lax.axis_index("seg") * segs

    def live(array, step):
        at = lax.broadcasted_iota(jnp.int32, array.shape, 0) // step
        return jnp.where(first + at < lengths[0], array, 0.0)

    frames_out[...] = (
        frames[...].astype(f32) + live(projected[:count], frame_count)
    ).astype(bf16)
    memory_out[...] = live(projected[count + segs :], 1).astype(bf16)


def columns_kernel(apart, *refs):
    count = len(apart)
    blocks, (out, wide, sems) = refs[:count], refs[-3:]
    width = blocks[0].shape[1]
    copies = []
    for i, block in enumerate(blocks):
        wide[i] = block[...].astype(f32)
        at = pl.ds(aligned(member_of() ^ apart[i], width), width)
        copies.append(pltpu.make_async_copy(wide.at[i], out.at[:, at], sems.at[i]))
        copies[-1].start()
    for copy in copies:
        copy.wait()


def gathered(piece):
    size = lax.axis_size("fsdp")
    pieces = {0: piece}
    bit = 1
    while bit < size:
        for have in sorted(pieces):
            pieces[have ^ bit] = swapped(pieces[have], "fsdp", bit)
        bit *= 2
    return [pieces[j] for j in range(size)]


def pairs(seg_size):
    straight, turned, first, last = [], [], [], []
    for s in range(seg_size):
        along = 1 if s & 1 else 2
        for f in range(GROUP):
            straight.append((s * GROUP + f, s * GROUP + (f ^ along)))
            turned.append((s * GROUP + f, s * GROUP + (f ^ along ^ 3)))
        k = s % GROUP
        first.append((s * GROUP + k, s * GROUP + (k ^ 1)))
        first.append(((s ^ 1) * GROUP + k, s * GROUP + (k ^ 2)))
        first.append(((s ^ 3) * GROUP + k, (s ^ 3) * GROUP + (k ^ 3)))
        last.append(((s ^ 3) * GROUP + (k ^ 3), s * GROUP + (k ^ 3)))
    return straight, turned, first, last


def on_device(
    frames, memory_in, lengths, ln_gain, w_query, w_key, w_value, w_out, grad_frames, grad_memory
):
    utterances, segs, frame_count, width = frames.shape
    seg_size = lax.axis_size("seg")
    fsdp_size = lax.axis_size("fsdp")
    group = GROUP
    assert utterances == 1 and segs == MEMORY and frame_count == LEFT and seg_size % group == 0
    heads = HEADS // group
    block = width // group
    rows = w_query.shape[0]
    frame_rows = segs * frame_count
    queries = frame_rows + 2 * segs
    halo_rows = LEFT + 2 * MEMORY
    keys = halo_rows + queries
    all_rows = halo_rows + group * queries
    seg = lax.axis_index("seg")
    member = seg % group

    crossed = fsdp_size == group
    own_blocks, tokens, tail = pl.pallas_call(
        functools.partial(pack_kernel, frame_count),
        in_specs=[hbm] * 8,
        out_specs=[vmem] * 3,
        out_shape=[
            jax.ShapeDtypeStruct((1 + crossed, rows, 3 * block), bf16),
            jax.ShapeDtypeStruct((2 * queries, width), bf16),
            jax.ShapeDtypeStruct((halo_rows, width), bf16),
        ],
        scratch_shapes=[
            pltpu.VMEM((frame_rows, width), bf16),
            pltpu.VMEM((2, segs, width), bf16),
            pltpu.VMEM((1, width), f32),
            pltpu.SemaphoreType.DMA((11,)),
        ],
        compiler_params=params(60),
        name="pack",
    )(
        w_query, w_key, w_value, frames.reshape(frame_rows, width),
        grad_frames.reshape(frame_rows, width), memory_in.reshape(segs, width),
        grad_memory.reshape(segs, width), ln_gain.reshape(1, width),
    )
    w_out, own_blocks = lax.optimization_barrier((w_out, own_blocks))

    far = swapped(tokens, "seg", 2)
    near = swapped(tokens, "seg", 1)
    starts = range(group, seg_size, group)
    halo = [
        lax.ppermute(tail, "seg", [(s - 1, s + ahead) for s in starts]) for ahead in (0, 2)
    ]
    bias = pl.pallas_call(
        functools.partial(mask_kernel, heads, frame_count, segs, group),
        out_specs=vmem,
        out_shape=jax.ShapeDtypeStruct((2, keys, heads * queries), f32),
        compiler_params=params(),
        name="mask",
    )()
    if crossed:
        both = ("seg", "fsdp")
        straight, turned, first, last = pairs(seg_size)
        came = lax.ppermute(own_blocks, both, straight)
        wo_came = lax.ppermute(w_out, both, first)
        came, far, near, halo, wo_came, bias = lax.optimization_barrier(
            (came, far, near, halo, wo_came, bias)
        )
        wo_last = lax.ppermute(wo_came, both, last)
    else:
        came = jnp.concatenate([own_blocks, own_blocks])
        wo_near = lax.dynamic_slice_in_dim(
            lax.all_gather(w_out, "fsdp", axis=0, tiled=True), member * block, block, 0
        )
    mine, mine_values, other, far, far_grads = pl.pallas_call(
        split_kernel,
        in_specs=[vmem] * 4,
        out_specs=[vmem] * 5,
        out_shape=[jax.ShapeDtypeStruct((rows, 2 * block), bf16)]
        + [jax.ShapeDtypeStruct((rows, block), bf16)]
        + [jax.ShapeDtypeStruct(came.shape[1:], bf16)]
        + [
            jax.ShapeDtypeStruct((queries + halo_rows, width), bf16),
            jax.ShapeDtypeStruct((queries, width), bf16),
        ],
        compiler_params=params(),
        name="split",
    )(came, far, *halo)
    if crossed:
        other = swapped(other, "seg", 1)
        forwarded = lax.ppermute(mine, both, turned)
        wo_near = pl.pallas_call(
            pick_kernel,
            in_specs=[vmem] * 2,
            out_specs=vmem,
            out_shape=jax.ShapeDtypeStruct((block, width), bf16),
            compiler_params=params(),
            name="pick",
        )(w_out, wo_came)
    else:
        wqkv_parts = gathered(own_blocks)
    parts = [tokens, near, far, far_grads, swapped(far, "seg", 1), swapped(far_grads, "seg", 1)]

    x_all, x_turned, u_all = pl.pallas_call(
        merge_kernel,
        in_specs=[vmem] * len(parts),
        out_specs=[vmem] * 3,
        out_shape=[
            jax.ShapeDtypeStruct((all_rows, width), bf16),
            jax.ShapeDtypeStruct((width, all_rows), bf16),
            jax.ShapeDtypeStruct((group * queries, width), bf16),
        ],
        compiler_params=params(),
        name="merge",
    )(*parts)
    x_all, wo_near = lax.optimization_barrier((x_all, wo_near))

    back = pl.pallas_call(
        back_kernel,
        in_specs=[vmem] * 2,
        out_specs=vmem,
        out_shape=jax.ShapeDtypeStruct((group * queries, block), f32),
        compiler_params=params(),
        name="back",
    )(u_all, wo_near)
    back, x_all = lax.optimization_barrier((back, x_all))
    soft_shape = jax.ShapeDtypeStruct((group, keys, heads * queries), bf16)
    values_shape = jax.ShapeDtypeStruct((all_rows, block), bf16)
    if crossed:
        early = pl.pallas_call(
            early_kernel,
            in_specs=[vmem] * 4,
            out_specs=vmem,
            out_shape=jax.ShapeDtypeStruct((all_rows, 2 * block), f32),
            compiler_params=params(),
            name="early",
        )(x_all, own_blocks, mine, other)
        early, waiting = lax.optimization_barrier((early, mine_values))
        forwarded_values = lax.ppermute(waiting, both, turned)
        wqkv_parts = [early, forwarded]
    soft, *values = pl.pallas_call(
        functools.partial(weights_kernel, heads, crossed),
        in_specs=[vmem] * (2 + len(wqkv_parts)),
        out_specs=[vmem] * (2 - crossed),
        out_shape=[soft_shape] + [values_shape] * (1 - crossed),
        scratch_shapes=[] if crossed else [pltpu.VMEM((width, 3 * block), bf16)],
        compiler_params=params(),
        name="soft_weights",
    )(x_all, bias, *wqkv_parts)
    if crossed:
        values = pl.pallas_call(
            values_kernel,
            in_specs=[vmem] * 5,
            out_specs=vmem,
            out_shape=values_shape,
            compiler_params=params(),
            name="values",
        )(x_all, own_blocks, mine_values, other, forwarded_values)
    else:
        (values,) = values

    values_grad_shape = jax.ShapeDtypeStruct((all_rows, block), bf16)
    wo_from = [wo_near] + ([wo_last] if crossed else [])
    sent_shape = [jax.ShapeDtypeStruct((2, rows, block), bf16)] * crossed
    wo_mine, values_grad, *sent = pl.pallas_call(
        functools.partial(grad_kernel, heads, frame_count, segs, crossed),
        in_specs=[smem] + [vmem] * (4 + len(wo_from)),
        out_specs=[vmem] * (2 + crossed),
        out_shape=[jax.ShapeDtypeStruct((block, width), bf16), values_grad_shape] + sent_shape,
        scratch_shapes=[
            pltpu.VMEM((all_rows, block), f32),
            pltpu.VMEM((group * queries, block), f32),
        ],
        compiler_params=params(),
        name="values_grad",
    )(lengths, u_all, soft, x_turned, back, *wo_from)

    def grad_rows(which, shapes):
        return pl.pallas_call(
            functools.partial(rows_kernel, which),
            in_specs=[vmem] * 2,
            out_specs=[vmem] * len(shapes),
            out_shape=shapes,
            compiler_params=params(),
            name="grad_rows_" + which,
        )(x_turned, values_grad)

    if crossed:
        (sent,) = sent
        (kept,) = grad_rows("kept", [jax.ShapeDtypeStruct((2, rows, block), f32)])
    else:
        grad_chunks = grad_rows(
            "all", [jax.ShapeDtypeStruct((rows, block), bf16)] * fsdp_size
        )

    def attend(start, name, pieces):
        cut = queries // pieces // 16 * 16
        sizes = [cut] * (pieces - 1) + [queries - cut * (pieces - 1)]
        keep, *send = pl.pallas_call(
            functools.partial(out_kernel, heads, start),
            in_specs=[vmem] * 3,
            out_specs=[vmem] * (1 + pieces),
            out_shape=[jax.ShapeDtypeStruct((queries, width), f32)]
            + [jax.ShapeDtypeStruct((size, width), bf16) for size in sizes],
            compiler_params=params(),
            name=name,
        )(soft, values, wo_mine)
        return keep, send

    keep_far, send_far = attend(2, "attend_far", PIECES)
    keep, send = attend(0, "attend_near", 1)
    near = [swapped(piece, "seg", 1) for piece in send]
    near_far = [swapped(piece, "seg", 1) for piece in send_far]
    onward = pl.pallas_call(
        onward_kernel,
        in_specs=[vmem] * (1 + PIECES),
        out_specs=vmem,
        out_shape=jax.ShapeDtypeStruct((queries, width), bf16),
        compiler_params=params(),
        name="onward",
    )(keep_far, *near_far)
    if crossed:
        came = lax.ppermute(sent, both, straight)
        passing = (kept[1] + came[1].astype(f32)).astype(bf16)
        passing, onward = lax.optimization_barrier((passing, onward))
        last = lax.ppermute(passing, both, turned)
        grad_sum = kept[0] + came[0].astype(f32) + last.astype(f32)
    else:
        grad_sum = grad_chunks[0].astype(f32)
        for j in range(1, fsdp_size):
            grad_sum = grad_sum + swapped(grad_chunks[j], "fsdp", j).astype(f32)
    returned = swapped(onward, "seg", 2)
    bit = group
    while bit < seg_size:
        mine = grad_sum.astype(bf16)
        other, returned = lax.optimization_barrier((swapped(mine, "seg", bit), returned))
        grad_sum = mine.astype(f32) + other.astype(f32)
        bit *= 2
    mine = grad_sum.astype(bf16)
    frames_out, memory_out = pl.pallas_call(
        functools.partial(finish_kernel, frame_count),
        in_specs=[smem] + [vmem] * 4,
        out_specs=[vmem] * 2,
        out_shape=[
            jax.ShapeDtypeStruct((frame_rows, width), bf16),
            jax.ShapeDtypeStruct((segs, width), bf16),
        ],
        compiler_params=params(),
        name="finish",
    )(lengths, frames.reshape(frame_rows, width), keep, returned, *near)
    far, frames_out, memory_out = lax.optimization_barrier(
        (swapped(mine, "seg", 2), frames_out, memory_out)
    )

    def columns(apart, blocks, *onto):
        count = len(blocks)
        return pl.pallas_call(
            functools.partial(columns_kernel, apart),
            in_specs=[vmem] * count + [hbm] * len(onto),
            out_specs=hbm,
            out_shape=jax.ShapeDtypeStruct((rows, width), f32),
            scratch_shapes=[
                pltpu.VMEM((count, rows, block), f32),
                pltpu.SemaphoreType.DMA((count,)),
            ],
            input_output_aliases={count: 0} if onto else {},
            compiler_params=params(),
            name="columns" + "_rest" * len(onto),
        )(*blocks, *onto)

    begun = columns((0, 2, 1), (mine, far, swapped(mine, "seg", 1)))
    value_grad = columns((3,), (swapped(far, "seg", 1),), begun)
    frames_out = frames_out.reshape(frames.shape)
    memory_out = memory_out.reshape(memory_in.shape)
    return (frames_out, memory_out, value_grad)


def solution(mesh):
    return jax.shard_map(
        on_device,
        mesh=mesh,
        in_specs=(
            P("fsdp", "seg", None, None),
            P("fsdp", "seg", None),
            P("fsdp"),
            P(),
            P("fsdp", None),
            P("fsdp", None),
            P("fsdp", None),
            P("fsdp", None),
            P("fsdp", "seg", None, None),
            P("fsdp", "seg", None),
        ),
        out_specs=(P("fsdp", "seg", None, None), P("fsdp", "seg", None), P("fsdp", None)),
        check_vma=False,
    )
```

```python
import functools
import math

import jax
import jax.numpy as jnp
from jax import lax
from jax.experimental import pallas as pl
from jax.experimental.pallas import tpu as pltpu
from jax.sharding import PartitionSpec as P

HEADS = 16
LEFT = 16
MEMORY = 8
GROUP = 4
PIECES = 2


epsilon = 1e-05
masked_score = -1e30
bf16 = jnp.bfloat16
f32 = jnp.float32
vmem = pl.BlockSpec(memory_space=pltpu.VMEM)
smem = pl.BlockSpec(memory_space=pltpu.SMEM)
hbm = pl.BlockSpec(memory_space=pltpu.HBM)
NT = (((1,), (1,)), ((), ()))
TN = (((0,), (0,)), ((), ()))


def params(mib=40):
    return pltpu.CompilerParams(vmem_limit_bytes=mib * 1024 * 1024)


def swapped(array, axis, bit):
    size = lax.axis_size(axis)
    return lax.ppermute(array, axis, [(i, i ^ bit) for i in range(size)])


def halving_bits(size):
    return [1 << b for b in range(size.bit_length() - 1)]


def member_of():
    return lax.axis_index("seg") % GROUP


def aligned(start, step):
    return pl.multiple_of(start * step, step)


def normed_rows(rows, gain):
    wide = rows.astype(f32)
    centred = wide - jnp.mean(wide, axis=-1, keepdims=True)
    var = jnp.mean(centred * centred, axis=-1, keepdims=True)
    return (centred * lax.rsqrt(var + epsilon) * gain).astype(bf16)


def pack_kernel(frame_count, wq, wk, wv, frames, gf, mem, gm, gain, *refs):
    blocks, tokens, tail, raw, few, one, sems = refs
    width = blocks.shape[2] // 3
    rows, model_width = gf.shape
    segs = mem.shape[0]
    half = tokens.shape[0] // 2
    copies = [
        pltpu.make_async_copy(frames, raw, sems.at[0]),
        pltpu.make_async_copy(gain, one, sems.at[1]),
        pltpu.make_async_copy(mem, few.at[0], sems.at[2]),
        pltpu.make_async_copy(gm, few.at[1], sems.at[3]),
        pltpu.make_async_copy(gf, tokens.at[pl.ds(half, rows)], sems.at[4]),
    ]
    for i in range(blocks.shape[0]):
        at = aligned(member_of() ^ i, width)
        for j, w in enumerate((wq, wk, wv)):
            into = blocks.at[i, :, pl.ds(j * width, width)]
            sem = sems.at[5 + 3 * i + j]
            copies.append(pltpu.make_async_copy(w.at[:, pl.ds(at, width)], into, sem))
    for copy in copies:
        copy.start()
    for copy in copies[:4]:
        copy.wait()
    normed = normed_rows(raw[...], one[...])
    tokens[:rows, :] = normed
    summary = jnp.sum(normed.astype(f32).reshape(segs, frame_count, model_width), axis=1)
    tokens[rows:half, :] = jnp.concatenate(
        [few[0], (summary / frame_count).astype(bf16)], axis=0
    )
    tokens[half + rows :, :] = jnp.concatenate([jnp.zeros_like(few[1]), few[1]], axis=0)
    tail[...] = tokens[half - tail.shape[0] : half, :]
    for copy in copies[4:]:
        copy.wait()


def split_kernel(both, far, halo_first, halo_third, mine, mine_values, other, far_tokens, far_grads):
    width = mine.shape[1]
    mine[...] = both[0, :, :width]
    mine_values[...] = both[0, :, width:]
    other[...] = both[1]
    half = far_grads.shape[0]
    far_tokens[:half, :] = far[:half, :]
    far_tokens[half:, :] = jnp.where(member_of() == 0, halo_first[...], halo_third[...])
    far_grads[...] = far[half:, :]


def merge_kernel(tokens, near, far, far_grads, last, last_grads, x_all, x_turned, u_all):
    half = far_grads.shape[0]
    parts = [
        (tokens[:half, :], tokens[half:, :]),
        (near[:half, :], near[half:, :]),
        (far[:half, :], far_grads[...]),
        (last[:half, :], last_grads[...]),
    ]
    halo = far.shape[0] - half
    odd = (member_of() & 1) > 0
    x_all[:halo, :] = jnp.where(odd, last[half:, :], far[half:, :])
    for i, (x_part, u_part) in enumerate(parts):
        at = aligned(member_of() ^ i, half)
        x_all[pl.ds(pl.multiple_of(halo + at, 16), half), :] = x_part
        u_all[pl.ds(at, half), :] = u_part
    x_turned[...] = x_all[...].T


def pick_kernel(own, came, wo):
    wo[...] = jnp.where(lax.axis_index("fsdp") == member_of(), own[...], came[...])


def assemble(pieces, whole):
    own = lax.axis_index("fsdp")
    rows = pieces[0].shape[-2]
    for j, piece in enumerate(pieces):
        into = whole.at[pl.ds(aligned(own ^ j, rows), rows), :]
        into[...] = piece[0] if len(piece.shape) == 3 else piece[...]


def head_stack(array, heads):
    width = array.shape[1]
    head = lax.broadcasted_iota(jnp.int32, array.shape, 1) // (width // heads)
    zero = jnp.zeros_like(array)
    return jnp.concatenate([jnp.where(head == h, array, zero) for h in range(heads)], axis=0)


def early_kernel(x_all, mine, beside, swapped_in, total):
    own = lax.axis_index("fsdp")
    along = 2 - (lax.axis_index("seg") & 1)
    rows, width = beside.shape
    product = 0.0
    for j, piece in ((0, mine.at[0]), (along, beside), (along ^ 3, swapped_in)):
        columns = x_all[:, pl.ds(aligned(own ^ j, rows), rows)]
        product = product + jnp.dot(columns, piece[:, :width], preferred_element_type=f32)
    total[...] = product


def values_kernel(x_all, mine, beside, swapped_in, across, values):
    own = lax.axis_index("fsdp")
    along = 2 - (lax.axis_index("seg") & 1)
    rows, width = beside.shape
    total = 0.0
    for j, piece in ((0, mine.at[0]), (along, beside), (along ^ 3, swapped_in), (3, across)):
        columns = x_all[:, pl.ds(aligned(own ^ j, rows), rows)]
        start = piece.shape[1] - width
        total = total + jnp.dot(columns, piece[:, start:], preferred_element_type=f32)
    values[...] = total.astype(bf16)


def weights_kernel(heads, crossed, x_all, bias, *refs):
    if crossed:
        total, last, soft = refs
        rows = last.shape[0]
        at = aligned(lax.axis_index("fsdp") ^ 3, rows)
        product = total[...] + jnp.dot(
            x_all[:, pl.ds(at, rows)], last[...], preferred_element_type=f32
        )
    else:
        soft, values, whole = refs[-3:]
        assemble(refs[:-3], whole)
        product = jnp.dot(x_all[...], whole[...], preferred_element_type=f32)
    projected = product.astype(bf16)
    blocks, keys, lanes = soft.shape
    queries = lanes // heads
    halo = keys - queries
    block = projected.shape[1] // (2 if crossed else 3)
    q_all, k_all = projected[:, :block], projected[:, block : 2 * block]
    if not crossed:
        values[...] = projected[:, 2 * block :]
    scale = 1.0 / math.sqrt(block // heads)
    for b in range(blocks):
        start = b * queries
        q_b = head_stack(q_all[halo + start : halo + start + queries], heads)
        scores = (
            lax.dot_general(k_all[start : start + keys], q_b, NT, preferred_element_type=f32)
            * scale
            + bias[min(b, 1)]
        )
        exponent = jnp.exp(scores - jnp.max(scores, axis=0, keepdims=True))
        inverse = 1.0 / jnp.sum(exponent, axis=0, keepdims=True)
        soft[b] = (exponent * inverse).astype(bf16)


def mask_kernel(heads, frame_count, segs, group, bias):
    _, keys, lanes = bias.shape
    queries = lanes // heads
    halo = keys - queries
    frames = segs * frame_count
    key = lax.broadcasted_iota(jnp.int32, (keys, lanes), 0)
    row = lax.broadcasted_iota(jnp.int32, (keys, lanes), 1)
    for h in range(1, heads):
        row = jnp.where(row >= queries, row - queries, row)
    at = jnp.where(row < frames, row // frame_count, jnp.maximum(row - frames - segs, 0))
    own = key - halo
    own_seg = own // frame_count
    own_mem = own - frames
    valid_own = ((own >= 0) & (own < frames) & ((own_seg == at) | (own_seg == at - 1))) | (
        (own_mem >= 0) & (own_mem < segs) & (own_mem < at) & (own_mem >= at - MEMORY)
    )
    halo_mem = key - LEFT
    valid_halo = ((key < LEFT) & (at == 0)) | (
        (halo_mem >= 0) & (halo_mem < MEMORY) & (halo_mem >= at)
    )
    inside = lax.axis_index("seg") >= group
    bias[0] = jnp.where(valid_own | (valid_halo & inside), 0.0, masked_score)
    bias[1] = jnp.where(valid_own | valid_halo, 0.0, masked_score)


def back_kernel(crossed, u_all, wo, back):
    def product():
        back[...] = lax.dot_general(u_all[...], wo[...], NT, preferred_element_type=f32)

    if crossed:
        pl.when((lax.axis_index("fsdp") ^ member_of()) != 3)(product)
    else:
        product()


def grad_kernel(heads, frame_count, segs, crossed, lengths, u_all, soft, x_turned, early, *refs):
    outputs = 4 + crossed
    wo_from, (wo, values, *sent, total, back) = refs[:-outputs], refs[-outputs:]
    blocks, keys, lanes = soft.shape
    queries = lanes // heads
    frames = segs * frame_count

    def here():
        wo[...] = wo_from[0][...]
        back[...] = early[...]

    def late():
        wo[...] = wo_from[1][...]
        back[...] = lax.dot_general(u_all[...], wo[...], NT, preferred_element_type=f32)

    if len(wo_from) > 1:
        opposite = (lax.axis_index("fsdp") ^ member_of()) == 3
        pl.when(opposite)(late)
        pl.when(jnp.logical_not(opposite))(here)
    else:
        here()
    row = lax.broadcasted_iota(jnp.int32, (queries, wo.shape[0]), 0)
    seg_of = jnp.where(row < frames, row // frame_count, row - frames - segs)
    first = lax.axis_index("seg") - member_of()
    split = keys - queries
    total[:split, :] = jnp.zeros((split, total.shape[1]), f32)
    for b in range(blocks):
        start = b * queries
        live = ((first + b) * segs + seg_of < lengths[0]).astype(f32)
        grad_attended = head_stack((live * back[start : start + queries]).astype(bf16), heads)
        term = jnp.dot(soft[b], grad_attended, preferred_element_type=f32)
        total[start : start + split, :] += term[:split]
        total[start + split : start + keys, :] = term[split:]
    values[...] = total[...].astype(bf16)
    if crossed:
        rows_kernel("sent", x_turned, values, *sent)


def rows_kernel(which, x_turned, values, *outs):
    own = lax.axis_index("fsdp")
    along = 2 - (lax.axis_index("seg") & 1)
    parts = {"kept": (0, along ^ 3), "sent": (along, 3)}
    if which in parts:
        into = [outs[0].at[i] for i in range(2)]
        apart = parts[which]
    else:
        into, apart = outs, range(len(outs))
    rows = into[0].shape[0]
    for out, j in zip(into, apart, strict=True):
        at = pl.ds(aligned(own ^ j, rows), rows)
        out[...] = jnp.dot(
            x_turned[at, :], values[...], preferred_element_type=f32
        ).astype(out.dtype)


def out_kernel(heads, first, soft, values, *refs):
    wo, keep, *send = refs
    blocks, keys, lanes = soft.shape
    queries = lanes // heads
    width = values.shape[1]
    head = lax.broadcasted_iota(jnp.int32, (queries, width), 1) // (width // heads)
    for i in (first, first + 1):
        b = member_of() ^ i
        stacked = lax.dot_general(
            soft[b],
            values[pl.ds(aligned(b, queries), keys), :],
            TN,
            preferred_element_type=f32,
        )
        attended = stacked[:queries]
        for h in range(1, heads):
            attended = jnp.where(head == h, stacked[h * queries : (h + 1) * queries], attended)
        projected = jnp.dot(attended.astype(bf16), wo[...], preferred_element_type=f32)
        if i == first:
            keep[...] = projected
        else:
            start = 0
            for into in send:
                into[...] = projected[start : start + into.shape[0]].astype(into.dtype)
                start += into.shape[0]


def onward_kernel(keep, *refs):
    pieces, onward = refs[:-1], refs[-1]
    start = 0
    for piece in pieces:
        part = slice(start, start + piece.shape[0])
        onward[part, :] = (keep[part, :] + piece[...].astype(f32)).astype(bf16)
        start += piece.shape[0]


def finish_kernel(frame_count, lengths, frames, keep, back, *refs):
    pieces, frames_out, memory_out = refs[:-2], refs[-2], refs[-1]
    segs = memory_out.shape[0]
    count = frames.shape[0]
    near = jnp.concatenate([piece[...].astype(f32) for piece in pieces], axis=0)
    projected = keep[...] + near + back[...].astype(f32)
    first = lax.axis_index("seg") * segs

    def live(array, step):
        at = lax.broadcasted_iota(jnp.int32, array.shape, 0) // step
        return jnp.where(first + at < lengths[0], array, 0.0)

    frames_out[...] = (
        frames[...].astype(f32) + live(projected[:count], frame_count)
    ).astype(bf16)
    memory_out[...] = live(projected[count + segs :], 1).astype(bf16)


def columns_kernel(apart, *refs):
    count = len(apart)
    blocks, (out, wide, sems) = refs[:count], refs[-3:]
    width = blocks[0].shape[1]
    copies = []
    for i, block in enumerate(blocks):
        wide[i] = block[...].astype(f32)
        at = pl.ds(aligned(member_of() ^ apart[i], width), width)
        copies.append(pltpu.make_async_copy(wide.at[i], out.at[:, at], sems.at[i]))
        copies[-1].start()
    for copy in copies:
        copy.wait()


def gathered(piece):
    size = lax.axis_size("fsdp")
    pieces = {0: piece}
    bit = 1
    while bit < size:
        for have in sorted(pieces):
            pieces[have ^ bit] = swapped(pieces[have], "fsdp", bit)
        bit *= 2
    return [pieces[j] for j in range(size)]


def pairs(seg_size):
    straight, turned, first, last = [], [], [], []
    for s in range(seg_size):
        along = 1 if s & 1 else 2
        for f in range(GROUP):
            straight.append((s * GROUP + f, s * GROUP + (f ^ along)))
            turned.append((s * GROUP + f, s * GROUP + (f ^ along ^ 3)))
        k = s % GROUP
        first.append((s * GROUP + k, s * GROUP + (k ^ 1)))
        first.append(((s ^ 1) * GROUP + k, s * GROUP + (k ^ 2)))
        first.append(((s ^ 3) * GROUP + k, (s ^ 3) * GROUP + (k ^ 3)))
        last.append(((s ^ 3) * GROUP + (k ^ 3), s * GROUP + (k ^ 3)))
    return straight, turned, first, last


def on_device(
    frames, memory_in, lengths, ln_gain, w_query, w_key, w_value, w_out, grad_frames, grad_memory
):
    utterances, segs, frame_count, width = frames.shape
    seg_size = lax.axis_size("seg")
    fsdp_size = lax.axis_size("fsdp")
    group = GROUP
    assert utterances == 1 and segs == MEMORY and frame_count == LEFT and seg_size % group == 0
    heads = HEADS // group
    block = width // group
    rows = w_query.shape[0]
    frame_rows = segs * frame_count
    queries = frame_rows + 2 * segs
    halo_rows = LEFT + 2 * MEMORY
    keys = halo_rows + queries
    all_rows = halo_rows + group * queries
    seg = lax.axis_index("seg")
    member = seg % group

    crossed = fsdp_size == group
    own_blocks, tokens, tail = pl.pallas_call(
        functools.partial(pack_kernel, frame_count),
        in_specs=[hbm] * 8,
        out_specs=[vmem] * 3,
        out_shape=[
            jax.ShapeDtypeStruct((1 + crossed, rows, 3 * block), bf16),
            jax.ShapeDtypeStruct((2 * queries, width), bf16),
            jax.ShapeDtypeStruct((halo_rows, width), bf16),
        ],
        scratch_shapes=[
            pltpu.VMEM((frame_rows, width), bf16),
            pltpu.VMEM((2, segs, width), bf16),
            pltpu.VMEM((1, width), f32),
            pltpu.SemaphoreType.DMA((11,)),
        ],
        compiler_params=params(60),
        name="pack",
    )(
        w_query, w_key, w_value, frames.reshape(frame_rows, width),
        grad_frames.reshape(frame_rows, width), memory_in.reshape(segs, width),
        grad_memory.reshape(segs, width), ln_gain.reshape(1, width),
    )
    w_out, own_blocks = lax.optimization_barrier((w_out, own_blocks))

    far = swapped(tokens, "seg", 2)
    near = swapped(tokens, "seg", 1)
    starts = range(group, seg_size, group)
    halo = [
        lax.ppermute(tail, "seg", [(s - 1, s + ahead) for s in starts]) for ahead in (0, 2)
    ]
    bias = pl.pallas_call(
        functools.partial(mask_kernel, heads, frame_count, segs, group),
        out_specs=vmem,
        out_shape=jax.ShapeDtypeStruct((2, keys, heads * queries), f32),
        compiler_params=params(),
        name="mask",
    )()
    if crossed:
        both = ("seg", "fsdp")
        straight, turned, first, last = pairs(seg_size)
        came = lax.ppermute(own_blocks, both, straight)
        wo_came = lax.ppermute(w_out, both, first)
        came, far, near, halo, wo_came, bias = lax.optimization_barrier(
            (came, far, near, halo, wo_came, bias)
        )
        wo_last = lax.ppermute(wo_came, both, last)
    else:
        came = jnp.concatenate([own_blocks, own_blocks])
        wo_near = lax.dynamic_slice_in_dim(
            lax.all_gather(w_out, "fsdp", axis=0, tiled=True), member * block, block, 0
        )
    mine, mine_values, other, far, far_grads = pl.pallas_call(
        split_kernel,
        in_specs=[vmem] * 4,
        out_specs=[vmem] * 5,
        out_shape=[jax.ShapeDtypeStruct((rows, 2 * block), bf16)]
        + [jax.ShapeDtypeStruct((rows, block), bf16)]
        + [jax.ShapeDtypeStruct(came.shape[1:], bf16)]
        + [
            jax.ShapeDtypeStruct((queries + halo_rows, width), bf16),
            jax.ShapeDtypeStruct((queries, width), bf16),
        ],
        compiler_params=params(),
        name="split",
    )(came, far, *halo)
    if crossed:
        other = swapped(other, "seg", 1)
        forwarded = lax.ppermute(mine, both, turned)
        wo_near = pl.pallas_call(
            pick_kernel,
            in_specs=[vmem] * 2,
            out_specs=vmem,
            out_shape=jax.ShapeDtypeStruct((block, width), bf16),
            compiler_params=params(),
            name="pick",
        )(w_out, wo_came)
    else:
        wqkv_parts = gathered(own_blocks)
    parts = [tokens, near, far, far_grads, swapped(far, "seg", 1), swapped(far_grads, "seg", 1)]

    x_all, x_turned, u_all = pl.pallas_call(
        merge_kernel,
        in_specs=[vmem] * len(parts),
        out_specs=[vmem] * 3,
        out_shape=[
            jax.ShapeDtypeStruct((all_rows, width), bf16),
            jax.ShapeDtypeStruct((width, all_rows), bf16),
            jax.ShapeDtypeStruct((group * queries, width), bf16),
        ],
        compiler_params=params(),
        name="merge",
    )(*parts)
    x_all, wo_near = lax.optimization_barrier((x_all, wo_near))

    back = pl.pallas_call(
        functools.partial(back_kernel, crossed),
        in_specs=[vmem] * 2,
        out_specs=vmem,
        out_shape=jax.ShapeDtypeStruct((group * queries, block), f32),
        compiler_params=params(),
        name="back",
    )(u_all, wo_near)
    back, x_all = lax.optimization_barrier((back, x_all))
    soft_shape = jax.ShapeDtypeStruct((group, keys, heads * queries), bf16)
    values_shape = jax.ShapeDtypeStruct((all_rows, block), bf16)
    if crossed:
        early = pl.pallas_call(
            early_kernel,
            in_specs=[vmem] * 4,
            out_specs=vmem,
            out_shape=jax.ShapeDtypeStruct((all_rows, 2 * block), f32),
            compiler_params=params(),
            name="early",
        )(x_all, own_blocks, mine, other)
        early, waiting = lax.optimization_barrier((early, mine_values))
        forwarded_values = lax.ppermute(waiting, both, turned)
        wqkv_parts = [early, forwarded]
    soft, *values = pl.pallas_call(
        functools.partial(weights_kernel, heads, crossed),
        in_specs=[vmem] * (2 + len(wqkv_parts)),
        out_specs=[vmem] * (2 - crossed),
        out_shape=[soft_shape] + [values_shape] * (1 - crossed),
        scratch_shapes=[] if crossed else [pltpu.VMEM((width, 3 * block), bf16)],
        compiler_params=params(),
        name="soft_weights",
    )(x_all, bias, *wqkv_parts)
    if crossed:
        values = pl.pallas_call(
            values_kernel,
            in_specs=[vmem] * 5,
            out_specs=vmem,
            out_shape=values_shape,
            compiler_params=params(),
            name="values",
        )(x_all, own_blocks, mine_values, other, forwarded_values)
    else:
        (values,) = values

    values_grad_shape = jax.ShapeDtypeStruct((all_rows, block), bf16)
    wo_from = [wo_near] + ([wo_last] if crossed else [])
    sent_shape = [jax.ShapeDtypeStruct((2, rows, block), bf16)] * crossed
    wo_mine, values_grad, *sent = pl.pallas_call(
        functools.partial(grad_kernel, heads, frame_count, segs, crossed),
        in_specs=[smem] + [vmem] * (4 + len(wo_from)),
        out_specs=[vmem] * (2 + crossed),
        out_shape=[jax.ShapeDtypeStruct((block, width), bf16), values_grad_shape] + sent_shape,
        scratch_shapes=[
            pltpu.VMEM((all_rows, block), f32),
            pltpu.VMEM((group * queries, block), f32),
        ],
        compiler_params=params(),
        name="values_grad",
    )(lengths, u_all, soft, x_turned, back, *wo_from)

    def grad_rows(which, shapes):
        return pl.pallas_call(
            functools.partial(rows_kernel, which),
            in_specs=[vmem] * 2,
            out_specs=[vmem] * len(shapes),
            out_shape=shapes,
            compiler_params=params(),
            name="grad_rows_" + which,
        )(x_turned, values_grad)

    if crossed:
        (sent,) = sent
        (kept,) = grad_rows("kept", [jax.ShapeDtypeStruct((2, rows, block), f32)])
    else:
        grad_chunks = grad_rows(
            "all", [jax.ShapeDtypeStruct((rows, block), bf16)] * fsdp_size
        )

    def attend(start, name, pieces):
        cut = queries // pieces // 16 * 16
        sizes = [cut] * (pieces - 1) + [queries - cut * (pieces - 1)]
        keep, *send = pl.pallas_call(
            functools.partial(out_kernel, heads, start),
            in_specs=[vmem] * 3,
            out_specs=[vmem] * (1 + pieces),
            out_shape=[jax.ShapeDtypeStruct((queries, width), f32)]
            + [jax.ShapeDtypeStruct((size, width), bf16) for size in sizes],
            compiler_params=params(),
            name=name,
        )(soft, values, wo_mine)
        return keep, send

    keep_far, send_far = attend(2, "attend_far", PIECES)
    keep, send = attend(0, "attend_near", 1)
    near = [swapped(piece, "seg", 1) for piece in send]
    near_far = [swapped(piece, "seg", 1) for piece in send_far]
    onward = pl.pallas_call(
        onward_kernel,
        in_specs=[vmem] * (1 + PIECES),
        out_specs=vmem,
        out_shape=jax.ShapeDtypeStruct((queries, width), bf16),
        compiler_params=params(),
        name="onward",
    )(keep_far, *near_far)
    if crossed:
        came = lax.ppermute(sent, both, straight)
        passing = (kept[1] + came[1].astype(f32)).astype(bf16)
        passing, onward = lax.optimization_barrier((passing, onward))
        last = lax.ppermute(passing, both, turned)
        grad_sum = kept[0] + came[0].astype(f32) + last.astype(f32)
    else:
        grad_sum = grad_chunks[0].astype(f32)
        for j in range(1, fsdp_size):
            grad_sum = grad_sum + swapped(grad_chunks[j], "fsdp", j).astype(f32)
    returned = swapped(onward, "seg", 2)
    bit = group
    while bit < seg_size:
        mine = grad_sum.astype(bf16)
        other, returned = lax.optimization_barrier((swapped(mine, "seg", bit), returned))
        grad_sum = mine.astype(f32) + other.astype(f32)
        bit *= 2
    mine = grad_sum.astype(bf16)
    frames_out, memory_out = pl.pallas_call(
        functools.partial(finish_kernel, frame_count),
        in_specs=[smem] + [vmem] * 4,
        out_specs=[vmem] * 2,
        out_shape=[
            jax.ShapeDtypeStruct((frame_rows, width), bf16),
            jax.ShapeDtypeStruct((segs, width), bf16),
        ],
        compiler_params=params(),
        name="finish",
    )(lengths, frames.reshape(frame_rows, width), keep, returned, *near)
    far, frames_out, memory_out = lax.optimization_barrier(
        (swapped(mine, "seg", 2), frames_out, memory_out)
    )

    def columns(apart, blocks, *onto):
        count = len(blocks)
        return pl.pallas_call(
            functools.partial(columns_kernel, apart),
            in_specs=[vmem] * count + [hbm] * len(onto),
            out_specs=hbm,
            out_shape=jax.ShapeDtypeStruct((rows, width), f32),
            scratch_shapes=[
                pltpu.VMEM((count, rows, block), f32),
                pltpu.SemaphoreType.DMA((count,)),
            ],
            input_output_aliases={count: 0} if onto else {},
            compiler_params=params(),
            name="columns" + "_rest" * len(onto),
        )(*blocks, *onto)

    begun = columns((0, 2, 1), (mine, far, swapped(mine, "seg", 1)))
    value_grad = columns((3,), (swapped(far, "seg", 1),), begun)
    frames_out = frames_out.reshape(frames.shape)
    memory_out = memory_out.reshape(memory_in.shape)
    return (frames_out, memory_out, value_grad)


def solution(mesh):
    return jax.shard_map(
        on_device,
        mesh=mesh,
        in_specs=(
            P("fsdp", "seg", None, None),
            P("fsdp", "seg", None),
            P("fsdp"),
            P(),
            P("fsdp", None),
            P("fsdp", None),
            P("fsdp", None),
            P("fsdp", None),
            P("fsdp", "seg", None, None),
            P("fsdp", "seg", None),
        ),
        out_specs=(P("fsdp", "seg", None, None), P("fsdp", "seg", None), P("fsdp", None)),
        check_vma=False,
    )
```
